32 devices in a mesh: rows: 8 (over z, y), seq: 4 (over x, core).
Axes of the slice: x: 2, y: 2, z: 4, core: 2. Of those that a mesh axis runs over, the one named last changes fastest.
Arguments:
- target: bfloat16 [16, 1024, 512], P('rows', 'seq'), may hold values from -6 to 6
- memory: bfloat16 [16, 1024, 512], P('rows', 'seq'), may hold values from -6 to 6
- tgt_group: int32 [16, 1024], P('rows', 'seq'), may hold values from -1 to 3, as said below
- src_group: int32 [16, 1024], P('rows', 'seq'), may hold values from -1 to 3, as said below
- self_qkv: bfloat16 [512, 1536], replicated, may hold values from -0.25 to 0.25
- self_out: bfloat16 [512, 512], replicated, may hold values from -1.5 to 1.5
- self_bias: float32 [3, 512], replicated, may hold values from -3 to 3
- cross_q: bfloat16 [512, 512], replicated, may hold values from -0.25 to 0.25
- cross_kv: bfloat16 [512, 1024], replicated, may hold values from -0.25 to 0.25
- cross_out: bfloat16 [512, 512], replicated, may hold values from -1.5 to 1.5
- cross_bias: float32 [3, 512], replicated, may hold values from -3 to 3
- ffn_in: bfloat16 [512, 2048], replicated, may hold values from -0.25 to 0.25
- ffn_in_bias: float32 [2048], replicated, may hold values from -3 to 3
- ffn_out: bfloat16 [2048, 512], replicated, may hold values from -0.125 to 0.125
- ffn_out_bias: float32 [512], replicated, may hold values from -3 to 3
- norm_gain: float32 [3, 512], replicated, may hold values from 0.5 to 1.5
- norm_bias: float32 [3, 512], replicated, may hold values from -3 to 3
- cotangent: bfloat16 [16, 1024, 512], P('rows', 'seq'), may hold values from -6 to 6
Outputs:
- layer_out: float32 [16, 1024, 512], P('rows', 'seq')
- d_target: float32 [16, 1024, 512], P('rows', 'seq')
- d_memory: float32 [16, 1024, 512], P('rows', 'seq')
- d_self_qkv: float32 [512, 1536], replicated
- d_self_out: float32 [512, 512], replicated
- d_self_bias: float32 [3, 512], replicated
- d_cross_q: float32 [512, 512], replicated
- d_cross_kv: float32 [512, 1024], replicated
- d_cross_out: float32 [512, 512], replicated
- d_cross_bias: float32 [3, 512], replicated
- d_ffn_in: float32 [512, 2048], replicated
- d_ffn_in_bias: float32 [2048], replicated
- d_ffn_out: float32 [2048, 512], replicated
- d_ffn_out_bias: float32 [512], replicated
- d_norm_gain: float32 [3, 512], replicated
- d_norm_bias: float32 [3, 512], replicated
The draws below stay inside these ranges and needn't reach their ends.
Inputs may be any that keep to these rules, and one draw needn't show every extreme that they name: In every row, the positions hold documents 0 to 3 in order, then padding marked -1 (at least one position). One document of each row, which one drawn from the seed and the same number in tgt_group and src_group, begins within the first 256 positions and ends within the last 256. `src_group`: same law as tgt_group, with its own lengths; every document number of a row appears in both.
All inputs are finite; a program needn't handle non-finite values.
Results may differ from the reference program's by a relative error of at most 0.03.
Values may be sent and summed in bfloat16 or wider, within the bound.
No kernel may reach another device: no remote copies, remote signals or barrier semaphores. Data moves between devices by JAX's collectives and lax.ppermute only.
A program may use at most 256 MiB of HBM per device.

```python
import jax
import jax.numpy as jnp
from jax import lax

D = 512
HEADS = 8
HEAD_DIM = 64
FF = 2048
TOK = 256
NDOC = 4
ROWS = 16
LEN = 1024


def long_document(key):
    return jax.random.randint(jax.random.fold_in(key, 7), (ROWS, 1), 0, NDOC)


def group_ids(key, long_index):
    places = jnp.arange(LEN)
    key_gaps, key_padding = jax.random.split(key)
    longest_gap = max(TOK // (2 * NDOC), 1)
    gap_sizes = jax.random.randint(key_gaps, (ROWS, NDOC), 1, longest_gap + 1)
    padding = jax.random.randint(key_padding, (ROWS, 1), max(TOK // 16, 1), TOK // 4 + 1)
    slot_ids = jnp.arange(NDOC)[None, :]
    others = jnp.where(slot_ids == long_index, 0, gap_sizes)
    rest = LEN - padding - jnp.sum(others, axis=1, keepdims=True)
    lengths = jnp.where(slot_ids == long_index, rest, others)
    bounds = jnp.cumsum(lengths, axis=1)
    doc_number = jnp.sum((places[None, :, None] >= bounds[:, None, :]).astype(jnp.int32), axis=2)
    return jnp.where(doc_number == NDOC, -1, doc_number).astype(jnp.int32)


def draw_tgt_group(key, part):
    long_index = long_document(key)
    key = jax.random.fold_in(key, 11)
    return group_ids(key, long_index)


def draw_src_group(key, part):
    long_index = long_document(key)
    key = jax.random.fold_in(key, 13)
    return group_ids(key, long_index)


def block_levels(own_key, extent, shards, low, top_value):
    loudness = 1.0
    for dim, parts in shards:
        steps = jax.random.uniform(jax.random.fold_in(jax.random.fold_in(own_key, 6), dim), (parts,), jnp.float32, low / len(shards), top_value / len(shards))
        loudness = loudness * jnp.repeat(jnp.exp(steps), extent[dim] // parts).reshape((-1,) + (1,) * (len(extent) - 1 - dim))
    return loudness


def normal_values(rng, dims, spread, limit, cuts=(), held_as=jnp.bfloat16):
    entries = jax.random.normal(rng, dims, jnp.float32) * spread
    if len(cuts) > 0:
        entries = block_levels(rng, dims, cuts, -0.22, 0.18) * entries
    return jnp.clip(entries, min=-limit, max=limit).astype(held_as)


def setup_inputs(seed: int = 0) -> dict:
    key_of = jax.random.split(jax.random.key(seed), 19)
    target = normal_values(key_of[0], (ROWS, LEN, D), 1.0, 6.0, ((0, 8), (1, 4)))
    memory = normal_values(key_of[1], (ROWS, LEN, D), 1.0, 6.0, ((0, 8), (1, 4)))
    tgt_group = draw_tgt_group(jax.random.fold_in(key_of[18], 71), 0)
    src_group = draw_src_group(jax.random.fold_in(key_of[18], 71), 0)
    self_qkv = normal_values(key_of[4], (D, 3 * D), D ** -0.5, 0.25)
    self_out = normal_values(key_of[5], (D, D), (D // 32) ** -0.5, 1.5)
    self_bias = normal_values(key_of[6], (3, D), 0.5, 3.0, (), jnp.float32)
    cross_q = normal_values(key_of[7], (D, D), D ** -0.5, 0.25)
    cross_kv = normal_values(key_of[8], (D, 2 * D), D ** -0.5, 0.25)
    cross_out = normal_values(key_of[9], (D, D), (D // 32) ** -0.5, 1.5)
    cross_bias = normal_values(key_of[10], (3, D), 0.5, 3.0, (), jnp.float32)
    ffn_in = normal_values(key_of[11], (D, FF), D ** -0.5, 0.25)
    ffn_in_bias = normal_values(key_of[12], (FF,), 0.5, 3.0, (), jnp.float32)
    ffn_out = normal_values(key_of[13], (FF, D), FF ** -0.5, 0.125)
    ffn_out_bias = normal_values(key_of[14], (D,), 0.5, 3.0, (), jnp.float32)
    norm_gain = jnp.clip(1.0 + 0.1 * jax.random.normal(key_of[15], (3, D), jnp.float32), 0.5, 1.5)
    norm_bias = normal_values(key_of[16], (3, D), 0.5, 3.0, (), jnp.float32)
    cotangent = normal_values(key_of[17], (ROWS, LEN, D), 1.0, 6.0, ((0, 8), (1, 4)))
    return dict(target=target, memory=memory, tgt_group=tgt_group, src_group=src_group, self_qkv=self_qkv, self_out=self_out, self_bias=self_bias, cross_q=cross_q, cross_kv=cross_kv, cross_out=cross_out, cross_bias=cross_bias, ffn_in=ffn_in, ffn_in_bias=ffn_in_bias, ffn_out=ffn_out, ffn_out_bias=ffn_out_bias, norm_gain=norm_gain, norm_bias=norm_bias, cotangent=cotangent)


@jax.custom_vjp
def low(v):
    return lax.optimization_barrier(v.astype(jnp.bfloat16)).astype(jnp.float32)

@jax.custom_vjp
def low_back(v):
    return v

def low_keep(v):
    return (low(v), None)

def low_pass(kept, grad):
    return (grad,)

def back_keep(v):
    return (v, None)

def back_low(kept, grad):
    return (low(grad),)
low.defvjp(low_keep, low_pass)
low_back.defvjp(back_keep, back_low)
highest = lax.Precision.HIGHEST
eps_norm = 1e-05
score_scale = 0.125
lowest = -1e+30

def matmul(left, right):
    return jnp.dot(left, right, precision=highest)

def layer_norm(hidden, scales, shifts):
    average = lax.optimization_barrier(jnp.mean(hidden, axis=-1, keepdims=True))
    centred = hidden - average
    variance = lax.optimization_barrier(jnp.mean(centred * centred, axis=-1, keepdims=True))
    return centred * lax.rsqrt(variance + eps_norm) * scales + shifts

def split_heads(tensor):
    return tensor.reshape(tensor.shape[0], HEADS, HEAD_DIM).transpose(1, 0, 2)

def attend(queries, key_rows, value_rows, allowed):
    queries = low(low_back(queries))
    key_rows = low(low_back(key_rows))
    value_rows = low(low_back(value_rows))
    raw = jnp.einsum('hqd,hkd->hqk', split_heads(queries), split_heads(key_rows), precision=highest) * score_scale
    scores = low_back(raw)
    masked = jnp.where(allowed[None], scores, lowest)
    row_top = lax.optimization_barrier(jnp.max(masked, axis=-1, keepdims=True))
    weights = jnp.where(allowed[None], jnp.exp(masked - row_top), 0.0)
    shares = weights / lax.optimization_barrier(jnp.sum(weights, axis=-1, keepdims=True))
    mixed = jnp.einsum('hqk,hkd->hqd', low(shares), split_heads(value_rows), precision=highest)
    mixed = mixed.transpose(1, 0, 2).reshape(queries.shape[0], D)
    return low(low_back(mixed))

def row_forward(params, tokens_in, memory_in, target_group, source_group):
    self_qkv, self_out, self_bias, cross_q, cross_kv, cross_out, cross_bias, ffn_in, ffn_in_bias, ffn_out, ffn_out_bias, norm_gain, norm_bias = params
    places = jnp.arange(LEN)
    causal = (target_group[:, None] == target_group[None, :]) & (places[None, :] <= places[:, None])
    across = target_group[:, None] == source_group[None, :]
    projected = matmul(low(tokens_in), self_qkv)
    queries = projected[:, :D] + self_bias[0]
    key_rows = projected[:, D:2 * D]
    value_rows = projected[:, 2 * D:] + self_bias[1]
    self_mixed = attend(queries, key_rows, value_rows, causal)
    branch = low_back(matmul(self_mixed, self_out) + self_bias[2])
    first_norm = layer_norm(tokens_in + branch, norm_gain[0], norm_bias[0])
    cross_queries = matmul(low(first_norm), cross_q) + cross_bias[0]
    cross_proj = matmul(low(memory_in), cross_kv)
    cross_keys = cross_proj[:, :D]
    cross_values = cross_proj[:, D:] + cross_bias[1]
    cross_mixed = attend(cross_queries, cross_keys, cross_values, across)
    cross_branch = low_back(matmul(cross_mixed, cross_out) + cross_bias[2])
    second = layer_norm(first_norm + cross_branch, norm_gain[1], norm_bias[1])
    inner_act = jax.nn.gelu(low_back(matmul(low(second), ffn_in) + ffn_in_bias))
    outer_out = low_back(matmul(low(inner_act), ffn_out) + ffn_out_bias)
    return layer_norm(second + outer_out, norm_gain[2], norm_bias[2])

def reference(target, memory, tgt_group, src_group, self_qkv, self_out, self_bias, cross_q, cross_kv, cross_out, cross_bias, ffn_in, ffn_in_bias, ffn_out, ffn_out_bias, norm_gain, norm_bias, cotangent):
    params = tuple((weight.astype(jnp.float32) for weight in (self_qkv, self_out, self_bias, cross_q, cross_kv, cross_out, cross_bias, ffn_in, ffn_in_bias, ffn_out, ffn_out_bias, norm_gain, norm_bias)))
    tokens_all = target.astype(jnp.float32)
    memory_all = memory.astype(jnp.float32)

    def run(params, tokens_all, memory_all):

        def one_row(items):
            tokens_in, memory_in, target_group, source_group = items
            return row_forward(params, tokens_in, memory_in, target_group, source_group)
        return lax.map(jax.checkpoint(one_row), (tokens_all, memory_all, tgt_group, src_group))
    layer_out, pullback = jax.vjp(run, params, tokens_all, memory_all)
    grad_params, grad_tokens, grad_memory = pullback(cotangent.astype(jnp.float32))
    return (layer_out, grad_tokens, grad_memory) + tuple(grad_params)
```

```python
import functools
import math

import jax
import jax.numpy as jnp
from jax import lax
from jax.experimental import pallas as pl
from jax.experimental.pallas import tpu as pltpu
from jax.sharding import PartitionSpec as P

HEADS = 8
PAIR = 128
EPS = 1e-05
SCALE = 0.125
NEG = -1e30
VMEM = 60 * 1024 * 1024
bf16 = jnp.bfloat16
f32 = jnp.float32


def params():
    return pltpu.CompilerParams(vmem_limit_bytes=VMEM)


def cost(flops, nbytes, trans=0):
    return pl.CostEstimate(flops=int(flops), bytes_accessed=int(nbytes), transcendentals=int(trans))


def dot(a, b):
    return jnp.dot(a, b, preferred_element_type=f32)


def dot_nt(a, b):
    return lax.dot_general(a, b, (((1,), (1,)), ((), ())), preferred_element_type=f32)


def dot_tn(a, b):
    return lax.dot_general(a, b, (((0,), (0,)), ((), ())), preferred_element_type=f32)


def col_sum(v):
    return jnp.sum(v.astype(f32), axis=0, keepdims=True)


def normalize(h):
    mean = jnp.mean(h, axis=-1, keepdims=True)
    c = h - mean
    r = lax.rsqrt(jnp.mean(c * c, axis=-1, keepdims=True) + EPS)
    return c * r, r


def norm_back(u, n, r, gain):
    w = u * gain
    return r * (
        w
        - jnp.mean(w, axis=-1, keepdims=True)
        - n * jnp.mean(w * n, axis=-1, keepdims=True)
    )


def whole(shape):
    return pl.BlockSpec(shape, lambda *_: (0,) * len(shape))


def smem():
    return pl.BlockSpec(memory_space=pltpu.SMEM)


def half_rows(g, which, count):
    at = g if which == 0 else 1 - g
    return pl.ds(pl.multiple_of(at * count, count), count)


class Plan:
    def __init__(self, dims, n, minimum=16):
        self.n, self.scatter, self.everywhere = n, [], []
        k = n
        for axis, base, m, at in dims:
            if m == 1:
                continue
            if not self.everywhere and k % m == 0 and k // m >= minimum:
                self.scatter.append((axis, base, m))
                k //= m
            else:
                self.everywhere.append((axis, base, m))
        self.k = k
        self.chunks = n // k
        place = 0
        for (axis, base, m), (_, _, _, at) in zip(self.scatter, [d for d in dims if d[2] > 1]):
            place = place * m + at
        self.place = place


def store_rel(ref, first, value, place, k, chunks):
    for w in range(value.shape[0] // k):
        at = jnp.bitwise_xor(place, first + w)
        ref[pl.ds(pl.multiple_of(at * k, k), k), :] = value[w * k : (w + 1) * k].astype(ref.dtype)


def swap(x, axis, off):
    size = lax.axis_size(axis)
    return lax.ppermute(x, axis, [(i, i ^ off) for i in range(size)])


def add_all(parts):
    total = parts[0].astype(f32)
    for part in parts[1:]:
        total = total + part.astype(f32)
    return total


def reduce_scatter(buf, plan):
    for axis, base, m in plan.scatter:
        k = buf.shape[0] // m
        parts = [buf[:k]]
        for j in range(1, m):
            parts.append(swap(buf[j * k : (j + 1) * k], axis, j * base))
        buf = add_all(parts).astype(buf.dtype)
    for axis, base, m in plan.everywhere:
        buf = add_all([buf] + [swap(buf, axis, j * base) for j in range(1, m)]).astype(buf.dtype)
    return buf


def all_gather(buf, plan):
    for axis, base, m in reversed(plan.scatter[1:]):
        buf = jnp.concatenate([buf] + [swap(buf, axis, j * base) for j in range(1, m)], axis=0)
    return buf, swap(buf, "seq", 1)


def unpack(name, sources, out_shape, out_map, blocks):
    size = 512
    scalars, operands, specs = [], [], []
    for own, other, plan in sources:
        scalars += [plan.place]
    table = {}
    for q, (src, b) in enumerate(blocks):
        table.setdefault(src, []).append((q, b))

    def rel_block(src, q, sc):
        plan = sources[src][2]
        entries = table[src]
        q0, b0 = entries[0]
        logical = jnp.clip(q - q0 + b0, b0, b0 + len(entries) - 1)
        return jnp.bitwise_xor(logical, sc[src] // (size // plan.k))

    for i, (own, other, plan) in enumerate(sources):
        nbh = own.shape[0] // size
        for arr in (own, other):
            operands.append(arr)
            specs.append(
                pl.BlockSpec(
                    (size, 512), lambda q, sc, i=i, nbh=nbh: (rel_block(i, q, sc) % nbh, 0)
                )
            )

    def kernel(sc, *refs):
        out = refs[-1]
        q = pl.program_id(0)
        for i, (own, other, plan) in enumerate(sources):
            nbh = own.shape[0] // size
            per = size // plan.k
            q0, q1 = table[i][0][0], table[i][-1][0]
            top = rel_block(i, q, sc) // nbh
            here = (q >= q0) & (q <= q1)
            for half in range(2):
                src = refs[2 * i + half]

                @pl.when(here & (top == half))
                def _():
                    low = sc[i] % per
                    for w in range(per):
                        at = jnp.bitwise_xor(low, w)
                        out[w * plan.k : (w + 1) * plan.k, :] = src[
                            pl.ds(pl.multiple_of(at * plan.k, plan.k), plan.k), :
                        ].astype(f32)

    return pl.pallas_call(
        kernel,
        grid_spec=pltpu.PrefetchScalarGridSpec(
            num_scalar_prefetch=1,
            grid=(len(blocks),),
            in_specs=specs,
            out_specs=pl.BlockSpec((size, 512), lambda q, sc: out_map(q)),
        ),
        out_shape=jax.ShapeDtypeStruct(out_shape, f32),
        compiler_params=params(),
        cost_estimate=cost(0, 6 * math.prod(out_shape)),
        name=name,
    )(jnp.stack(scalars).astype(jnp.int32), *operands)


def embed_kernel(parts, sc, tgt, recv, w, b, x_out, *outs):
    g = sc[0]
    tok = recv.shape[0]
    for which, x in ((0, tgt[g]), (1, recv[...])):
        rows = half_rows(g, which, tok)
        x_out[rows, :] = x
        y = dot(x, w[...]) + b[...]
        for i, (out, scale) in enumerate(zip(outs, parts)):
            piece = y[:, i * 512 : (i + 1) * 512]
            if scale != 1.0:
                piece = piece.astype(bf16).astype(f32) * scale
            out[rows, :] = piece.astype(bf16)


def embed(name, sc, local, recv, w, b, parts):
    tokens = 2 * recv.shape[0]
    one = jax.ShapeDtypeStruct((tokens, 512), bf16)
    vm = pl.BlockSpec(memory_space=pltpu.VMEM)
    return pl.pallas_call(
        functools.partial(embed_kernel, parts),
        in_specs=[smem()] + [vm] * 4,
        out_specs=[vm] * (1 + len(parts)),
        out_shape=[one] * (1 + len(parts)),
        compiler_params=params(),
        cost_estimate=cost(2 * tokens * 512 * w.shape[1], 4e6),
        name=name,
    )(sc, local, recv, w, b)


def row_to_cols(row):
    return jnp.transpose(jnp.broadcast_to(row, (PAIR, row.shape[1])))


def places(t, length, members, tok, shape, axis):
    at = lax.broadcasted_iota(jnp.int32, shape, axis)
    member = at // (2 * tok)
    inner = at - member * (2 * tok)
    low = jnp.bitwise_xor(member, t)
    block = jnp.where(inner < tok, low, 2 * members - 1 - low)
    return block * tok + jnp.where(inner < tok, inner, inner - tok)


def bias_of(causal, t, ids, tok, transposed):
    length = ids.shape[1]
    members = length // (2 * tok)
    q_row = ids[0:1, : 2 * tok]
    k_row = ids[0:1, :] if causal else ids[1:2, :]
    if transposed:
        allowed = row_to_cols(k_row)[:, 0:1] == q_row
        if causal:
            kp = places(t, length, members, tok, (length, 1), 0)
            qp = places(t, length, members, tok, (1, 2 * tok), 1)
            allowed = allowed & (kp <= qp)
    else:
        allowed = row_to_cols(q_row)[:, 0:1] == k_row
        if causal:
            kp = places(t, length, members, tok, (1, length), 1)
            qp = places(t, length, members, tok, (2 * tok, 1), 0)
            allowed = allowed & (kp <= qp)
    return jnp.where(allowed, 0.0, NEG).astype(f32)


def key_parts(own, others, tok):
    every = [own[...]] + [o[...] for o in others]
    low = jnp.concatenate([e[:tok] for e in every], axis=0)
    high = jnp.concatenate([e[tok:] for e in every], axis=0)
    return low, high


def bias_rows(bias, tok, members, half, transposed, cols):
    if transposed:
        return jnp.concatenate(
            [bias[(2 * j + half) * tok : (2 * j + half + 1) * tok, cols] for j in range(members)], axis=0
        )
    return jnp.concatenate(
        [bias[cols, (2 * j + half) * tok : (2 * j + half + 1) * tok] for j in range(members)], axis=1
    )


def lane_of_pair(shape):
    return lax.broadcasted_iota(jnp.int32, shape, 1) // 64


def attend_kernel(causal, tok, members, sc, ids, q, *refs):
    others = members - 1
    k_own, k_others = refs[0], refs[1 : 1 + others]
    v_own, v_others = refs[1 + others], refs[2 + others : 2 + 2 * others]
    out, lse, bias = refs[2 + 2 * others :]

    @pl.when(pl.program_id(0) == 0)
    def _():
        bias[...] = bias_of(causal, sc[1], ids[...], tok, False)

    k_low, k_high = key_parts(k_own, k_others, tok)
    v_low, v_high = key_parts(v_own, v_others, tok)
    k_all = jnp.concatenate([k_low, k_high], axis=0)
    v_all = jnp.concatenate([v_low, v_high], axis=0)
    lane = lane_of_pair((tok, PAIR))
    for b in range(2):
        rows = slice(b * tok, (b + 1) * tok)
        short = causal and b == 0
        kk, vv = (k_low, v_low) if short else (k_all, v_all)
        mask = bias_rows(bias, tok, members, 0, False, rows)
        if not short:
            mask = jnp.concatenate([mask, bias_rows(bias, tok, members, 1, False, rows)], axis=1)
        mixed, logs = [], []
        for h in range(2):
            qm = jnp.where(lane == h, q[rows, :], jnp.zeros((), bf16))
            s = dot_nt(qm, kk) + mask
            top = jnp.max(s, axis=-1, keepdims=True)
            p = jnp.exp(s - top)
            total = jnp.sum(p, axis=-1, keepdims=True)
            mixed.append(dot(p.astype(bf16), vv) / total)
            logs.append(top + jnp.log(total))
        out[rows, :] = jnp.where(lane == 0, mixed[0], mixed[1]).astype(bf16)
        both = jnp.transpose(jnp.where(lane == 0, logs[0], logs[1]))
        lse[0, 0:1, rows] = both[0:1]
        lse[0, 1:2, rows] = both[64:65]


def attend(name, causal, sc, ids, q, ks, vs):
    tokens = q.shape[0]
    length = ids.shape[1]
    members = len(ks)
    pair = pl.BlockSpec((tokens, PAIR), lambda p: (0, p))
    return pl.pallas_call(
        functools.partial(attend_kernel, causal, tokens // 2, members),
        grid=(4,),
        in_specs=[smem(), whole(ids.shape)] + [pair] * (1 + 2 * members),
        out_specs=[pair, pl.BlockSpec((1, 2, tokens), lambda p: (p, 0, 0))],
        out_shape=[
            jax.ShapeDtypeStruct((tokens, 512), bf16),
            jax.ShapeDtypeStruct((4, 2, tokens), f32),
        ],
        scratch_shapes=[pltpu.VMEM((tokens, length), f32)],
        compiler_params=params(),
        cost_estimate=cost(16 * tokens * length * 512, 4e6, 8 * tokens * length),
        name=name,
    )(sc, ids, q, *ks, *vs)


def attend_back_kernel(causal, tok, members, sc, ids, q, grad, lse, delta, *refs):
    others = members - 1
    k_own, k_others = refs[0], refs[1 : 1 + others]
    v_own, v_others = refs[1 + others], refs[2 + others : 2 + 2 * others]
    dq, dk, dv, bias = refs[2 + 2 * others :]

    @pl.when(pl.program_id(0) == 0)
    def _():
        bias[...] = bias_of(causal, sc[1], ids[...], tok, True)

    keys = key_parts(k_own, k_others, tok)
    values = key_parts(v_own, v_others, tok)
    lane = lane_of_pair((tok, PAIR))
    key_lane = lane_of_pair((tok * members, PAIR))
    grad_k, grad_v = [None, None], [None, None]

    def plus(total, term):
        return term if total is None else total + term

    for b in range(2):
        rows = slice(b * tok, (b + 1) * tok)
        grad_q = None
        for half in range(2):
            if causal and b == 0 and half == 1:
                continue
            kk, vv = keys[half], values[half]
            mask = bias_rows(bias, tok, members, half, True, rows)
            for h in range(2):
                qm = jnp.where(lane == h, q[rows, :], jnp.zeros((), bf16))
                gm = jnp.where(lane == h, grad[rows, :], jnp.zeros((), bf16))
                km = jnp.where(key_lane == h, kk, jnp.zeros((), bf16))
                p = jnp.exp(dot_nt(kk, qm) + mask - lse[0, h : h + 1, rows])
                ds = (p * (dot_nt(vv, gm) - delta[0, h : h + 1, rows])).astype(bf16)
                grad_v[half] = plus(grad_v[half], dot(p.astype(bf16), gm))
                grad_k[half] = plus(grad_k[half], dot(ds, qm))
                grad_q = plus(grad_q, dot_tn(ds, km))
        dq[rows, :] = (grad_q * SCALE).astype(bf16)
    for half in range(2):
        for j in range(members):
            to = slice((2 * j + half) * tok, (2 * j + half + 1) * tok)
            dk[to, :] = grad_k[half][j * tok : (j + 1) * tok].astype(bf16)
            dv[to, :] = grad_v[half][j * tok : (j + 1) * tok].astype(bf16)


def attend_back(name, causal, sc, ids, q, grad, lse, delta, ks, vs):
    tokens = q.shape[0]
    length = ids.shape[1]
    members = len(ks)
    pair = pl.BlockSpec((tokens, PAIR), lambda p: (0, p))
    row = pl.BlockSpec((1, 2, tokens), lambda p: (p, 0, 0))
    long = pl.BlockSpec((length, PAIR), lambda p: (0, p))
    return pl.pallas_call(
        functools.partial(attend_back_kernel, causal, tokens // 2, members),
        grid=(4,),
        in_specs=[smem(), whole(ids.shape), pair, pair, row, row] + [pair] * (2 * members),
        out_specs=[pair, long, long],
        out_shape=[
            jax.ShapeDtypeStruct((tokens, 512), bf16),
            jax.ShapeDtypeStruct((length, 512), bf16),
            jax.ShapeDtypeStruct((length, 512), bf16),
        ],
        scratch_shapes=[pltpu.VMEM((length, tokens), f32)],
        compiler_params=params(),
        cost_estimate=cost(40 * tokens * length * 512, 6e6, 8 * tokens * length),
        name=name,
    )(sc, ids, q, grad, lse, delta, *ks, *vs)


def after_self_kernel(x, mixed, w_out, sbias, gain, shift, w_q, cbias, n0, r0, q2):
    h = x[...].astype(f32) + dot(mixed[...], w_out[...]) + sbias[2:3, :]
    n, r = normalize(h)
    n0[...] = n
    r0[...] = r
    first = n * gain[0:1, :] + shift[0:1, :]
    q = dot(first.astype(bf16), w_q[...]) + cbias[0:1, :]
    q2[...] = (q.astype(bf16).astype(f32) * SCALE).astype(bf16)


def after_self(x, mixed, w_out, sbias, gain, shift, w_q, cbias):
    tokens = x.shape[0]
    vm = pl.BlockSpec(memory_space=pltpu.VMEM)
    return pl.pallas_call(
        after_self_kernel,
        in_specs=[vm] * 8,
        out_specs=[vm] * 3,
        out_shape=[
            jax.ShapeDtypeStruct((tokens, 512), f32),
            jax.ShapeDtypeStruct((tokens, 1), f32),
            jax.ShapeDtypeStruct((tokens, 512), bf16),
        ],
        compiler_params=params(),
        cost_estimate=cost(4 * tokens * 512 * 512, 4e6),
        name="after_self",
    )(x, mixed, w_out, sbias, gain, shift, w_q, cbias)


def head_sums(a, b):
    prod = a * b
    high = prod.astype(bf16)
    low = (prod - high.astype(f32)).astype(bf16)
    pick = (
        lax.broadcasted_iota(jnp.int32, (HEADS, 512), 1) // 64
        == lax.broadcasted_iota(jnp.int32, (HEADS, 512), 0)
    ).astype(bf16)
    return dot_nt(pick, high) + dot_nt(pick, low)


def put_head_rows(ref, rows):
    for p in range(4):
        ref[p] = rows[2 * p : 2 * p + 2]


def gelu_parts(v):
    c = math.sqrt(2.0 / math.pi)
    v2 = v * v
    t = jnp.tanh(c * v * (1.0 + 0.044715 * v2))
    half = 0.5 * (1.0 + t)
    slope = half + 0.5 * v * (1.0 - t * t) * (c * (1.0 + 3.0 * 0.044715 * v2))
    return v * half, slope


def mid_kernel(
    chunks, k_in, k_out, sc, n0, mixed, cout, cbias, gain, shift, w_in, b_in, w_out, b_out, cot,
    cot_recv, own_out, send_out, d_in, d_out, d_cout, small, grad_two, grad_mixed, delta,
    inner, slope, low, n1, r1, total, grad_three, outer,
):
    i = pl.program_id(0)
    g = sc[0]
    tok = cot_recv.shape[0]

    @pl.when(i == 0)
    def _():
        first = n0[...] * gain[0:1, :] + shift[0:1, :]
        n, r = normalize(first + dot(mixed[...], cout[...]) + cbias[2:3, :])
        n1[...] = n
        r1[...] = r
        second = n * gain[1:2, :] + shift[1:2, :]
        low[...] = second.astype(bf16)
        total[...] = second + b_out[...]
        small[...] = jnp.zeros_like(small)

    @pl.when(i < chunks)
    def _():
        pre = dot(low[...], w_in[...]) + b_in[...]
        act, grad_act = gelu_parts(pre)
        act = act.astype(bf16)
        inner[i] = act
        slope[i] = grad_act.astype(bf16)
        total[...] += dot(act, w_out[...])

    @pl.when(i == chunks - 1)
    def _():
        n, r = normalize(total[...])
        result = n * gain[2:3, :] + shift[2:3, :]
        total[...] = result
        own_out[...] = total[half_rows(g, 0, tok), :]
        send_out[...] = total[half_rows(g, 1, tok), :].astype(bf16)
        total[half_rows(g, 0, tok), :] = cot[g].astype(f32)
        total[half_rows(g, 1, tok), :] = cot_recv[...].astype(f32)
        u = total[...]
        small[0:1, :] = col_sum(u * n)
        small[1:2, :] = col_sum(u)
        back = norm_back(u, n, r, gain[2:3, :])
        grad_three[...] = back
        back_low = back.astype(bf16)
        outer[...] = back_low
        small[2:3, :] = col_sum(back_low)
        total[...] = back

    @pl.when(i >= chunks)
    def _():
        j = i - chunks
        back = dot_nt(outer[...], w_out[...]) * slope[j].astype(f32)
        pre_low = back.astype(bf16)
        small[pl.ds(8 + j, 1), :] = col_sum(pre_low)
        per = 512 // k_in
        store_rel(d_in, 0, dot_tn(low[...], pre_low), sc[2] % per, k_in, per)
        per = 512 // k_out
        store_rel(d_out, 0, dot_tn(inner[j], outer[...]), sc[3] % per, k_out, per)
        total[...] += dot_nt(pre_low, w_in[...])

    @pl.when(i == 2 * chunks - 1)
    def _():
        u = total[...]
        n = n1[...]
        small[3:4, :] = col_sum(u * n)
        small[4:5, :] = col_sum(u)
        back = norm_back(u, n, r1[...], gain[1:2, :])
        grad_two[...] = back
        back_low = back.astype(bf16)
        small[5:6, :] = col_sum(back_low)
        d_cout[...] = dot_tn(mixed[...], back_low).astype(bf16)
        g_mixed = dot_nt(back_low, cout[...]).astype(bf16)
        grad_mixed[...] = g_mixed
        put_head_rows(delta, head_sums(g_mixed.astype(f32), mixed[...].astype(f32)))


def middle(sc, plan_in, plan_out, n0, mixed, cout, cbias, gain, shift, w_in, b_in, w_out, b_out, cot, cot_recv):
    tokens = n0.shape[0]
    tok = tokens // 2
    ff = w_in.shape[1]
    chunks = ff // 512
    sds = jax.ShapeDtypeStruct

    def rel(plan, which):
        per = 512 // plan.k
        return pl.BlockSpec(
            (512, 512),
            lambda i, sc: (jnp.bitwise_xor(jnp.maximum(i - chunks, 0), sc[which] // per), 0),
        )

    return pl.pallas_call(
        functools.partial(mid_kernel, chunks, plan_in.k, plan_out.k),
        grid_spec=pltpu.PrefetchScalarGridSpec(
            num_scalar_prefetch=1,
            grid=(2 * chunks,),
            in_specs=[
                whole((tokens, 512)),
                whole((tokens, 512)),
                whole((512, 512)),
                whole((3, 512)),
                whole((3, 512)),
                whole((3, 512)),
                pl.BlockSpec((512, 512), lambda i, sc: (0, i % chunks)),
                pl.BlockSpec((1, 512), lambda i, sc: (0, i % chunks)),
                pl.BlockSpec((512, 512), lambda i, sc: (i % chunks, 0)),
                whole((1, 512)),
                whole(cot.shape),
                whole(cot_recv.shape),
            ],
            out_specs=[
                whole((tok, 512)),
                whole((tok, 512)),
                rel(plan_in, 2),
                rel(plan_out, 3),
                whole((512, 512)),
                whole((8 + chunks + 4, 512)),
                whole((tokens, 512)),
                whole((tokens, 512)),
                whole((4, 2, tokens)),
            ],
            scratch_shapes=[
                pltpu.VMEM((chunks, tokens, 512), bf16),
                pltpu.VMEM((chunks, tokens, 512), bf16),
                pltpu.VMEM((tokens, 512), bf16),
                pltpu.VMEM((tokens, 512), f32),
                pltpu.VMEM((tokens, 1), f32),
                pltpu.VMEM((tokens, 512), f32),
                pltpu.VMEM((tokens, 512), f32),
                pltpu.VMEM((tokens, 512), bf16),
            ],
        ),
        out_shape=[
            sds((tok, 512), f32),
            sds((tok, 512), bf16),
            sds((ff, 512), bf16),
            sds((ff, 512), bf16),
            sds((512, 512), bf16),
            sds((8 + chunks + 4, 512), f32),
            sds((tokens, 512), f32),
            sds((tokens, 512), bf16),
            sds((4, 2, tokens), f32),
        ],
        compiler_params=params(),
        cost_estimate=cost(2 * tokens * 512 * (6 * ff + 3 * 512), 2e7),
        name="middle",
    )(sc, n0, mixed, cout, cbias, gain, shift, w_in, b_in, w_out, b_out, cot, cot_recv)


def after_cross_kernel(
    k, chunks, sc, dq, grad_two, n0, r0, w_q, mixed, w_out, gain, shift, d_cout,
    buf, d_sout, small, grad_one, grad_mixed, delta,
):
    place = sc[4]
    n = n0[...]
    first = (n * gain[0:1, :] + shift[0:1, :]).astype(bf16)
    half = 512 // k
    store_rel(buf, 0, d_cout[...], place, k, chunks)
    store_rel(buf, half, dot_tn(first, dq[...]), place, k, chunks)
    u = grad_two[...] + dot_nt(dq[...], w_q[...])
    small[...] = jnp.zeros_like(small)
    small[0:1, :] = col_sum(u * n)
    small[1:2, :] = col_sum(u)
    small[2:3, :] = col_sum(dq[...])
    back = norm_back(u, n, r0[...], gain[0:1, :])
    grad_one[...] = back
    back_low = back.astype(bf16)
    small[3:4, :] = col_sum(back_low)
    d_sout[...] = dot_tn(mixed[...], back_low).astype(bf16)
    g_mixed = dot_nt(back_low, w_out[...]).astype(bf16)
    grad_mixed[...] = g_mixed
    put_head_rows(delta, head_sums(g_mixed.astype(f32), mixed[...].astype(f32)))


def after_cross(sc, plan, dq, grad_two, n0, r0, w_q, mixed, w_out, gain, shift, d_cout):
    tokens = dq.shape[0]
    sds = jax.ShapeDtypeStruct
    vm = pl.BlockSpec(memory_space=pltpu.VMEM)
    return pl.pallas_call(
        functools.partial(after_cross_kernel, plan.k, plan.chunks),
        in_specs=[smem()] + [vm] * 10,
        out_specs=[vm] * 6,
        out_shape=[
            sds((1024, 512), bf16),
            sds((512, 512), bf16),
            sds((8, 512), f32),
            sds((tokens, 512), f32),
            sds((tokens, 512), bf16),
            sds((4, 2, tokens), f32),
        ],
        compiler_params=params(),
        cost_estimate=cost(8 * tokens * 512 * 512, 6e6),
        name="after_cross",
    )(sc, dq, grad_two, n0, r0, w_q, mixed, w_out, gain, shift, d_cout)


def sum_parts(own, others, tokens):
    total = own[:tokens].astype(f32)
    for o in others:
        total = total + o[...].astype(f32)
    return total.astype(bf16)


def memory_grad_kernel(n_other, k, chunks, sc, x, w, *refs):
    dk = sum_parts(refs[0], refs[1 : 1 + n_other], x.shape[0])
    dv = sum_parts(refs[1 + n_other], refs[2 + n_other : 2 + 2 * n_other], x.shape[0])
    own_out, send_out, buf, small, total = refs[2 + 2 * n_other :]
    tok = own_out.shape[0]
    g, place = sc[0], sc[5]
    per = 512 // k
    store_rel(buf, 0, dot_tn(x[...], dk), place, k, chunks)
    store_rel(buf, per, dot_tn(x[...], dv), place, k, chunks)
    small[...] = jnp.zeros_like(small)
    small[0:1, :] = col_sum(dv)
    total[...] = dot_nt(dk, w[:, :512]) + dot_nt(dv, w[:, 512:])
    own_out[...] = total[half_rows(g, 0, tok), :]
    send_out[...] = total[half_rows(g, 1, tok), :].astype(bf16)


def memory_grad(sc, plan, x, w, dks, dvs):
    tokens = x.shape[0]
    tok = tokens // 2
    sds = jax.ShapeDtypeStruct
    vm = pl.BlockSpec(memory_space=pltpu.VMEM)
    n_other = len(dks) - 1
    keys = [vm] * (1 + n_other)
    return pl.pallas_call(
        functools.partial(memory_grad_kernel, n_other, plan.k, plan.chunks),
        in_specs=[smem(), vm, vm] + keys + keys,
        out_specs=[vm] * 4,
        out_shape=[
            sds((tok, 512), f32),
            sds((tok, 512), bf16),
            sds((1024, 512), bf16),
            sds((8, 512), f32),
        ],
        scratch_shapes=[pltpu.VMEM((tokens, 512), f32)],
        compiler_params=params(),
        cost_estimate=cost(8 * tokens * 512 * 512, 6e6),
        name="memory_grad",
    )(sc, x, w, *dks, *dvs)


def target_grad_kernel(n_other, ka, ca, kb, cb, sc, x, w, grad_one, dq, d_sout, *refs):
    dk = sum_parts(refs[0], refs[1 : 1 + n_other], x.shape[0])
    dv = sum_parts(refs[1 + n_other], refs[2 + n_other : 2 + 2 * n_other], x.shape[0])
    own_out, send_out, buf_a, buf_b, small, total = refs[2 + 2 * n_other :]
    tok = own_out.shape[0]
    g = sc[0]
    store_rel(buf_a, 0, dot_tn(x[...], dq[...]), sc[6], ka, ca)
    store_rel(buf_a, 512 // ka, dot_tn(x[...], dk), sc[6], ka, ca)
    store_rel(buf_b, 0, dot_tn(x[...], dv), sc[7], kb, cb)
    store_rel(buf_b, 512 // kb, d_sout[...], sc[7], kb, cb)
    small[...] = jnp.zeros_like(small)
    small[0:1, :] = col_sum(dq[...])
    small[1:2, :] = col_sum(dv)
    total[...] = (
        grad_one[...]
        + dot_nt(dq[...], w[:, :512])
        + dot_nt(dk, w[:, 512:1024])
        + dot_nt(dv, w[:, 1024:])
    )
    own_out[...] = total[half_rows(g, 0, tok), :]
    send_out[...] = total[half_rows(g, 1, tok), :].astype(bf16)


def target_grad(sc, plan_a, plan_b, x, w, grad_one, dq, d_sout, dks, dvs):
    tokens = x.shape[0]
    tok = tokens // 2
    sds = jax.ShapeDtypeStruct
    vm = pl.BlockSpec(memory_space=pltpu.VMEM)
    n_other = len(dks) - 1
    keys = [vm] * (1 + n_other)
    return pl.pallas_call(
        functools.partial(target_grad_kernel, n_other, plan_a.k, plan_a.chunks, plan_b.k, plan_b.chunks),
        in_specs=[smem()] + [vm] * 5 + keys + keys,
        out_specs=[vm] * 5,
        out_shape=[
            sds((tok, 512), f32),
            sds((tok, 512), bf16),
            sds((1024, 512), bf16),
            sds((1024, 512), bf16),
            sds((8, 512), f32),
        ],
        scratch_shapes=[pltpu.VMEM((tokens, 512), f32)],
        compiler_params=params(),
        cost_estimate=cost(12 * tokens * 512 * 512, 8e6),
        name="target_grad",
    )(sc, x, w, grad_one, dq, d_sout, *dks, *dvs)


def per_device(
    target, memory, tgt_group, src_group, self_qkv, self_out, self_bias, cross_q, cross_kv, cross_out,
    cross_bias, ffn_in, ffn_in_bias, ffn_out, ffn_out_bias, norm_gain, norm_bias, cotangent,
):
    rows_here, tok, width = target.shape
    ff = ffn_in.shape[1]
    seq, rows = lax.axis_size("seq"), lax.axis_size("rows")
    members = seq // 2
    s, r = lax.axis_index("seq"), lax.axis_index("rows")
    g = s // members
    t = jnp.where(g == 0, s, seq - 1 - s)

    dim_c = ("seq", 1, 2, s % 2)
    dim_x = ("seq", 2, seq // 2, s // 2)
    dim_y = ("rows", 1, 2, r % 2)
    dim_z = ("rows", 2, rows // 2, r // 2)
    order_a = [dim_c, dim_x, dim_y, dim_z]
    order_b = [dim_c, dim_y, dim_x, dim_z]
    ffa, ffb = Plan(order_a, ff), Plan(order_b, ff)
    pa, pb = Plan(order_a, 1024), Plan(order_b, 1024)
    sc = jnp.stack([g, t, ffa.place, ffb.place, pb.place, pa.place, pa.place, pb.place]).astype(jnp.int32)

    def partner(x):
        return swap(x, "seq", seq - 1)

    def others_of(x):
        return [swap(x, "seq", j) for j in range(1, members)]

    def pick(x, which):
        return lax.dynamic_index_in_dim(x, g if which == 0 else 1 - g, 0, keepdims=False)

    def home(own, back):
        back = back.astype(f32)
        return jnp.where(g == 0, jnp.stack([own, back]), jnp.stack([back, own]))

    ids = jnp.stack([tgt_group, src_group]).astype(f32)
    ids_own = lax.dynamic_index_in_dim(ids, g, 1, keepdims=False)
    ids_recv = partner(lax.dynamic_index_in_dim(ids, 1 - g, 1, keepdims=False))
    tgt_recv = partner(pick(target, 1))
    mem_recv = partner(pick(memory, 1))
    cot_recv = partner(pick(cotangent, 1))
    ids_here = jnp.concatenate(
        [jnp.where(g == 0, ids_own, ids_recv), jnp.where(g == 0, ids_recv, ids_own)], axis=1
    )
    ids_all = jnp.concatenate([ids_here] + others_of(ids_here), axis=1)

    zero = jnp.zeros((width,), f32)
    qkv_bias = jnp.concatenate([self_bias[0], zero, self_bias[1]])[None]
    kv_bias = jnp.concatenate([zero, cross_bias[1]])[None]
    x, q1, k1, v1 = embed("embed_target", sc, target, tgt_recv, self_qkv, qkv_bias, (SCALE, 1.0, 1.0))
    k1s, v1s = [k1] + others_of(k1), [v1] + others_of(v1)
    xm, k2, v2 = embed("embed_memory", sc, memory, mem_recv, cross_kv, kv_bias, (1.0, 1.0))
    k2s, v2s = [k2] + others_of(k2), [v2] + others_of(v2)

    mixed1, lse1 = attend("self_attend", True, sc, ids_all, q1, k1s, v1s)
    n0, r0, q2 = after_self(x, mixed1, self_out, self_bias, norm_gain, norm_bias, cross_q, cross_bias)
    mixed2, lse2 = attend("cross_attend", False, sc, ids_all, q2, k2s, v2s)
    own_y, send_y, d_in, d_out, d_cout, small_mid, grad_two, grad_mixed2, delta2 = middle(
        sc, ffa, ffb, n0, mixed2, cross_out, cross_bias, norm_gain, norm_bias, ffn_in, ffn_in_bias[None],
        ffn_out, ffn_out_bias[None], cotangent, cot_recv,
    )
    layer_out = home(own_y, partner(send_y))

    red_in, red_out = reduce_scatter(d_in, ffa), reduce_scatter(d_out, ffb)
    got_in, got_out = all_gather(red_in, ffa), all_gather(red_out, ffb)
    nb = ff // 512
    d_ffn_in = unpack(
        "unpack_in", [(*got_in, ffa)], (512, ff), lambda q: (0, q), [(0, b) for b in range(nb)]
    )
    d_ffn_out = unpack(
        "unpack_out", [(*got_out, ffb)], (ff, 512), lambda q: (q, 0), [(0, b) for b in range(nb)]
    )

    dq2, dk2, dv2 = attend_back("cross_back", False, sc, ids_all, q2, grad_mixed2, lse2, delta2, k2s, v2s)

    def home_parts(d):
        tokens = 2 * tok
        return [d] + [swap(d[j * tokens : (j + 1) * tokens], "seq", j) for j in range(1, members)]

    buf_b, d_sout, small_cross, grad_one, grad_mixed1, delta1 = after_cross(
        sc, pb, dq2, grad_two, n0, r0, cross_q, mixed1, self_out, norm_gain, norm_bias, d_cout
    )
    own_m, send_m, buf_a, small_mem = memory_grad(sc, pa, xm, cross_kv, home_parts(dk2), home_parts(dv2))
    d_memory = home(own_m, partner(send_m))
    got_a = all_gather(reduce_scatter(buf_a, pa), pa)
    got_b = all_gather(reduce_scatter(buf_b, pb), pb)
    d_cross_kv = unpack("unpack_kv", [(*got_a, pa)], (512, 1024), lambda q: (0, q), [(0, 0), (0, 1)])
    d_cross_out = unpack("unpack_co", [(*got_b, pb)], (512, 512), lambda q: (0, 0), [(0, 0)])
    d_cross_q = unpack("unpack_cq", [(*got_b, pb)], (512, 512), lambda q: (0, 0), [(0, 1)])

    dq1, dk1, dv1 = attend_back("self_back", True, sc, ids_all, q1, grad_mixed1, lse1, delta1, k1s, v1s)
    own_t, send_t, buf_c, buf_d, small_tgt = target_grad(
        sc, pa, pb, x, self_qkv, grad_one, dq1, d_sout, home_parts(dk1), home_parts(dv1)
    )
    d_target = home(own_t, partner(send_t))
    got_c = all_gather(reduce_scatter(buf_c, pa), pa)
    got_d = all_gather(reduce_scatter(buf_d, pb), pb)
    d_self_qkv = unpack(
        "unpack_qkv", [(*got_c, pa), (*got_d, pb)], (512, 1536), lambda q: (0, q), [(0, 0), (0, 1), (1, 0)]
    )
    d_self_out = unpack("unpack_so", [(*got_d, pb)], (512, 512), lambda q: (0, 0), [(0, 1)])

    small = jnp.concatenate([small_mid, small_cross, small_mem, small_tgt], axis=0)
    for axis, base, m, _ in order_a:
        if m > 1:
            small = add_all([small] + [swap(small, axis, j * base) for j in range(1, m)])
    mid = small_mid.shape[0]
    crs, mem, tg = small[mid:], small[mid + 8 :], small[mid + 16 :]
    d_self_bias = jnp.stack([tg[0], tg[1], crs[3]])
    d_cross_bias = jnp.stack([crs[2], mem[0], small[5]])
    d_ffn_in_bias = small[8 : 8 + nb].reshape(ff)
    d_norm_gain = jnp.stack([crs[0], small[3], small[0]])
    d_norm_bias = jnp.stack([crs[1], small[4], small[1]])
    return (
        layer_out, d_target, d_memory, d_self_qkv, d_self_out, d_self_bias, d_cross_q, d_cross_kv,
        d_cross_out, d_cross_bias, d_ffn_in, d_ffn_in_bias, d_ffn_out, small[2], d_norm_gain, d_norm_bias,
    )


def solution(mesh):
    sharded, ids, copied = P("rows", "seq", None), P("rows", "seq"), P()
    in_specs = (sharded, sharded, ids, ids) + (copied,) * 13 + (sharded,)
    out_specs = (sharded,) * 3 + (copied,) * 13
    return jax.shard_map(per_device, mesh=mesh, in_specs=in_specs, out_specs=out_specs, check_vma=False)
```

```python
import functools
import math

import jax
import jax.numpy as jnp
from jax import lax
from jax.experimental import pallas as pl
from jax.experimental.pallas import tpu as pltpu
from jax.sharding import PartitionSpec as P

HEADS = 8
PAIR = 128
EPS = 1e-05
SCALE = 0.125
NEG = -1e30
VMEM = 16 * 1024 * 1024
CROSS_SPLIT, SELF_SPLIT = (1, 3), (2, 2)
MEMORY_FIRST, CUT_FF, BACK_EARLY = True, False, False
FORCE_FIRST, FORCE_SECOND = 3, 1
ORDER = (1, 1, 3, 2, 9, 3, 3, 2, 3, 1, 3, 2, 2, 7, 3, 8, 2)
bf16 = jnp.bfloat16
f32 = jnp.float32


def params():
    return pltpu.CompilerParams(vmem_limit_bytes=VMEM)


def cost(flops, nbytes, trans=0):
    return pl.CostEstimate(flops=int(flops), bytes_accessed=int(nbytes), transcendentals=int(trans))


def dot(a, b):
    return jnp.dot(a, b, preferred_element_type=f32)


def dot_nt(a, b):
    return lax.dot_general(a, b, (((1,), (1,)), ((), ())), preferred_element_type=f32)


def dot_tn(a, b):
    return lax.dot_general(a, b, (((0,), (0,)), ((), ())), preferred_element_type=f32)


def col_sum(v):
    return jnp.sum(v.astype(f32), axis=0, keepdims=True)


def normalize(h):
    mean = jnp.mean(h, axis=-1, keepdims=True)
    c = h - mean
    r = lax.rsqrt(jnp.mean(c * c, axis=-1, keepdims=True) + EPS)
    return c * r, r


def norm_back(u, n, r, gain):
    w = u * gain
    return r * (
        w
        - jnp.mean(w, axis=-1, keepdims=True)
        - n * jnp.mean(w * n, axis=-1, keepdims=True)
    )


def whole(shape):
    return pl.BlockSpec(shape, lambda *_: (0,) * len(shape))


def smem():
    return pl.BlockSpec(memory_space=pltpu.SMEM)


def half_rows(g, which, count):
    at = g if which == 0 else 1 - g
    return pl.ds(pl.multiple_of(at * count, count), count)


class Plan:
    def __init__(self, cut, whole, n, digit, minimum=16):
        first = (("seq", 1), ("seq", 1))
        self.scatter, self.everywhere = [], list(whole)
        k = n
        places = [0, 0]
        for step in [first] + list(cut):
            if k % 2 == 0 and k // 2 >= minimum:
                self.scatter.append(step)
                k //= 2
                places = [place * 2 + digit(*bit) for place, bit in zip(places, step)]
            else:
                self.everywhere.append(step)
        self.n, self.k, self.chunks = n, k, n // k
        self.half = self.chunks // 2
        self.places = [place % self.half for place in places]


def swap(x, axis, off):
    size = lax.axis_size(axis)
    return lax.ppermute(x, axis, [(i, i ^ off) for i in range(size)])


def exchange(x, step):
    if step[0] == step[1]:
        return swap(x, *step[0])
    rows, seq = lax.axis_size("rows"), lax.axis_size("seq")
    pairs = []
    for r in range(rows):
        for s in range(seq):
            axis, off = step[s % 2]
            to = ((r ^ off) * seq + s) if axis == "rows" else (r * seq + (s ^ off))
            pairs.append((r * seq + s, to))
    return lax.ppermute(x, ("rows", "seq"), pairs)


CORE, FF_PLACES, W_PLACES = 2, 3, 5


def store_rel(both, value, sc, k, cols):
    half = value.shape[0] // k // 2
    for core in range(2):
        side = jnp.bitwise_xor(sc[CORE], core)
        for w in range(half):
            at = jnp.bitwise_xor(sc[W_PLACES + core], w)
            row = (core * half + w) * k
            both[side, pl.ds(pl.multiple_of(at * k, k), k), cols] = value[row : row + k].astype(both.dtype)


def place_of(q, half_blocks, sc):
    return jnp.where(q < half_blocks, sc[FF_PLACES], sc[FF_PLACES + 1])


def block_of(q, half_blocks, per, sc):
    return jnp.bitwise_xor(q % half_blocks, place_of(q, half_blocks, sc) // per)


def half_block(mine, half_blocks, per):
    def index(q, sc):
        core = sc[CORE] if mine else 1 - sc[CORE]
        return block_of(jnp.clip(q, core * half_blocks, (core + 1) * half_blocks - 1), half_blocks, per, sc), 0

    return index


def store_half(keep, send, make, q, half_blocks, sc, k):
    here = (q // half_blocks) == sc[CORE]
    for mine, ref in ((True, keep), (False, send)):

        @pl.when(here == mine)
        def _():
            store_block(ref, make(), place_of(q, half_blocks, sc), k)


def store_narrow(both, value, half_blocks, sc, k):
    share, per = value.shape[1] // (2 * half_blocks), 512 // k
    for q in range(2 * half_blocks):
        core = q // half_blocks
        side = jnp.bitwise_xor(sc[CORE], core)
        place = sc[FF_PLACES + core]
        for w in range(per):
            at = jnp.bitwise_xor(place, (q % half_blocks) * per + w) * k
            both[side, pl.ds(pl.multiple_of(at, k), k), :] = value[
                w * k : (w + 1) * k, q * share : (q + 1) * share
            ].astype(both.dtype)


def store_block(ref, value, place, k):
    per = value.shape[0] // k
    for w in range(per):
        at = jnp.bitwise_xor(place % per, w)
        ref[pl.ds(pl.multiple_of(at * k, k), k), :] = value[w * k : (w + 1) * k].astype(ref.dtype)


def wide(zero, width):
    if jnp.ndim(zero) < 2:
        return zero
    return jnp.pad(zero, ((0, 0), (0, width - zero.shape[1])))


class Chain:
    def __init__(self, plan):
        self.plan, self.parts, self.other, self.after = plan, [], None, 0.0
        self.todo = [("rs", d) for d in plan.scatter[1:]] + [("all", d) for d in plan.everywhere]
        self.todo += [("ag", d) for d in reversed(plan.scatter[1:])] + [("last", plan.scatter[0])]

    def sum(self, mine, got):
        return (mine.astype(f32) + got.astype(f32) + wide(self.after, mine.shape[1])).astype(bf16)

    def add(self, keep, send):
        got = exchange(send, self.plan.scatter[0])
        self.parts.append(self.sum(keep, got))
        return self.parts[-1]

    def join(self):
        if self.parts:
            self.buf = jnp.concatenate(self.parts, axis=1)
            self.parts = []

    def step(self, after=0.0):
        self.after = after
        self.join()
        kind, step = self.todo.pop(0)
        buf = self.buf
        if kind == "rs":
            half = buf.shape[0] // 2
            self.buf = self.sum(buf[:half], exchange(buf[half:], step))
        elif kind == "all":
            self.buf = self.sum(buf, exchange(buf, step))
        elif kind == "ag":
            got = exchange(buf, step).astype(f32) + wide(after, buf.shape[1])
            self.buf = jnp.concatenate([buf, got.astype(bf16)], axis=0)
        else:
            self.other = exchange(buf, step)
        return self.buf

    def finish(self):
        while self.todo:
            self.step()

    def zero(self):
        return self.buf[0:1, :PAIR].astype(f32) * 0.0


def call(kernel, operands, in_specs, out_specs, out_shape, name, work, scratch=(), grid=None, scalars=(), deps=(), vmem=VMEM):
    n_front, n_deps = len(scalars) + len(operands), len(deps)

    def body(*refs):
        kernel(*refs[:n_front], *refs[n_front + n_deps :])

    specs = list(in_specs) + [pl.BlockSpec(memory_space=pl.ANY)] * n_deps
    common = dict(
        out_shape=out_shape,
        compiler_params=pltpu.CompilerParams(vmem_limit_bytes=vmem),
        cost_estimate=work,
        name=name,
    )
    if scalars:
        spec = pltpu.PrefetchScalarGridSpec(
            num_scalar_prefetch=len(scalars), grid=grid, in_specs=specs, out_specs=out_specs, scratch_shapes=list(scratch)
        )
        return pl.pallas_call(body, grid_spec=spec, **common)(*scalars, *operands, *deps)
    if grid is not None:
        common["grid"] = grid
    return pl.pallas_call(
        body, in_specs=specs, out_specs=out_specs, scratch_shapes=list(scratch), **common
    )(*operands, *deps)


def unpack(name, sc, places, chain, outs, rows=(), deps=()):
    own, other = chain.buf, chain.other
    half, k = own.shape[0], chain.plan.k
    blocks = half // 512 if half >= 512 else 1
    size = half // blocks
    n_out = len(outs)

    def kernel(sc, own_ref, other_ref, *refs):
        goal, narrow, done = refs[:n_out], refs[n_out : n_out + len(rows)], refs[n_out + len(rows)]
        stage, sems = refs[-2:]
        done[0, 0] = 0.0
        copies = []
        for side, src in enumerate((own_ref, other_ref)):
            core = jnp.bitwise_xor(sc[CORE], side)
            place = sc[places + core]
            for w in range(half // k):
                at = pl.multiple_of(jnp.bitwise_xor(place, w) * k, k)
                stage[side, pl.ds(at, k), :] = src[w * k : (w + 1) * k, :].astype(f32)
            for i, (shape, first, width, by) in enumerate(outs):
                cols = slice(first, first + width)
                if by == 0:
                    to = goal[i].at[pl.ds(pl.multiple_of(core * half, half), half), :]
                    copies.append(pltpu.make_async_copy(stage.at[side, :, cols], to, sems.at[len(copies)]))
                    copies[-1].start()
                    continue
                for b in range(blocks):
                    at = pl.multiple_of((core * blocks + b) * width, width)
                    to = goal[i].at[:, pl.ds(at, width)]
                    copies.append(
                        pltpu.make_async_copy(stage.at[side, b * size : (b + 1) * size, cols], to, sems.at[len(copies)])
                    )
                    copies[-1].start()
        if rows:
            last = chain.buf.shape[1] - PAIR
            mine, far = stage[0, :, last:], stage[1, :, last:]
            straight = sc[CORE] == 0
            turned = jnp.transpose(
                jnp.concatenate([jnp.where(straight, mine, far), jnp.where(straight, far, mine)], axis=0)
            )
            for ref, picks in zip(narrow, rows):
                for i, pick in enumerate(picks):
                    ref[i : i + 1, :] = turned[pick : pick + 1, :]
        for copy in copies:
            copy.wait()

    vm = pl.BlockSpec(memory_space=pltpu.VMEM)
    n_copies = sum(2 * (1 if out[3] == 0 else blocks) for out in outs)
    shapes = [jax.ShapeDtypeStruct(out[0], f32) for out in outs]
    shapes += [jax.ShapeDtypeStruct((len(picks), 512), f32) for picks in rows]
    return call(
        kernel, [sc, own, other], [smem(), vm, vm], [hbm()] * n_out + [vm] * len(rows) + [smem()],
        shapes + [jax.ShapeDtypeStruct((1, 1), f32)], name, cost(0, 12 * own.size),
        scratch=[pltpu.VMEM((2,) + own.shape, f32), pltpu.SemaphoreType.DMA((n_copies,))], deps=deps, vmem=24 << 20,
    )


def hbm():
    return pl.BlockSpec(memory_space=pltpu.HBM)


def project_kernel(scales, biases, sc, tgt, w, b, out, tgt_vm, w_vm, sems):
    copies = [
        pltpu.make_async_copy(tgt.at[sc[0]], tgt_vm, sems.at[0]),
        pltpu.make_async_copy(w, w_vm, sems.at[1]),
    ]
    for copy in copies:
        copy.start()
    for copy in copies:
        copy.wait()
    write_parts(dot(tgt_vm[...], w_vm[...]), scales, biases, b, out, slice(None))


def write_parts(y, scales, biases, b, outs, rows):
    for i, (scale, bias) in enumerate(zip(scales, biases)):
        cols = slice(i * 512, (i + 1) * 512)
        piece = y[:, cols] if bias is None else y[:, cols] + b[bias : bias + 1, :]
        piece = piece.astype(bf16)
        if scale != 1.0:
            piece = (piece.astype(f32) * scale).astype(bf16)
        if isinstance(outs, (tuple, list)):
            outs[i][rows, :] = piece
        else:
            outs[rows, cols] = piece


def embed_own(name, sc, local, w, b, scales, biases, deps=()):
    tok = local.shape[1]
    vm = pl.BlockSpec(memory_space=pltpu.VMEM)
    return call(
        functools.partial(project_kernel, scales, biases), [sc, local, w, b], [smem(), hbm(), hbm(), vm], vm,
        jax.ShapeDtypeStruct((tok, w.shape[1]), bf16), name, cost(2 * tok * 512 * w.shape[1], 3e6),
        scratch=[pltpu.VMEM((tok, 512), bf16), pltpu.VMEM(w.shape, bf16), pltpu.SemaphoreType.DMA((2,))], deps=deps,
    )


def embed_kernel(scales, biases, sc, tgt, recv, done, w, b, x_out, *refs):
    outs, (tgt_vm, w_vm, sems) = refs[:-3], refs[-3:]
    g = sc[0]
    tok = tgt.shape[1]
    copies = [
        pltpu.make_async_copy(tgt.at[g], tgt_vm, sems.at[0]),
        pltpu.make_async_copy(w, w_vm, sems.at[1]),
    ]
    for copy in copies:
        copy.start()
    own, far = half_rows(g, 0, tok), half_rows(g, 1, tok)
    x_out[far, :] = recv[...]
    for i, out in enumerate(outs):
        out[own, :] = done[:, i * 512 : (i + 1) * 512]
    for copy in copies:
        copy.wait()
    x_out[own, :] = tgt_vm[...]
    write_parts(dot(recv[...], w_vm[...]), scales, biases, b, outs, far)


def embed(name, sc, local, recv, done, w, b, scales, biases, deps=()):
    tok = local.shape[1]
    one = jax.ShapeDtypeStruct((2 * tok, 512), bf16)
    vm = pl.BlockSpec(memory_space=pltpu.VMEM)
    return call(
        functools.partial(embed_kernel, scales, biases), [sc, local, recv, done, w, b],
        [smem(), hbm(), vm, vm, hbm(), vm], [vm] * (1 + len(scales)), [one] * (1 + len(scales)), name,
        cost(2 * tok * 512 * w.shape[1], 4e6),
        scratch=[pltpu.VMEM((tok, 512), bf16), pltpu.VMEM(w.shape, bf16), pltpu.SemaphoreType.DMA((2,))], deps=deps,
    )


BIG = 2.0**100


def to_cols(row):
    return jnp.transpose(jnp.broadcast_to(row, (PAIR, row.shape[1])))


def halves(parts, tok, axis=0):
    cut = (lambda e, at: e[at : at + tok]) if axis == 0 else (lambda e, at: e[:, at : at + tok])
    return jnp.concatenate([cut(e, 0) for e in parts] + [cut(e, tok) for e in parts], axis=axis)


def key_mask(causal, t, ids, tok, axis):
    length = ids.shape[1]
    members = length // (2 * tok)
    group = ids[0:1, :] if causal else ids[1:2, :]
    group = halves([group[:, 2 * tok * j : 2 * tok * (j + 1)] for j in range(members)], tok, 1)
    shape = (PAIR, length) if axis == 0 else (length, PAIR)
    if axis == 1:
        group = to_cols(group)
    feature = lax.broadcasted_iota(jnp.int32, shape, axis) % 64
    out = jnp.where((feature < 5) & (group + 1.0 != feature.astype(f32)), -BIG, 0.0)
    out = jnp.where((feature >= 5) & (feature < 8), 1.0, out)
    if causal:
        at = lax.broadcasted_iota(jnp.int32, shape, 1 - axis)
        low = jnp.bitwise_xor((at % (members * tok)) // tok, t)
        second = at >= members * tok
        out = jnp.where((feature == 8) & (second | (low > t)), -BIG, out)
        out = jnp.where((feature == 9) & second & (low < t), -BIG, out)
    return out.astype(bf16)


def query_mask(ids, tok, axis):
    group = ids[0:1, : 2 * tok]
    shape = (PAIR, 2 * tok) if axis == 0 else (2 * tok, PAIR)
    if axis == 1:
        group = to_cols(group)
    feature = lax.broadcasted_iota(jnp.int32, shape, axis) % 64
    second = (lax.broadcasted_iota(jnp.int32, shape, 1 - axis) >= tok).astype(jnp.int32)
    hot = (feature < 5) & (group + 1.0 == feature.astype(f32))
    return jnp.where(hot | (feature == 8 + second), 1.0, 0.0).astype(bf16)


def mixed_in(h, axis, mine, other):
    return jnp.where(lax.broadcasted_iota(jnp.int32, mine.shape, axis) // 64 == h, mine, other)


def with_own(s, at, later, axis):
    end, size = at + later.shape[0], s.shape[axis]
    cut = (lambda i, j: s[i:j]) if axis == 0 else (lambda i, j: s[:, i:j])
    pieces = [cut(0, at)] if at else []
    pieces.append(cut(at, end) + later)
    if end < size:
        pieces.append(cut(end, size))
    return jnp.concatenate(pieces, axis=axis) if len(pieces) > 1 else pieces[0]


def blocks_of(causal, tok, length):
    if not causal:
        return [(slice(0, 2 * tok), length, None)]
    return [(slice(0, tok), length // 2, 0), (slice(tok, 2 * tok), length, length // 2)]


def attend_kernel(causal, tok, members, sc, ids, q, *refs):
    out, lse, keys_side, queries_side = refs[2 * members :]
    length = 2 * tok * members

    @pl.when(pl.program_id(0) == 0)
    def _():
        keys_side[...] = key_mask(causal, sc[1], ids[...], tok, 1)
        queries_side[...] = query_mask(ids[...], tok, 0)

    k = halves([ref[...] for ref in refs[:members]], tok)
    v = jnp.transpose(halves([ref[...] for ref in refs[members : 2 * members]], tok))
    qt = jnp.transpose(q[...])
    key_at = lax.broadcasted_iota(jnp.int32, (tok, tok), 0)
    later = jnp.where(key_at > lax.broadcasted_iota(jnp.int32, (tok, tok), 1), NEG, 0.0)
    ones = jnp.ones((64, length), bf16)
    parts = []
    for h in range(2):
        kh = mixed_in(h, 1, k, keys_side[...])
        qh = mixed_in(h, 0, qt, queries_side[...])
        vh = jnp.concatenate([v[h * 64 : (h + 1) * 64], ones], axis=0)
        row = []
        for cols, seen, own in blocks_of(causal, tok, length):
            s = dot(kh[:seen], qh[:, cols])
            if own is not None:
                s = with_own(s, own, later, 0)
            top = jnp.max(s, axis=0, keepdims=True)
            got = dot(vh[:, :seen], jnp.exp(s - top).astype(bf16))
            total = got[64:65]
            row.append(got[:64] * (1.0 / total))
            lse[0, h : h + 1, cols] = top + jnp.log(total)
        parts.append(jnp.concatenate(row, axis=1))
    out[...] = jnp.transpose(jnp.concatenate(parts, axis=0)).astype(bf16)


def attend_vmem(length):
    return min(VMEM * max(length // 1024, 1), 60 * 1024 * 1024)


def attend(name, causal, sc, ids, q, ks, vs, deps=()):
    tokens = q.shape[0]
    length = ids.shape[1]
    members = len(ks)
    pair = pl.BlockSpec((tokens, PAIR), lambda p: (0, p))
    return call(
        functools.partial(attend_kernel, causal, tokens // 2, members),
        [sc, ids, q, *ks, *vs],
        [smem(), whole(ids.shape)] + [pair] * (1 + 2 * members),
        [pair, pl.BlockSpec((1, 2, tokens), lambda p: (p, 0, 0))],
        [jax.ShapeDtypeStruct((tokens, 512), bf16), jax.ShapeDtypeStruct((4, 2, tokens), f32)],
        name,
        cost(42 * tokens * length * 512, 4e6, 8 * tokens * length),
        scratch=[pltpu.VMEM((length, PAIR), bf16), pltpu.VMEM((PAIR, tokens), bf16)],
        grid=(4,),
        deps=deps,
        vmem=attend_vmem(length),
    )


def three(x):
    a = x.astype(bf16)
    rest = x - a.astype(f32)
    b = rest.astype(bf16)
    return a, b, (rest - b.astype(f32)).astype(bf16)


def with_terms(side, terms):
    feature = lax.broadcasted_iota(jnp.int32, side.shape, 1) % 64
    for i, term in enumerate(terms):
        side = jnp.where(feature == 5 + i, term, side)
    return side


def attend_back_kernel(causal, tok, members, sc, ids, q, grad, lse, delta, *refs):
    dq, own_out, far, done, keys_side, queries_side = refs[2 * members :]
    done[0, 0] = 0.0
    length = 2 * tok * members

    @pl.when(pl.program_id(0) == 0)
    def _():
        keys_side[...] = key_mask(causal, sc[1], ids[...], tok, 0)
        queries_side[...] = query_mask(ids[...], tok, 1)

    k = halves([ref[...] for ref in refs[:members]], tok)
    v = halves([ref[...] for ref in refs[members : 2 * members]], tok)
    kt, vt = jnp.transpose(k), jnp.transpose(v)
    qt, gt = jnp.transpose(q[...]), jnp.transpose(grad[...])
    zero = jnp.zeros((), bf16)
    feature = lax.broadcasted_iota(jnp.int32, (PAIR, length), 0) % 64
    ones = jnp.where((feature >= 5) & (feature < 8), 1.0, 0.0).astype(bf16)
    key_at = lax.broadcasted_iota(jnp.int32, (tok, tok), 1)
    later = jnp.where(key_at > lax.broadcasted_iota(jnp.int32, (tok, tok), 0), NEG, 0.0)
    half = length // 2
    grad_k, grad_v, grad_q = [None, None], [None, None], {}

    def plus(total, term):
        return term if total is None else total + term

    for h in range(2):
        minus_lse, minus_delta = to_cols(-lse[0, h : h + 1, :]), to_cols(-delta[0, h : h + 1, :])
        qh = mixed_in(h, 1, q[...], with_terms(queries_side[...], three(minus_lse)))
        gh = mixed_in(h, 1, grad[...], with_terms(jnp.zeros((2 * tok, PAIR), bf16), three(minus_delta)))
        kh, vh = mixed_in(h, 0, kt, keys_side[...]), mixed_in(h, 0, vt, ones)
        k_only, q_only, g_only = mixed_in(h, 1, k, zero), mixed_in(h, 0, qt, zero), mixed_in(h, 0, gt, zero)
        for b in range(2):
            rows = slice(b * tok, (b + 1) * tok)
            seen = half if causal and b == 0 else length
            s = dot(qh[rows], kh[:, :seen])
            if causal:
                own = b * half
                s = with_own(s, own, later, 1)
            p = jnp.exp(s)
            ds = (p * dot(gh[rows], vh[:, :seen])).astype(bf16)
            got_v, got_k = dot(g_only[:, rows], p.astype(bf16)), dot(q_only[:, rows], ds)
            for i in range(seen // half):
                cols = slice(i * half, (i + 1) * half)
                grad_v[i], grad_k[i] = plus(grad_v[i], got_v[:, cols]), plus(grad_k[i], got_k[:, cols])
            grad_q[b] = plus(grad_q.get(b), dot(ds, k_only[:seen]))
    for b in range(2):
        dq[b * tok : (b + 1) * tok, :] = (grad_q[b] * SCALE).astype(bf16)
    for i, total in enumerate((grad_k, grad_v)):
        for b in range(2):
            value = jnp.transpose(total[b]).astype(bf16)
            for j in range(members):
                ref = far if j else own_out
                at = (2 * j - 2 if j else 0) * tok + b * tok
                ref[i, at : at + tok, :] = value[j * tok : (j + 1) * tok]


def attend_back(name, causal, sc, ids, q, grad, lse, delta, ks, vs, first, count, deps=()):
    tokens = q.shape[0]
    length = ids.shape[1]
    members = len(ks)
    pair = pl.BlockSpec((tokens, PAIR), lambda p: (0, p + first))
    row = pl.BlockSpec((1, 2, tokens), lambda p: (p + first, 0, 0))
    width = count * PAIR
    sds = jax.ShapeDtypeStruct
    return call(
        functools.partial(attend_back_kernel, causal, tokens // 2, members),
        [sc, ids, q, grad, lse, delta, *ks, *vs],
        [smem(), whole(ids.shape), pair, pair, row, row] + [pair] * (2 * members),
        [
            pl.BlockSpec((tokens, PAIR), lambda p: (0, p)),
            pl.BlockSpec((2, tokens, PAIR), lambda p: (0, 0, p)),
            pl.BlockSpec((2, length - tokens, PAIR), lambda p: (0, 0, p)),
            smem(),
        ],
        [
            sds((tokens, width), bf16),
            sds((2, tokens, width), bf16),
            sds((2, length - tokens, width), bf16),
            sds((1, 1), f32),
        ],
        name,
        cost(17 * count * tokens * length * 512, 2e6 * count, 2 * count * tokens * length),
        scratch=[pltpu.VMEM((PAIR, length), bf16), pltpu.VMEM((tokens, PAIR), bf16)],
        grid=(count,),
        deps=deps,
        vmem=attend_vmem(length),
    )


def after_self_kernel(x, mixed, w_out, sbias, gain, shift, w_q, cbias, n0, r0, q2):
    h = x[...].astype(f32) + dot(mixed[...], w_out[...]) + sbias[2:3, :]
    n, r = normalize(h)
    n0[...] = n
    r0[...] = r
    first = n * gain[0:1, :] + shift[0:1, :]
    q = dot(first.astype(bf16), w_q[...]) + cbias[0:1, :]
    q2[...] = (q.astype(bf16).astype(f32) * SCALE).astype(bf16)


def after_self(x, mixed, w_out, sbias, gain, shift, w_q, cbias):
    tokens = x.shape[0]
    vm = pl.BlockSpec(memory_space=pltpu.VMEM)
    return pl.pallas_call(
        after_self_kernel,
        in_specs=[vm] * 8,
        out_specs=[vm] * 3,
        out_shape=[
            jax.ShapeDtypeStruct((tokens, 512), f32),
            jax.ShapeDtypeStruct((tokens, 1), f32),
            jax.ShapeDtypeStruct((tokens, 512), bf16),
        ],
        compiler_params=params(),
        cost_estimate=cost(4 * tokens * 512 * 512, 4e6),
        name="after_self",
    )(x, mixed, w_out, sbias, gain, shift, w_q, cbias)


def head_sums(a, b):
    prod = a * b
    high = prod.astype(bf16)
    low = (prod - high.astype(f32)).astype(bf16)
    pick = (
        lax.broadcasted_iota(jnp.int32, (HEADS, 512), 1) // 64
        == lax.broadcasted_iota(jnp.int32, (HEADS, 512), 0)
    ).astype(bf16)
    return dot_nt(pick, high) + dot_nt(pick, low)


def put_head_rows(ref, rows):
    for p in range(4):
        ref[p] = rows[2 * p : 2 * p + 2]


def gelu_parts(v):
    c = math.sqrt(2.0 / math.pi)
    v2 = v * v
    t = jnp.tanh(c * v * (1.0 + 0.044715 * v2))
    half = 0.5 * (1.0 + t)
    slope = half + 0.5 * v * (1.0 - t * t) * (c * (1.0 + 3.0 * 0.044715 * v2))
    return v * half, slope


def ffn_forward_kernel(
    chunks, k_out, sc, n0, mixed, cout, cbias, gain, shift, w_in, b_in, w_out, b_out, cot, cot_recv,
    own_out, send_out, d_keep, d_send, small, slope, low, n1, r1, grad_three, outer, inner, total,
):
    i = pl.program_id(0)
    g = sc[0]
    tok = cot_recv.shape[0]

    @pl.when(i == 0)
    def _():
        first = n0[...] * gain[0:1, :] + shift[0:1, :]
        n, r = normalize(first + dot(mixed[...], cout[...]) + cbias[2:3, :])
        n1[...] = n
        r1[...] = r
        second = n * gain[1:2, :] + shift[1:2, :]
        low[...] = second.astype(bf16)
        total[...] = second + b_out[...]
        small[...] = jnp.zeros_like(small)

    @pl.when(i < chunks)
    def _():
        pre = dot(low[...], w_in[...]) + b_in[...]
        act, grad_act = gelu_parts(pre)
        act = act.astype(bf16)
        inner[i] = act
        slope[...] = grad_act.astype(bf16)
        total[...] += dot(act, w_out[...])

    @pl.when(i == chunks - 1)
    def _():
        n, r = normalize(total[...])
        result = n * gain[2:3, :] + shift[2:3, :]
        total[...] = result
        own_out[...] = total[half_rows(g, 0, tok), :]
        send_out[...] = total[half_rows(g, 1, tok), :].astype(bf16)
        total[half_rows(g, 0, tok), :] = cot[g].astype(f32)
        total[half_rows(g, 1, tok), :] = cot_recv[...].astype(f32)
        u = total[...]
        small[0:1, :] = col_sum(u * n)
        small[1:2, :] = col_sum(u)
        back = norm_back(u, n, r, gain[2:3, :])
        grad_three[...] = back
        back_low = back.astype(bf16)
        outer[...] = back_low
        small[2:3, :] = col_sum(back_low)

    @pl.when(i >= chunks)
    def _():
        j = i - chunks
        store_half(d_keep, d_send, lambda: dot_tn(inner[j], outer[...]), j, chunks // 2, sc, k_out)


def ffn_forward(sc, plan, n0, mixed, cout, cbias, gain, shift, w_in, b_in, w_out, b_out, cot, cot_recv, deps=()):
    tokens = n0.shape[0]
    tok = tokens // 2
    ff = w_in.shape[1]
    chunks = ff // 512
    sds = jax.ShapeDtypeStruct
    per = 512 // plan.k

    keep, send = half_block(True, chunks // 2, per), half_block(False, chunks // 2, per)

    def now(i):
        return jnp.minimum(i, chunks - 1)

    return call(
        functools.partial(ffn_forward_kernel, chunks, plan.k),
        [n0, mixed, cout, cbias, gain, shift, w_in, b_in, w_out, b_out, cot, cot_recv],
        [
            whole((tokens, 512)),
            whole((tokens, 512)),
            whole((512, 512)),
            whole((3, 512)),
            whole((3, 512)),
            whole((3, 512)),
            pl.BlockSpec((512, 512), lambda i, sc: (0, now(i))),
            pl.BlockSpec((1, 512), lambda i, sc: (0, now(i))),
            pl.BlockSpec((512, 512), lambda i, sc: (now(i), 0)),
            whole((1, 512)),
            whole(cot.shape),
            whole(cot_recv.shape),
        ],
        [
            whole((tok, 512)),
            whole((tok, 512)),
            pl.BlockSpec((512, 512), lambda i, sc: keep(i - chunks, sc)),
            pl.BlockSpec((512, 512), lambda i, sc: send(i - chunks, sc)),
            whole((8, 512)),
            pl.BlockSpec((tokens, 512), lambda i, sc: (0, now(i))),
            whole((tokens, 512)),
            whole((tokens, 512)),
            whole((tokens, 1)),
            whole((tokens, 512)),
            whole((tokens, 512)),
        ],
        [
            sds((tok, 512), f32),
            sds((tok, 512), bf16),
            sds((ff // 2, 512), bf16),
            sds((ff // 2, 512), bf16),
            sds((8, 512), f32),
            sds((tokens, ff), bf16),
            sds((tokens, 512), bf16),
            sds((tokens, 512), f32),
            sds((tokens, 1), f32),
            sds((tokens, 512), f32),
            sds((tokens, 512), bf16),
        ],
        "ffn_forward",
        cost(4 * tokens * 512 * (3 * ff + 512), 1.5e7),
        scratch=[pltpu.VMEM((chunks, tokens, 512), bf16), pltpu.VMEM((tokens, 512), f32)],
        grid=(2 * chunks,),
        scalars=[sc],
        deps=deps,
    )


def ffn_back_kernel(
    chunks, k_in, sc, mixed, cout, gain, w_in, w_out, slope, low, n1, r1, grad_three, outer,
    d_keep, d_send, c_keep, c_send, small, grad_two, grad_mixed, delta, total, both,
):
    i = pl.program_id(0)

    @pl.when(i == 0)
    def _():
        total[...] = grad_three[...]
        small[...] = jnp.zeros_like(small)

    pre_low = (dot_nt(outer[...], w_out[...]) * slope[...].astype(f32)).astype(bf16)
    small[pl.ds(8 + i, 1), :] = col_sum(pre_low)
    store_half(d_keep, d_send, lambda: dot_tn(low[...], pre_low), i, chunks // 2, sc, k_in)
    total[...] += dot_nt(pre_low, w_in[...])

    @pl.when(i == chunks - 1)
    def _():
        u = total[...]
        n = n1[...]
        small[0:1, :] = col_sum(u * n)
        small[1:2, :] = col_sum(u)
        back = norm_back(u, n, r1[...], gain[1:2, :])
        grad_two[...] = back
        back_low = back.astype(bf16)
        small[2:3, :] = col_sum(back_low)
        store_narrow(both, dot_tn(mixed[...], back_low), chunks // 2, sc, k_in)
        c_keep[...] = both[0]
        c_send[...] = both[1]
        g_mixed = dot_nt(back_low, cout[...]).astype(bf16)
        grad_mixed[...] = g_mixed
        put_head_rows(delta, head_sums(g_mixed.astype(f32), mixed[...].astype(f32)))


def ffn_back(sc, plan, mixed, cout, gain, w_in, w_out, slope, low, n1, r1, grad_three, outer, deps=()):
    tokens = mixed.shape[0]
    ff = w_in.shape[1]
    chunks = ff // 512
    sds = jax.ShapeDtypeStruct
    per = 512 // plan.k
    share = 512 // chunks
    return call(
        functools.partial(ffn_back_kernel, chunks, plan.k),
        [mixed, cout, gain, w_in, w_out, slope, low, n1, r1, grad_three, outer],
        [
            whole((tokens, 512)),
            whole((512, 512)),
            whole((3, 512)),
            pl.BlockSpec((512, 512), lambda i, sc: (0, i)),
            pl.BlockSpec((512, 512), lambda i, sc: (i, 0)),
            pl.BlockSpec((tokens, 512), lambda i, sc: (0, i)),
            whole((tokens, 512)),
            whole((tokens, 512)),
            whole((tokens, 1)),
            whole((tokens, 512)),
            whole((tokens, 512)),
        ],
        [
            pl.BlockSpec((512, 512), half_block(True, chunks // 2, per)),
            pl.BlockSpec((512, 512), half_block(False, chunks // 2, per)),
            whole((ff // 2, share)),
            whole((ff // 2, share)),
            whole((8 + chunks + 4, 512)),
            whole((tokens, 512)),
            whole((tokens, 512)),
            whole((4, 2, tokens)),
        ],
        [
            sds((ff // 2, 512), bf16),
            sds((ff // 2, 512), bf16),
            sds((ff // 2, share), bf16),
            sds((ff // 2, share), bf16),
            sds((8 + chunks + 4, 512), f32),
            sds((tokens, 512), f32),
            sds((tokens, 512), bf16),
            sds((4, 2, tokens), f32),
        ],
        "ffn_back",
        cost(4 * tokens * 512 * (3 * ff + 1024), 1.5e7),
        scratch=[pltpu.VMEM((tokens, 512), f32), pltpu.VMEM((2, ff // 2, share), bf16)],
        grid=(chunks,),
        scalars=[sc],
        deps=deps,
    )


def after_cross_kernel(
    n_parts, k, sc, grad_two, n0, r0, w_q, mixed, w_out, gain, shift, *refs
):
    dq = jnp.concatenate([ref[...] for ref in refs[:n_parts]], axis=1)
    keep, send, small, grad_one, grad_mixed, delta, done, both = refs[n_parts:]
    done[0, 0] = 0.0
    n = n0[...]
    first = (n * gain[0:1, :] + shift[0:1, :]).astype(bf16)
    store_rel(both, dot_tn(first, dq), sc, k, slice(0, 512))
    u = grad_two[...] + dot_nt(dq, w_q[...])
    small[...] = jnp.zeros_like(small)
    small[0:1, :] = col_sum(u * n)
    small[1:2, :] = col_sum(u)
    small[2:3, :] = col_sum(dq)
    back = norm_back(u, n, r0[...], gain[0:1, :])
    grad_one[...] = back
    back_low = back.astype(bf16)
    small[3:4, :] = col_sum(back_low)
    store_rel(both, dot_tn(mixed[...], back_low), sc, k, slice(512, 1024))
    keep[...] = both[0]
    send[...] = both[1]
    g_mixed = dot_nt(back_low, w_out[...]).astype(bf16)
    grad_mixed[...] = g_mixed
    put_head_rows(delta, head_sums(g_mixed.astype(f32), mixed[...].astype(f32)))


def after_cross(sc, plan, dqs, grad_two, n0, r0, w_q, mixed, w_out, gain, shift, deps=()):
    tokens = n0.shape[0]
    sds = jax.ShapeDtypeStruct
    vm = pl.BlockSpec(memory_space=pltpu.VMEM)
    return call(
        functools.partial(after_cross_kernel, len(dqs), plan.k),
        [sc, grad_two, n0, r0, w_q, mixed, w_out, gain, shift, *dqs],
        [smem()] + [vm] * (8 + len(dqs)),
        [vm] * 6 + [smem()],
        [
            sds((256, 1024), bf16),
            sds((256, 1024), bf16),
            sds((8, 512), f32),
            sds((tokens, 512), f32),
            sds((tokens, 512), bf16),
            sds((4, 2, tokens), f32),
            sds((1, 1), f32),
        ],
        "after_cross",
        cost(12 * tokens * 512 * 512, 6e6),
        scratch=[pltpu.VMEM((2, 256, 1024), bf16)],
        deps=deps,
    )


def sum_members(refs, members):
    out = []
    for i in range(2):
        parts = []
        for at in range(0, len(refs), members):
            total = refs[at][i].astype(f32)
            for ref in refs[at + 1 : at + members]:
                total = total + ref[i].astype(f32)
            parts.append(total.astype(bf16))
        out.append(jnp.concatenate(parts, axis=1))
    return out


def memory_grad_kernel(members, count, k, sc, x, w, *refs):
    dk, dv = sum_members(refs[:count], members)
    own_out, send_out, keep, send, small, total, both = refs[count:]
    tok = own_out.shape[0]
    g = sc[0]
    store_rel(both, dot_tn(x[...], dk), sc, k, slice(0, 512))
    store_rel(both, dot_tn(x[...], dv), sc, k, slice(512, 1024))
    small[...] = jnp.zeros_like(small)
    small[0:1, :] = col_sum(dv)
    total[...] = dot_nt(dk, w[:, :512]) + dot_nt(dv, w[:, 512:])
    keep[...] = both[0]
    send[...] = both[1]
    own_out[...] = total[half_rows(g, 0, tok), :]
    send_out[...] = total[half_rows(g, 1, tok), :].astype(bf16)


def memory_grad(sc, plan, x, w, members, parts, deps=()):
    tokens = x.shape[0]
    tok = tokens // 2
    sds = jax.ShapeDtypeStruct
    vm = pl.BlockSpec(memory_space=pltpu.VMEM)
    return call(
        functools.partial(memory_grad_kernel, members, len(parts), plan.k),
        [sc, x, w, *parts],
        [smem()] + [vm] * (2 + len(parts)),
        [vm] * 5,
        [sds((tok, 512), f32), sds((tok, 512), bf16)] + [sds((256, 1024), bf16)] * 2 + [sds((8, 512), f32)],
        "memory_grad",
        cost(12 * tokens * 512 * 512, 6e6),
        scratch=[pltpu.VMEM((tokens, 512), f32), pltpu.VMEM((2, 256, 1024), bf16)],
        deps=deps,
    )


def target_grad_kernel(members, n_dq, count, n_small, k, sc, x, w, grad_one, *refs):
    dq = jnp.concatenate([ref[...] for ref in refs[:n_dq]], axis=1)
    refs = refs[n_dq:]
    dk, dv = sum_members(refs[:count], members)
    smalls = refs[count : count + n_small]
    own_out, send_out, keep, send, done, total, both = refs[count + n_small :]
    done[0, 0] = 0.0
    tok = own_out.shape[0]
    g = sc[0]
    for i, d in enumerate((dq, dk, dv)):
        store_rel(both, dot_tn(x[...], d), sc, k, slice(i * 512, (i + 1) * 512))
    rows = [ref[...] for ref in smalls] + [col_sum(dq), col_sum(dv)]
    used = sum(row.shape[0] for row in rows)
    rows.append(jnp.zeros((PAIR - used, 512), f32))
    store_rel(both, jnp.transpose(jnp.concatenate(rows, axis=0)), sc, k, slice(1536, 1536 + PAIR))
    total[...] = (
        grad_one[...]
        + dot_nt(dq, w[:, :512])
        + dot_nt(dk, w[:, 512:1024])
        + dot_nt(dv, w[:, 1024:])
    )
    keep[...] = both[0]
    send[...] = both[1]
    own_out[...] = total[half_rows(g, 0, tok), :]
    send_out[...] = total[half_rows(g, 1, tok), :].astype(bf16)


def target_grad(sc, plan, x, w, grad_one, dqs, members, parts, smalls, deps=()):
    tokens = x.shape[0]
    tok = tokens // 2
    sds = jax.ShapeDtypeStruct
    vm = pl.BlockSpec(memory_space=pltpu.VMEM)
    return call(
        functools.partial(target_grad_kernel, members, len(dqs), len(parts), len(smalls), plan.k),
        [sc, x, w, grad_one, *dqs, *parts, *smalls],
        [smem()] + [vm] * (3 + len(dqs) + len(parts) + len(smalls)),
        [vm] * 4 + [smem()],
        [sds((tok, 512), f32), sds((tok, 512), bf16)] + [sds((256, 1536 + PAIR), bf16)] * 2 + [sds((1, 1), f32)],
        "target_grad",
        cost(18 * tokens * 512 * 512, 8e6),
        scratch=[pltpu.VMEM((tokens, 512), f32), pltpu.VMEM((2, 256, 1536 + PAIR), bf16)],
        deps=deps,
    )


def per_device(
    target, memory, tgt_group, src_group, self_qkv, self_out, self_bias, cross_q, cross_kv, cross_out,
    cross_bias, ffn_in, ffn_in_bias, ffn_out, ffn_out_bias, norm_gain, norm_bias, cotangent,
):
    rows_here, tok, width = target.shape
    ff = ffn_in.shape[1]
    seq, rows = lax.axis_size("seq"), lax.axis_size("rows")
    members = seq // 2
    s, r = lax.axis_index("seq"), lax.axis_index("rows")
    g = s // members
    t = jnp.where(g == 0, s, seq - 1 - s)

    def digit(axis, bit):
        return ((s if axis == "seq" else r) // bit) % 2

    def bits_of(axis, size, low):
        return [(axis, 1 << i) for i in range(low, size.bit_length() - 1)]

    x_bits, y_bits, z_bits = bits_of("seq", seq, 1), bits_of("rows", rows, 0)[:1], bits_of("rows", rows, 1)
    cut, whole_z = list(zip(x_bits + y_bits, y_bits + x_bits)), list(zip(z_bits[::-1], z_bits))
    plan_w = Plan(cut, whole_z, width, digit)
    plan_ff = Plan(cut + whole_z, [], ff, digit) if CUT_FF else Plan(cut, whole_z, ff, digit)
    sc = jnp.stack([g, t, s % 2, *plan_ff.places, *plan_w.places]).astype(jnp.int32)

    def partner(x):
        return swap(x, "seq", seq - 1)

    def others_of(x):
        return [swap(x, "seq", j) for j in range(1, members)]

    def pick(x, which):
        return lax.dynamic_index_in_dim(x, g if which == 0 else 1 - g, 0, keepdims=False)

    def home(own, back):
        back = back.astype(f32)
        return jnp.where(g == 0, jnp.stack([own, back]), jnp.stack([back, own]))

    tgt_recv = partner(pick(target, 1))
    zero = tgt_recv[0, 0] * bf16(0.0)
    ids = jnp.stack([tgt_group, src_group])
    ids_own = lax.dynamic_index_in_dim(ids, g, 1, keepdims=False)
    ids_recv = partner(lax.dynamic_index_in_dim(ids, 1 - g, 1, keepdims=False))
    mem_recv = partner(pick(memory, 1) + zero)
    cot_recv = partner(pick(cotangent, 1) + mem_recv[0, 0] * bf16(0.0))
    ids_here = jnp.concatenate(
        [jnp.where(g == 0, ids_own, ids_recv), jnp.where(g == 0, ids_recv, ids_own)], axis=1
    ).astype(f32)
    ids_all = jnp.concatenate([ids_here] + others_of(ids_here), axis=1)

    scales, biases = (SCALE, 1.0, 1.0), (0, None, 1)
    done = embed_own("embed_own", sc, target, self_qkv, self_bias, scales, biases)
    x, q1, k1, v1 = embed("embed_target", sc, target, tgt_recv, done, self_qkv, self_bias, scales, biases)
    k1s, v1s = [k1] + others_of(k1), [v1] + others_of(v1)
    done = embed_own("embed_own_memory", sc, memory, cross_kv, cross_bias, scales[1:], biases[1:], [x])
    mixed1, lse1 = attend("self_attend", True, sc, ids_all, q1, k1s, v1s, [done])
    xm, k2, v2 = embed(
        "embed_memory", sc, memory, mem_recv, done, cross_kv, cross_bias, scales[1:], biases[1:], [mixed1]
    )
    k2s, v2s = [k2] + others_of(k2), [v2] + others_of(v2)

    n0, r0, q2 = after_self(x, mixed1, self_out, self_bias, norm_gain, norm_bias, cross_q, cross_bias)
    mixed2, lse2 = attend("cross_attend", False, sc, ids_all, q2, k2s, v2s)
    own_y, send_y, *d_out, small_ffn, slope, low, n1, r1, grad_three, outer = ffn_forward(
        sc, plan_ff, n0, mixed2, cross_out, cross_bias, norm_gain, norm_bias, ffn_in, ffn_in_bias[None],
        ffn_out, ffn_out_bias[None], cotangent, cot_recv,
    )
    layer_out = home(own_y, partner(send_y))
    first = Chain(plan_ff)
    first.add(*d_out)
    d_in, d_in_send, *d_cout, small_mid, grad_two, grad_mixed2, delta2 = ffn_back(
        sc, plan_ff, mixed2, cross_out, norm_gain, ffn_in, ffn_out, slope, low, n1, r1, grad_three, outer
    )
    first.add(d_in, d_in_send)
    first.add(*d_cout)

    def send_home(parts):
        tokens = 2 * tok
        found = []
        for _, own, far, _ in parts:
            found.append(own)
            for j in range(1, members):
                found.append(swap(far[:, (j - 1) * tokens : j * tokens], "seq", j))
        return found

    def cross_back(at, count, deps):
        return attend_back(
            "cross_back", False, sc, ids_all, q2, grad_mixed2, lse2, delta2, k2s, v2s, at, count, deps
        )

    n = CROSS_SPLIT[0]
    cb = [cross_back(0, n, [layer_out])]
    cb.append(cross_back(n, 4 - n, [cb[0][0], *first.parts]))
    *buf_b, small_cross, grad_one, grad_mixed1, delta1, done_cross = after_cross(
        sc, plan_w, [c[0] for c in cb], grad_two, n0, r0, cross_q, mixed1, self_out, norm_gain, norm_bias,
    )
    def self_back(at, count, deps):
        return attend_back(
            "self_back", True, sc, ids_all, q1, grad_mixed1, lse1, delta1, k1s, v1s, at, count, deps
        )

    second, third = Chain(plan_w), Chain(plan_w)
    n = SELF_SPLIT[0]
    one = first.step(after=done_cross[0, 0])
    sb = []
    if not MEMORY_FIRST:
        sb.append(self_back(0, n, [one]))
        one = first.step(after=sb[0][3][0, 0])
    own_m, send_m, *buf_a, small_mem = memory_grad(
        sc, plan_w, xm, cross_kv, members, send_home(cb), deps=[grad_one, one] + [part[0] for part in sb]
    )
    if MEMORY_FIRST:
        sb.append(self_back(0, n, [small_mem]))
        one = first.step(after=sb[0][3][0, 0])
    second.after = sb[0][3][0, 0]
    second.add(*buf_b)
    second.add(*buf_a)
    sb.append(self_back(n, 4 - n, [small_mem, one, *second.parts]))
    forced = [first.step(after=sb[1][3][0, 0]) for _ in range(FORCE_FIRST - 2)]
    forced += [second.step(after=sb[1][3][0, 0]) for _ in range(FORCE_SECOND)]
    if BACK_EARLY:
        back_m = partner(send_m)
        forced.append(back_m)
    own_t, send_t, *buf_c, done = target_grad(
        sc, plan_w, x, self_qkv, grad_one, [part[0] for part in sb], members, send_home(sb),
        [small_ffn, small_mid, small_cross, small_mem], deps=forced,
    )
    third.after = done[0, 0]
    third.add(*buf_c)
    third.join()
    sends = send_t if BACK_EARLY else jnp.concatenate([send_t, send_m], axis=0)
    nb = ff // 512
    last = third.zero()
    chains = {1: first, 2: second, 3: third}
    for what in ORDER:
        if what in chains:
            if chains[what].todo:
                chains[what].step(after=last)
                last = chains[what].zero()
        elif what == 9:
            back = partner((sends.astype(f32) + wide(last, width)).astype(bf16))
        elif what == 7:
            last = last + back[0, 0].astype(f32) * 0.0
        else:
            first.finish()
            share = 512 // nb
            d_ffn_out, d_ffn_in, d_cross_out, done = unpack(
                "unpack_ffn", sc, FF_PLACES, first,
                (((ff, 512), 0, 512, 0), ((512, ff), 512, 512, 1), ((512, 512), 1024, share, 1)),
            )
            last = last + done[0, 0]
    second.finish()
    third.finish()
    if not BACK_EARLY:
        back, back_m = back[:tok], back[tok:]
    d_target, d_memory = home(own_t, back), home(own_m, back_m)
    d_cross_q, d_self_out, d_cross_kv, _ = unpack(
        "unpack_cross", sc, W_PLACES, second,
        (((512, 512), 0, 512, 0), ((512, 512), 512, 512, 0), ((512, 1024), 1024, 1024, 0)),
    )
    at = 8 + small_mid.shape[0]
    crs, mem, tg = at, at + 8, at + 16
    d_self_qkv, d_self_bias, d_cross_bias, d_norm_gain, d_norm_bias, d_ffn_in_bias, d_ffn_out_bias, _ = unpack(
        "unpack_self", sc, W_PLACES, third, (((512, 1536), 0, 1536, 0),),
        rows=(
            (tg, tg + 1, crs + 3), (crs + 2, mem, 8 + 2), (crs, 8, 0), (crs + 1, 9, 1),
            tuple(16 + i for i in range(nb)), (2,),
        ),
    )
    d_ffn_in_bias, d_ffn_out_bias = d_ffn_in_bias.reshape(ff), d_ffn_out_bias.reshape(width)
    return (
        layer_out, d_target, d_memory, d_self_qkv, d_self_out, d_self_bias, d_cross_q, d_cross_kv,
        d_cross_out, d_cross_bias, d_ffn_in, d_ffn_in_bias, d_ffn_out, d_ffn_out_bias, d_norm_gain, d_norm_bias,
    )


def solution(mesh):
    sharded, ids, copied = P("rows", "seq", None), P("rows", "seq"), P()
    in_specs = (sharded, sharded, ids, ids) + (copied,) * 13 + (sharded,)
    out_specs = (sharded,) * 3 + (copied,) * 13
    return jax.shard_map(per_device, mesh=mesh, in_specs=in_specs, out_specs=out_specs, check_vma=False)
```

```python
import functools
import math

import jax
import jax.numpy as jnp
from jax import lax
from jax.experimental import pallas as pl
from jax.experimental.pallas import tpu as pltpu
from jax.sharding import PartitionSpec as P

HEADS = 8
PAIR = 128
EPS = 1e-05
SCALE = 0.125
NEG = -1e30
VMEM = 16 * 1024 * 1024
CROSS_SPLIT, SELF_SPLIT = (1, 3), (2, 2)
MEMORY_FIRST, CUT_FF, BACK_EARLY = True, True, True
FORCE_FIRST, FORCE_SECOND = 3, 1
ORDER = (1, 1, 1, 3, 2, 9, 3, 3, 1, 2, 3, 1, 3, 2, 2, 7, 3, 8, 2)
bf16 = jnp.bfloat16
f32 = jnp.float32


def params():
    return pltpu.CompilerParams(vmem_limit_bytes=VMEM)


def cost(flops, nbytes, trans=0):
    return pl.CostEstimate(flops=int(flops), bytes_accessed=int(nbytes), transcendentals=int(trans))


def dot(a, b):
    return jnp.dot(a, b, preferred_element_type=f32)


def dot_nt(a, b):
    return lax.dot_general(a, b, (((1,), (1,)), ((), ())), preferred_element_type=f32)


def dot_tn(a, b):
    return lax.dot_general(a, b, (((0,), (0,)), ((), ())), preferred_element_type=f32)


def col_sum(v):
    return jnp.sum(v.astype(f32), axis=0, keepdims=True)


def normalize(h):
    mean = jnp.mean(h, axis=-1, keepdims=True)
    c = h - mean
    r = lax.rsqrt(jnp.mean(c * c, axis=-1, keepdims=True) + EPS)
    return c * r, r


def norm_back(u, n, r, gain):
    w = u * gain
    return r * (
        w
        - jnp.mean(w, axis=-1, keepdims=True)
        - n * jnp.mean(w * n, axis=-1, keepdims=True)
    )


def whole(shape):
    return pl.BlockSpec(shape, lambda *_: (0,) * len(shape))


def smem():
    return pl.BlockSpec(memory_space=pltpu.SMEM)


def half_rows(g, which, count):
    at = g if which == 0 else 1 - g
    return pl.ds(pl.multiple_of(at * count, count), count)


class Plan:
    def __init__(self, cut, whole, n, digit, minimum=16):
        first = (("seq", 1), ("seq", 1))
        self.scatter, self.everywhere = [], list(whole)
        k = n
        places = [0, 0]
        for step in [first] + list(cut):
            if k % 2 == 0 and k // 2 >= minimum:
                self.scatter.append(step)
                k //= 2
                places = [place * 2 + digit(*bit) for place, bit in zip(places, step)]
            else:
                self.everywhere.append(step)
        self.n, self.k, self.chunks = n, k, n // k
        self.half = self.chunks // 2
        self.places = [place % self.half for place in places]


def swap(x, axis, off):
    size = lax.axis_size(axis)
    return lax.ppermute(x, axis, [(i, i ^ off) for i in range(size)])


def exchange(x, step):
    if step[0] == step[1]:
        return swap(x, *step[0])
    rows, seq = lax.axis_size("rows"), lax.axis_size("seq")
    pairs = []
    for r in range(rows):
        for s in range(seq):
            axis, off = step[s % 2]
            to = ((r ^ off) * seq + s) if axis == "rows" else (r * seq + (s ^ off))
            pairs.append((r * seq + s, to))
    return lax.ppermute(x, ("rows", "seq"), pairs)


CORE, FF_PLACES, W_PLACES = 2, 3, 5


def store_rel(both, value, sc, k, cols):
    half = value.shape[0] // k // 2
    for core in range(2):
        side = jnp.bitwise_xor(sc[CORE], core)
        for w in range(half):
            at = jnp.bitwise_xor(sc[W_PLACES + core], w)
            row = (core * half + w) * k
            both[side, pl.ds(pl.multiple_of(at * k, k), k), cols] = value[row : row + k].astype(both.dtype)


def store_half(keep, send, value, q, half_blocks, sc, k):
    core, at = q // half_blocks, q % half_blocks
    place = sc[FF_PLACES + core]
    value = value.astype(keep.dtype)
    for mine, ref in ((True, keep), (False, send)):

        @pl.when((sc[CORE] == core) == mine)
        def _():
            for w in range(512 // k):
                to = jnp.bitwise_xor(place, at * (512 // k) + w) * k
                ref[pl.ds(pl.multiple_of(to, k), k), :] = value[w * k : (w + 1) * k]


def store_narrow(both, value, half_blocks, sc, k):
    share, per = value.shape[1] // (2 * half_blocks), 512 // k
    for q in range(2 * half_blocks):
        core = q // half_blocks
        side = jnp.bitwise_xor(sc[CORE], core)
        place = sc[FF_PLACES + core]
        for w in range(per):
            at = jnp.bitwise_xor(place, (q % half_blocks) * per + w) * k
            both[side, pl.ds(pl.multiple_of(at, k), k), :] = value[
                w * k : (w + 1) * k, q * share : (q + 1) * share
            ].astype(both.dtype)


def wide(zero, width):
    if jnp.ndim(zero) < 2:
        return zero
    return jnp.pad(zero, ((0, 0), (0, width - zero.shape[1])))


class Chain:
    def __init__(self, plan):
        self.plan, self.parts, self.other, self.after = plan, [], None, 0.0
        self.todo = [("rs", d) for d in plan.scatter[1:]] + [("all", d) for d in plan.everywhere]
        self.todo += [("ag", d) for d in reversed(plan.scatter[1:])] + [("last", plan.scatter[0])]

    def sum(self, mine, got):
        return (mine.astype(f32) + got.astype(f32) + wide(self.after, mine.shape[1])).astype(bf16)

    def add(self, keep, send):
        got = exchange(send, self.plan.scatter[0])
        self.parts.append(self.sum(keep, got))
        return self.parts[-1]

    def join(self):
        if self.parts:
            self.buf = jnp.concatenate(self.parts, axis=1)
            self.parts = []

    def step(self, after=0.0):
        self.after = after
        self.join()
        kind, step = self.todo.pop(0)
        buf = self.buf
        if kind == "rs":
            half = buf.shape[0] // 2
            self.buf = self.sum(buf[:half], exchange(buf[half:], step))
        elif kind == "all":
            self.buf = self.sum(buf, exchange(buf, step))
        elif kind == "ag":
            got = exchange(buf, step).astype(f32) + wide(after, buf.shape[1])
            self.buf = jnp.concatenate([buf, got.astype(bf16)], axis=0)
        else:
            self.other = exchange(buf, step)
        return self.buf

    def finish(self):
        while self.todo:
            self.step()

    def zero(self):
        return self.buf[0:1, :PAIR].astype(f32) * 0.0


def call(kernel, operands, in_specs, out_specs, out_shape, name, work, scratch=(), grid=None, scalars=(), deps=(), vmem=VMEM, aliases={}):
    n_front, n_deps = len(scalars) + len(operands), len(deps)

    def body(*refs):
        kernel(*refs[:n_front], *refs[n_front + n_deps :])

    specs = list(in_specs) + [pl.BlockSpec(memory_space=pl.ANY)] * n_deps
    common = dict(
        out_shape=out_shape,
        compiler_params=pltpu.CompilerParams(vmem_limit_bytes=vmem),
        cost_estimate=work,
        input_output_aliases=aliases,
        name=name,
    )
    if scalars:
        spec = pltpu.PrefetchScalarGridSpec(
            num_scalar_prefetch=len(scalars), grid=grid, in_specs=specs, out_specs=out_specs, scratch_shapes=list(scratch)
        )
        return pl.pallas_call(body, grid_spec=spec, **common)(*scalars, *operands, *deps)
    if grid is not None:
        common["grid"] = grid
    return pl.pallas_call(
        body, in_specs=specs, out_specs=out_specs, scratch_shapes=list(scratch), **common
    )(*operands, *deps)


def unpack(name, sc, places, buffers, rows=(), deps=()):
    halves_of = [x for chain, _ in buffers for x in (chain.buf, chain.other)]
    n_out = sum(len(outs) for _, outs in buffers)
    k = buffers[0][0].plan.k
    n_copies = 0
    for chain, outs in buffers:
        blocks = max(chain.buf.shape[0] // 512, 1)
        n_copies += sum(2 * (1 if out[3] == 0 else blocks) for out in outs)

    def kernel(sc, *refs):
        sources, refs = refs[: len(halves_of)], refs[len(halves_of) :]
        goal, narrow, done = refs[:n_out], refs[n_out : n_out + len(rows)], refs[n_out + len(rows)]
        stages, sems = refs[n_out + len(rows) + 1 : -1], refs[-1]
        done[0, 0] = 0.0
        copies = []
        first_out = 0
        for i, (chain, outs) in enumerate(buffers):
            stage = stages[i]
            half = chain.buf.shape[0]
            blocks = max(half // 512, 1)
            size = half // blocks
            for side in range(2):
                src = sources[2 * i + side]
                core = jnp.bitwise_xor(sc[CORE], side)
                place = sc[places + core]
                for w in range(half // k):
                    at = pl.multiple_of(jnp.bitwise_xor(place, w) * k, k)
                    stage[side, pl.ds(at, k), :] = src[w * k : (w + 1) * k, :].astype(f32)
                for j, (shape, first, width, by) in enumerate(outs):
                    cols = slice(first, first + width)
                    out = goal[first_out + j]
                    for b in range(1 if by == 0 else blocks):
                        if by == 0:
                            part = stage.at[side, :, cols]
                            to = out.at[pl.ds(pl.multiple_of(core * half, half), half), :]
                        else:
                            at = pl.multiple_of((core * blocks + b) * width, width)
                            part, to = stage.at[side, b * size : (b + 1) * size, cols], out.at[:, pl.ds(at, width)]
                        copies.append(pltpu.make_async_copy(part, to, sems.at[len(copies)]))
                        copies[-1].start()
            first_out += len(outs)
        if rows:
            last = buffers[-1][0].buf.shape[1] - PAIR
            mine, far = stages[-1][0, :, last:], stages[-1][1, :, last:]
            straight = sc[CORE] == 0
            turned = jnp.transpose(
                jnp.concatenate([jnp.where(straight, mine, far), jnp.where(straight, far, mine)], axis=0)
            )
            for ref, picks in zip(narrow, rows):
                for i, pick in enumerate(picks):
                    ref[i : i + 1, :] = turned[pick : pick + 1, :]
        for copy in copies:
            copy.wait()

    vm = pl.BlockSpec(memory_space=pltpu.VMEM)
    shapes = [jax.ShapeDtypeStruct(out[0], f32) for _, outs in buffers for out in outs]
    shapes += [jax.ShapeDtypeStruct((len(picks), 512), f32) for picks in rows]
    scratch = [pltpu.VMEM((2,) + chain.buf.shape, f32) for chain, _ in buffers]
    return call(
        kernel, [sc, *halves_of], [smem()] + [vm] * len(halves_of), [hbm()] * n_out + [vm] * len(rows) + [smem()],
        shapes + [jax.ShapeDtypeStruct((1, 1), f32)], name, cost(0, 6 * sum(x.size for x in halves_of)),
        scratch=scratch + [pltpu.SemaphoreType.DMA((n_copies,))], deps=deps, vmem=24 << 20,
    )


def hbm():
    return pl.BlockSpec(memory_space=pltpu.HBM)


def project_kernel(scales, biases, sc, tgt, w, b, out, done, tgt_vm, w_vm, sems):
    done[0, 0] = 0.0
    copies = [
        pltpu.make_async_copy(tgt.at[sc[0]], tgt_vm, sems.at[0]),
        pltpu.make_async_copy(w, w_vm, sems.at[1]),
    ]
    for copy in copies:
        copy.start()
    for copy in copies:
        copy.wait()
    write_parts(dot(tgt_vm[...], w_vm[...]), scales, biases, b, out, slice(None))


def write_parts(y, scales, biases, b, outs, rows):
    for i, (scale, bias) in enumerate(zip(scales, biases)):
        cols = slice(i * 512, (i + 1) * 512)
        piece = y[:, cols] if bias is None else y[:, cols] + b[bias : bias + 1, :]
        piece = piece.astype(bf16)
        if scale != 1.0:
            piece = (piece.astype(f32) * scale).astype(bf16)
        if isinstance(outs, (tuple, list)):
            outs[i][rows, :] = piece
        else:
            outs[rows, cols] = piece


def embed_own(name, sc, local, w, b, scales, biases, deps=()):
    tok = local.shape[1]
    vm = pl.BlockSpec(memory_space=pltpu.VMEM)
    return call(
        functools.partial(project_kernel, scales, biases), [sc, local, w, b], [smem(), hbm(), hbm(), vm], [vm, smem()],
        [jax.ShapeDtypeStruct((tok, w.shape[1]), bf16), jax.ShapeDtypeStruct((1, 1), f32)], name, cost(2 * tok * 512 * w.shape[1], 3e6),
        scratch=[pltpu.VMEM((tok, 512), bf16), pltpu.VMEM(w.shape, bf16), pltpu.SemaphoreType.DMA((2,))], deps=deps,
    )


def embed_kernel(scales, biases, sc, tgt, recv, done, w, b, x_out, *refs):
    outs, (tgt_vm, w_vm, sems) = refs[:-3], refs[-3:]
    g = sc[0]
    tok = tgt.shape[1]
    copies = [
        pltpu.make_async_copy(tgt.at[g], tgt_vm, sems.at[0]),
        pltpu.make_async_copy(w, w_vm, sems.at[1]),
    ]
    for copy in copies:
        copy.start()
    own, far = half_rows(g, 0, tok), half_rows(g, 1, tok)
    x_out[far, :] = recv[...]
    for i, out in enumerate(outs):
        out[own, :] = done[:, i * 512 : (i + 1) * 512]
    for copy in copies:
        copy.wait()
    x_out[own, :] = tgt_vm[...]
    write_parts(dot(recv[...], w_vm[...]), scales, biases, b, outs, far)


def embed(name, sc, local, recv, done, w, b, scales, biases, deps=()):
    tok = local.shape[1]
    one = jax.ShapeDtypeStruct((2 * tok, 512), bf16)
    vm = pl.BlockSpec(memory_space=pltpu.VMEM)
    return call(
        functools.partial(embed_kernel, scales, biases), [sc, local, recv, done, w, b],
        [smem(), hbm(), vm, vm, hbm(), vm], [vm] * (1 + len(scales)), [one] * (1 + len(scales)), name,
        cost(2 * tok * 512 * w.shape[1], 4e6),
        scratch=[pltpu.VMEM((tok, 512), bf16), pltpu.VMEM(w.shape, bf16), pltpu.SemaphoreType.DMA((2,))], deps=deps,
    )


BIG = 2.0**100


def to_cols(row):
    return jnp.transpose(jnp.broadcast_to(row, (PAIR, row.shape[1])))


def halves(parts, tok, axis=0):
    cut = (lambda e, at: e[at : at + tok]) if axis == 0 else (lambda e, at: e[:, at : at + tok])
    return jnp.concatenate([cut(e, 0) for e in parts] + [cut(e, tok) for e in parts], axis=axis)


def key_mask(causal, t, ids, tok, axis):
    length = ids.shape[1]
    members = length // (2 * tok)
    group = ids[0:1, :] if causal else ids[1:2, :]
    group = halves([group[:, 2 * tok * j : 2 * tok * (j + 1)] for j in range(members)], tok, 1)
    shape = (PAIR, length) if axis == 0 else (length, PAIR)
    if axis == 1:
        group = to_cols(group)
    feature = lax.broadcasted_iota(jnp.int32, shape, axis) % 64
    out = jnp.where((feature < 5) & (group + 1.0 != feature.astype(f32)), -BIG, 0.0)
    out = jnp.where((feature >= 5) & (feature < 8), 1.0, out)
    if causal:
        at = lax.broadcasted_iota(jnp.int32, shape, 1 - axis)
        low = jnp.bitwise_xor((at % (members * tok)) // tok, t)
        second = at >= members * tok
        out = jnp.where((feature == 8) & (second | (low > t)), -BIG, out)
        out = jnp.where((feature == 9) & second & (low < t), -BIG, out)
    return out.astype(bf16)


def query_mask(ids, tok, axis):
    group = ids[0:1, : 2 * tok]
    shape = (PAIR, 2 * tok) if axis == 0 else (2 * tok, PAIR)
    if axis == 1:
        group = to_cols(group)
    feature = lax.broadcasted_iota(jnp.int32, shape, axis) % 64
    second = (lax.broadcasted_iota(jnp.int32, shape, 1 - axis) >= tok).astype(jnp.int32)
    hot = (feature < 5) & (group + 1.0 == feature.astype(f32))
    return jnp.where(hot | (feature == 8 + second), 1.0, 0.0).astype(bf16)


def mixed_in(h, axis, mine, other):
    return jnp.where(lax.broadcasted_iota(jnp.int32, mine.shape, axis) // 64 == h, mine, other)


def with_own(s, at, later, axis):
    end, size = at + later.shape[0], s.shape[axis]
    cut = (lambda i, j: s[i:j]) if axis == 0 else (lambda i, j: s[:, i:j])
    pieces = [cut(0, at)] if at else []
    pieces.append(cut(at, end) + later)
    if end < size:
        pieces.append(cut(end, size))
    return jnp.concatenate(pieces, axis=axis) if len(pieces) > 1 else pieces[0]


def blocks_of(causal, tok, length):
    if not causal:
        return [(slice(0, 2 * tok), length, None)]
    return [(slice(0, tok), length // 2, 0), (slice(tok, 2 * tok), length, length // 2)]


def each_pair(count, length, body):
    step = 2 if count % 2 == 0 and length <= 1024 else 1

    def some(i, carry):
        for p in range(step):
            body(i * step + p)
        return carry

    if count == step:
        some(0, 0)
    else:
        lax.fori_loop(0, count // step, some, 0)


def pair_lanes(p):
    return pl.ds(p * PAIR if isinstance(p, int) else pl.multiple_of(p * PAIR, PAIR), PAIR)


def attend_kernel(causal, tok, members, sc, ids, q, *refs):
    out, lse = refs[2 * members :]
    length = 2 * tok * members
    keys_side = key_mask(causal, sc[1], ids[...], tok, 1)
    queries_side = query_mask(ids[...], tok, 0)
    key_at = lax.broadcasted_iota(jnp.int32, (tok, tok), 0)
    later = jnp.where(key_at > lax.broadcasted_iota(jnp.int32, (tok, tok), 1), NEG, 0.0)
    ones = jnp.ones((64, length), bf16)

    def one_pair(p):
        lanes = pair_lanes(p)
        k = halves([ref[:, lanes] for ref in refs[:members]], tok)
        v = jnp.transpose(halves([ref[:, lanes] for ref in refs[members : 2 * members]], tok))
        qt = jnp.transpose(q[:, lanes])
        parts = []
        for h in range(2):
            kh = mixed_in(h, 1, k, keys_side)
            qh = mixed_in(h, 0, qt, queries_side)
            vh = jnp.concatenate([v[h * 64 : (h + 1) * 64], ones], axis=0)
            row = []
            for cols, seen, own in blocks_of(causal, tok, length):
                s = dot(kh[:seen], qh[:, cols])
                if own is not None:
                    s = with_own(s, own, later, 0)
                top = jnp.max(s, axis=0, keepdims=True)
                got = dot(vh[:, :seen], jnp.exp(s - top).astype(bf16))
                total = got[64:65]
                row.append(got[:64] * (1.0 / total))
                lse[p, h : h + 1, cols] = top + jnp.log(total)
            parts.append(jnp.concatenate(row, axis=1))
        out[:, lanes] = jnp.transpose(jnp.concatenate(parts, axis=0)).astype(bf16)

    each_pair(4, length, one_pair)


def attend_vmem(length):
    return min(VMEM * max(length // 1024, 1), 60 * 1024 * 1024)


def attend(name, causal, sc, ids, q, ks, vs, deps=()):
    tokens = q.shape[0]
    length = ids.shape[1]
    members = len(ks)
    vm = pl.BlockSpec(memory_space=pltpu.VMEM)
    return call(
        functools.partial(attend_kernel, causal, tokens // 2, members),
        [sc, ids, q, *ks, *vs],
        [smem()] + [vm] * (2 + 2 * members),
        [vm] * 2,
        [jax.ShapeDtypeStruct((tokens, 512), bf16), jax.ShapeDtypeStruct((4, 2, tokens), f32)],
        name,
        cost(42 * tokens * length * 512, 4e6, 8 * tokens * length),
        deps=deps,
        vmem=attend_vmem(length),
    )


def three(x):
    a = x.astype(bf16)
    rest = x - a.astype(f32)
    b = rest.astype(bf16)
    return a, b, (rest - b.astype(f32)).astype(bf16)


def with_terms(side, terms):
    feature = lax.broadcasted_iota(jnp.int32, side.shape, 1) % 64
    for i, term in enumerate(terms):
        side = jnp.where(feature == 5 + i, term, side)
    return side


def attend_back_kernel(causal, tok, members, pair, count, sc, ids, q, grad, lse, delta, *refs):
    dq, own_out, far, done = refs[2 * members :]
    done[0, 0] = 0.0
    length = 2 * tok * members
    keys_side = key_mask(causal, sc[1], ids[...], tok, 0)
    queries_side = query_mask(ids[...], tok, 1)
    zero = jnp.zeros((), bf16)
    feature = lax.broadcasted_iota(jnp.int32, (PAIR, length), 0) % 64
    ones = jnp.where((feature >= 5) & (feature < 8), 1.0, 0.0).astype(bf16)
    key_at = lax.broadcasted_iota(jnp.int32, (tok, tok), 1)
    later = jnp.where(key_at > lax.broadcasted_iota(jnp.int32, (tok, tok), 0), NEG, 0.0)
    half = length // 2

    def plus(total, term):
        return term if total is None else total + term

    def one_pair(p):
        from_lanes, lanes = pair_lanes(p + pair), pair_lanes(p)
        k = halves([ref[:, from_lanes] for ref in refs[:members]], tok)
        v = halves([ref[:, from_lanes] for ref in refs[members : 2 * members]], tok)
        q_here, g_here = q[:, from_lanes], grad[:, from_lanes]
        kt, vt = jnp.transpose(k), jnp.transpose(v)
        qt, gt = jnp.transpose(q_here), jnp.transpose(g_here)
        grad_k, grad_v, grad_q = [None, None], [None, None], {}
        for h in range(2):
            minus_lse = to_cols(-lse[p + pair, h : h + 1, :])
            minus_delta = to_cols(-delta[p + pair, h : h + 1, :])
            qh = mixed_in(h, 1, q_here, with_terms(queries_side, three(minus_lse)))
            gh = mixed_in(h, 1, g_here, with_terms(jnp.zeros((2 * tok, PAIR), bf16), three(minus_delta)))
            kh, vh = mixed_in(h, 0, kt, keys_side), mixed_in(h, 0, vt, ones)
            k_only, q_only, g_only = mixed_in(h, 1, k, zero), mixed_in(h, 0, qt, zero), mixed_in(h, 0, gt, zero)
            for b in range(2):
                rows = slice(b * tok, (b + 1) * tok)
                seen = half if causal and b == 0 else length
                s = dot(qh[rows], kh[:, :seen])
                if causal:
                    s = with_own(s, b * half, later, 1)
                w = jnp.exp(s)
                ds = (w * dot(gh[rows], vh[:, :seen])).astype(bf16)
                got_v, got_k = dot(g_only[:, rows], w.astype(bf16)), dot(q_only[:, rows], ds)
                for i in range(seen // half):
                    cols = slice(i * half, (i + 1) * half)
                    grad_v[i], grad_k[i] = plus(grad_v[i], got_v[:, cols]), plus(grad_k[i], got_k[:, cols])
                grad_q[b] = plus(grad_q.get(b), dot(ds, k_only[:seen]))
        for b in range(2):
            dq[b * tok : (b + 1) * tok, lanes] = (grad_q[b] * SCALE).astype(bf16)
        for i, total in enumerate((grad_k, grad_v)):
            for b in range(2):
                value = jnp.transpose(total[b]).astype(bf16)
                for j in range(members):
                    ref = far if j else own_out
                    at = (2 * j - 2 if j else 0) * tok + b * tok
                    ref[i, at : at + tok, lanes] = value[j * tok : (j + 1) * tok]

    each_pair(count, length, one_pair)


def attend_back(name, causal, sc, ids, q, grad, lse, delta, ks, vs, first, count, deps=()):
    tokens = q.shape[0]
    length = ids.shape[1]
    members = len(ks)
    width = count * PAIR
    sds = jax.ShapeDtypeStruct
    vm = pl.BlockSpec(memory_space=pltpu.VMEM)
    return call(
        functools.partial(attend_back_kernel, causal, tokens // 2, members, first, count),
        [sc, ids, q, grad, lse, delta, *ks, *vs],
        [smem()] + [vm] * (5 + 2 * members),
        [vm] * 3 + [smem()],
        [
            sds((tokens, width), bf16),
            sds((2, tokens, width), bf16),
            sds((2, length - tokens, width), bf16),
            sds((1, 1), f32),
        ],
        name,
        cost(17 * count * tokens * length * 512, 2e6 * count, 2 * count * tokens * length),
        deps=deps,
        vmem=attend_vmem(length),
    )


def after_self_kernel(x, mixed, w_out, sbias, gain, shift, w_q, cbias, n0, r0, q2):
    h = x[...].astype(f32) + dot(mixed[...], w_out[...]) + sbias[2:3, :]
    n, r = normalize(h)
    n0[...] = n
    r0[...] = r
    first = n * gain[0:1, :] + shift[0:1, :]
    q = dot(first.astype(bf16), w_q[...]) + cbias[0:1, :]
    q2[...] = (q.astype(bf16).astype(f32) * SCALE).astype(bf16)


def after_self(x, mixed, w_out, sbias, gain, shift, w_q, cbias):
    tokens = x.shape[0]
    vm = pl.BlockSpec(memory_space=pltpu.VMEM)
    return pl.pallas_call(
        after_self_kernel,
        in_specs=[vm] * 8,
        out_specs=[vm] * 3,
        out_shape=[
            jax.ShapeDtypeStruct((tokens, 512), f32),
            jax.ShapeDtypeStruct((tokens, 1), f32),
            jax.ShapeDtypeStruct((tokens, 512), bf16),
        ],
        compiler_params=params(),
        cost_estimate=cost(4 * tokens * 512 * 512, 4e6),
        name="after_self",
    )(x, mixed, w_out, sbias, gain, shift, w_q, cbias)


def head_sums(a, b):
    prod = a * b
    high = prod.astype(bf16)
    low = (prod - high.astype(f32)).astype(bf16)
    pick = (
        lax.broadcasted_iota(jnp.int32, (HEADS, 512), 1) // 64
        == lax.broadcasted_iota(jnp.int32, (HEADS, 512), 0)
    ).astype(bf16)
    return dot_nt(pick, high) + dot_nt(pick, low)


def put_head_rows(ref, rows):
    for p in range(4):
        ref[p] = rows[2 * p : 2 * p + 2]


def gelu_parts(v):
    c = math.sqrt(2.0 / math.pi)
    v2 = v * v
    t = jnp.tanh(c * v * (1.0 + 0.044715 * v2))
    half = 0.5 * (1.0 + t)
    slope = half + 0.5 * v * (1.0 - t * t) * (c * (1.0 + 3.0 * 0.044715 * v2))
    return v * half, slope


def ffn_forward_kernel(
    chunks, k_out, sc, n0, mixed, cout, cbias, gain, shift, w_in, b_in, w_out, b_out, cot, cot_recv,
    own_out, send_out, d_keep, d_send, small, slope, low, n1, r1, grad_three, outer, total,
):
    g = sc[0]
    tok = cot_recv.shape[0]
    first = n0[...] * gain[0:1, :] + shift[0:1, :]
    n, r = normalize(first + dot(mixed[...], cout[...]) + cbias[2:3, :])
    n1[...] = n
    r1[...] = r
    second = n * gain[1:2, :] + shift[1:2, :]
    second_low = second.astype(bf16)
    low[...] = second_low
    result = second + b_out[...]
    inner = []
    for j in range(chunks):
        cols = slice(j * 512, (j + 1) * 512)
        act, grad_act = gelu_parts(dot(second_low, w_in[:, cols]) + b_in[:, cols])
        inner.append(act.astype(bf16))
        slope[:, cols] = grad_act.astype(bf16)
        result = result + dot(inner[-1], w_out[cols, :])
    n, r = normalize(result)
    total[...] = n * gain[2:3, :] + shift[2:3, :]
    own_out[...] = total[half_rows(g, 0, tok), :]
    send_out[...] = total[half_rows(g, 1, tok), :].astype(bf16)
    total[half_rows(g, 0, tok), :] = cot[g].astype(f32)
    total[half_rows(g, 1, tok), :] = cot_recv[...].astype(f32)
    u = total[...]
    back = norm_back(u, n, r, gain[2:3, :])
    back_low = back.astype(bf16)
    grad_three[...] = back
    outer[...] = back_low
    small[...] = jnp.zeros_like(small)
    small[0:1, :] = col_sum(u * n)
    small[1:2, :] = col_sum(u)
    small[2:3, :] = col_sum(back_low)
    for j in range(chunks):
        store_half(d_keep, d_send, dot_tn(inner[j], back_low), j, chunks // 2, sc, k_out)


def ffn_forward(sc, plan, n0, mixed, cout, cbias, gain, shift, w_in, b_in, w_out, b_out, cot, cot_recv, deps=()):
    tokens = n0.shape[0]
    tok = tokens // 2
    ff = w_in.shape[1]
    chunks = ff // 512
    sds = jax.ShapeDtypeStruct
    vm = pl.BlockSpec(memory_space=pltpu.VMEM)
    return call(
        functools.partial(ffn_forward_kernel, chunks, plan.k),
        [sc, n0, mixed, cout, cbias, gain, shift, w_in, b_in, w_out, b_out, cot, cot_recv],
        [smem()] + [vm] * 12,
        [vm] * 11,
        [
            sds((tok, 512), f32),
            sds((tok, 512), bf16),
            sds((ff // 2, 512), bf16),
            sds((ff // 2, 512), bf16),
            sds((8, 512), f32),
            sds((tokens, ff), bf16),
            sds((tokens, 512), bf16),
            sds((tokens, 512), f32),
            sds((tokens, 1), f32),
            sds((tokens, 512), f32),
            sds((tokens, 512), bf16),
        ],
        "ffn_forward",
        cost(4 * tokens * 512 * (3 * ff + 512), 1.5e7),
        scratch=[pltpu.VMEM((tokens, 512), f32)],
        deps=deps,
    )


def ffn_back_kernel(
    chunks, k_in, sc, mixed, cout, gain, w_in, w_out, slope, low, n1, r1, grad_three, outer,
    d_keep, d_send, c_keep, c_send, small, grad_two, grad_mixed, delta, both,
):
    small[...] = jnp.zeros_like(small)
    u = grad_three[...]
    back_outer, second_low = outer[...], low[...]
    for j in range(chunks):
        cols = slice(j * 512, (j + 1) * 512)
        pre_low = (dot_nt(back_outer, w_out[cols, :]) * slope[:, cols].astype(f32)).astype(bf16)
        small[8 + j : 9 + j, :] = col_sum(pre_low)
        u = u + dot_nt(pre_low, w_in[:, cols])
        store_half(d_keep, d_send, dot_tn(second_low, pre_low), j, chunks // 2, sc, k_in)
    n = n1[...]
    small[0:1, :] = col_sum(u * n)
    small[1:2, :] = col_sum(u)
    back = norm_back(u, n, r1[...], gain[1:2, :])
    grad_two[...] = back
    back_low = back.astype(bf16)
    small[2:3, :] = col_sum(back_low)
    g_mixed = dot_nt(back_low, cout[...]).astype(bf16)
    grad_mixed[...] = g_mixed
    put_head_rows(delta, head_sums(g_mixed.astype(f32), mixed[...].astype(f32)))
    store_narrow(both, dot_tn(mixed[...], back_low), chunks // 2, sc, k_in)
    c_keep[...] = both[0]
    c_send[...] = both[1]


def ffn_back(sc, plan, mixed, cout, gain, w_in, w_out, slope, low, n1, r1, grad_three, outer, deps=()):
    tokens = mixed.shape[0]
    ff = w_in.shape[1]
    chunks = ff // 512
    share = 512 // chunks
    sds = jax.ShapeDtypeStruct
    vm = pl.BlockSpec(memory_space=pltpu.VMEM)
    return call(
        functools.partial(ffn_back_kernel, chunks, plan.k),
        [sc, mixed, cout, gain, w_in, w_out, slope, low, n1, r1, grad_three, outer],
        [smem()] + [vm] * 11,
        [vm] * 8,
        [
            sds((ff // 2, 512), bf16),
            sds((ff // 2, 512), bf16),
            sds((ff // 2, share), bf16),
            sds((ff // 2, share), bf16),
            sds((8 + chunks + 4, 512), f32),
            sds((tokens, 512), f32),
            sds((tokens, 512), bf16),
            sds((4, 2, tokens), f32),
        ],
        "ffn_back",
        cost(4 * tokens * 512 * (3 * ff + 1024), 1.5e7),
        scratch=[pltpu.VMEM((2, ff // 2, share), bf16)],
        deps=deps,
    )


def after_cross_kernel(
    n_parts, k, sc, grad_two, n0, r0, w_q, mixed, w_out, gain, shift, *refs
):
    dq = jnp.concatenate([ref[...] for ref in refs[:n_parts]], axis=1)
    keep, send, small, grad_one, grad_mixed, delta, done, both = refs[n_parts:]
    done[0, 0] = 0.0
    n = n0[...]
    first = (n * gain[0:1, :] + shift[0:1, :]).astype(bf16)
    store_rel(both, dot_tn(first, dq), sc, k, slice(0, 512))
    u = grad_two[...] + dot_nt(dq, w_q[...])
    small[...] = jnp.zeros_like(small)
    small[0:1, :] = col_sum(u * n)
    small[1:2, :] = col_sum(u)
    small[2:3, :] = col_sum(dq)
    back = norm_back(u, n, r0[...], gain[0:1, :])
    grad_one[...] = back
    back_low = back.astype(bf16)
    small[3:4, :] = col_sum(back_low)
    store_rel(both, dot_tn(mixed[...], back_low), sc, k, slice(512, 1024))
    keep[...] = both[0]
    send[...] = both[1]
    g_mixed = dot_nt(back_low, w_out[...]).astype(bf16)
    grad_mixed[...] = g_mixed
    put_head_rows(delta, head_sums(g_mixed.astype(f32), mixed[...].astype(f32)))


def after_cross(sc, plan, dqs, grad_two, n0, r0, w_q, mixed, w_out, gain, shift, deps=()):
    tokens = n0.shape[0]
    sds = jax.ShapeDtypeStruct
    vm = pl.BlockSpec(memory_space=pltpu.VMEM)
    return call(
        functools.partial(after_cross_kernel, len(dqs), plan.k),
        [sc, grad_two, n0, r0, w_q, mixed, w_out, gain, shift, *dqs],
        [smem()] + [vm] * (8 + len(dqs)),
        [vm] * 6 + [smem()],
        [
            sds((256, 1024), bf16),
            sds((256, 1024), bf16),
            sds((8, 512), f32),
            sds((tokens, 512), f32),
            sds((tokens, 512), bf16),
            sds((4, 2, tokens), f32),
            sds((1, 1), f32),
        ],
        "after_cross",
        cost(12 * tokens * 512 * 512, 6e6),
        scratch=[pltpu.VMEM((2, 256, 1024), bf16)],
        deps=deps,
    )


def sum_members(refs, members):
    out = []
    for i in range(2):
        parts = []
        for at in range(0, len(refs), members):
            total = refs[at][i].astype(f32)
            for ref in refs[at + 1 : at + members]:
                total = total + ref[i].astype(f32)
            parts.append(total.astype(bf16))
        out.append(jnp.concatenate(parts, axis=1))
    return out


def memory_grad_kernel(members, count, k, sc, x, w, *refs):
    dk, dv = sum_members(refs[:count], members)
    own_out, send_out, keep, send, small, total, both = refs[count:]
    tok = own_out.shape[0]
    g = sc[0]
    store_rel(both, dot_tn(x[...], dk), sc, k, slice(0, 512))
    store_rel(both, dot_tn(x[...], dv), sc, k, slice(512, 1024))
    small[...] = jnp.zeros_like(small)
    small[0:1, :] = col_sum(dv)
    total[...] = dot_nt(dk, w[:, :512]) + dot_nt(dv, w[:, 512:])
    keep[...] = both[0]
    send[...] = both[1]
    own_out[...] = total[half_rows(g, 0, tok), :]
    send_out[...] = total[half_rows(g, 1, tok), :].astype(bf16)


def memory_grad(sc, plan, x, w, members, parts, deps=()):
    tokens = x.shape[0]
    tok = tokens // 2
    sds = jax.ShapeDtypeStruct
    vm = pl.BlockSpec(memory_space=pltpu.VMEM)
    return call(
        functools.partial(memory_grad_kernel, members, len(parts), plan.k),
        [sc, x, w, *parts],
        [smem()] + [vm] * (2 + len(parts)),
        [vm] * 5,
        [sds((tok, 512), f32), sds((tok, 512), bf16)] + [sds((256, 1024), bf16)] * 2 + [sds((8, 512), f32)],
        "memory_grad",
        cost(12 * tokens * 512 * 512, 6e6),
        scratch=[pltpu.VMEM((tokens, 512), f32), pltpu.VMEM((2, 256, 1024), bf16)],
        deps=deps,
    )


def target_grad_kernel(members, n_dq, count, n_small, k, sc, x, w, grad_one, *refs):
    dq = jnp.concatenate([ref[...] for ref in refs[:n_dq]], axis=1)
    refs = refs[n_dq:]
    dk, dv = sum_members(refs[:count], members)
    smalls = refs[count : count + n_small]
    own_out, send_out, keep, send, done, total, both = refs[count + n_small :]
    done[0, 0] = 0.0
    tok = own_out.shape[0]
    g = sc[0]
    for i, d in enumerate((dq, dk, dv)):
        store_rel(both, dot_tn(x[...], d), sc, k, slice(i * 512, (i + 1) * 512))
    rows = [ref[...] for ref in smalls] + [col_sum(dq), col_sum(dv)]
    used = sum(row.shape[0] for row in rows)
    rows.append(jnp.zeros((PAIR - used, 512), f32))
    store_rel(both, jnp.transpose(jnp.concatenate(rows, axis=0)), sc, k, slice(1536, 1536 + PAIR))
    total[...] = (
        grad_one[...]
        + dot_nt(dq, w[:, :512])
        + dot_nt(dk, w[:, 512:1024])
        + dot_nt(dv, w[:, 1024:])
    )
    keep[...] = both[0]
    send[...] = both[1]
    own_out[...] = total[half_rows(g, 0, tok), :]
    send_out[...] = total[half_rows(g, 1, tok), :].astype(bf16)


def target_grad(sc, plan, x, w, grad_one, dqs, members, parts, smalls, deps=()):
    tokens = x.shape[0]
    tok = tokens // 2
    sds = jax.ShapeDtypeStruct
    vm = pl.BlockSpec(memory_space=pltpu.VMEM)
    return call(
        functools.partial(target_grad_kernel, members, len(dqs), len(parts), len(smalls), plan.k),
        [sc, x, w, grad_one, *dqs, *parts, *smalls],
        [smem()] + [vm] * (3 + len(dqs) + len(parts) + len(smalls)),
        [vm] * 4 + [smem()],
        [sds((tok, 512), f32), sds((tok, 512), bf16)] + [sds((256, 1536 + PAIR), bf16)] * 2 + [sds((1, 1), f32)],
        "target_grad",
        cost(18 * tokens * 512 * 512, 8e6),
        scratch=[pltpu.VMEM((tokens, 512), f32), pltpu.VMEM((2, 256, 1536 + PAIR), bf16)],
        deps=deps,
    )


def per_device(
    target, memory, tgt_group, src_group, self_qkv, self_out, self_bias, cross_q, cross_kv, cross_out,
    cross_bias, ffn_in, ffn_in_bias, ffn_out, ffn_out_bias, norm_gain, norm_bias, cotangent,
):
    rows_here, tok, width = target.shape
    ff = ffn_in.shape[1]
    seq, rows = lax.axis_size("seq"), lax.axis_size("rows")
    members = seq // 2
    s, r = lax.axis_index("seq"), lax.axis_index("rows")
    g = s // members
    t = jnp.where(g == 0, s, seq - 1 - s)

    def digit(axis, bit):
        return ((s if axis == "seq" else r) // bit) % 2

    def bits_of(axis, size, low):
        return [(axis, 1 << i) for i in range(low, size.bit_length() - 1)]

    x_bits, y_bits, z_bits = bits_of("seq", seq, 1), bits_of("rows", rows, 0)[:1], bits_of("rows", rows, 1)
    cut, whole_z = list(zip(x_bits + y_bits, y_bits + x_bits)), list(zip(z_bits[::-1], z_bits))
    plan_w = Plan(cut, whole_z, width, digit)
    plan_ff = Plan(cut + whole_z, [], ff, digit) if CUT_FF else Plan(cut, whole_z, ff, digit)
    sc = jnp.stack([g, t, s % 2, *plan_ff.places, *plan_w.places]).astype(jnp.int32)

    def partner(x):
        return swap(x, "seq", seq - 1)

    def others_of(x):
        return [swap(x, "seq", j) for j in range(1, members)]

    def pick(x, which):
        return lax.dynamic_index_in_dim(x, g if which == 0 else 1 - g, 0, keepdims=False)

    def home(own, back):
        back = back.astype(f32)
        return jnp.where(g == 0, jnp.stack([own, back]), jnp.stack([back, own]))

    tgt_recv = partner(pick(target, 1))
    ids = jnp.stack([tgt_group, src_group])
    ids_own = lax.dynamic_index_in_dim(ids, g, 1, keepdims=False)
    ids_recv = partner(lax.dynamic_index_in_dim(ids, 1 - g, 1, keepdims=False))
    scales, biases = (SCALE, 1.0, 1.0), (0, None, 1)
    own_qkv, done = embed_own("embed_own", sc, target, self_qkv, self_bias, scales, biases)
    mem_recv = partner(pick(memory, 1) + done[0, 0].astype(bf16))
    cot_recv = partner(pick(cotangent, 1) + mem_recv[0, 0] * bf16(0.0))
    ids_here = jnp.concatenate(
        [jnp.where(g == 0, ids_own, ids_recv), jnp.where(g == 0, ids_recv, ids_own)], axis=1
    ).astype(f32)
    ids_all = jnp.concatenate([ids_here] + others_of(ids_here), axis=1)

    x, q1, k1, v1 = embed(
        "embed_target", sc, target, tgt_recv, own_qkv, self_qkv, self_bias, scales, biases, [ids_here]
    )
    k1s, v1s = [k1] + others_of(k1), [v1] + others_of(v1)
    own_kv, done = embed_own("embed_own_memory", sc, memory, cross_kv, cross_bias, scales[1:], biases[1:], [x])
    mixed1, lse1 = attend("self_attend", True, sc, ids_all, q1, k1s, v1s, [done])
    xm, k2, v2 = embed(
        "embed_memory", sc, memory, mem_recv, own_kv, cross_kv, cross_bias, scales[1:], biases[1:], [mixed1]
    )
    k2s, v2s = [k2] + others_of(k2), [v2] + others_of(v2)

    n0, r0, q2 = after_self(x, mixed1, self_out, self_bias, norm_gain, norm_bias, cross_q, cross_bias)
    mixed2, lse2 = attend("cross_attend", False, sc, ids_all, q2, k2s, v2s)
    own_y, send_y, *d_out, small_ffn, slope, low, n1, r1, grad_three, outer = ffn_forward(
        sc, plan_ff, n0, mixed2, cross_out, cross_bias, norm_gain, norm_bias, ffn_in, ffn_in_bias[None],
        ffn_out, ffn_out_bias[None], cotangent, cot_recv,
    )
    layer_out = home(own_y, partner(send_y))
    first = Chain(plan_ff)
    first.add(*d_out)
    d_in, d_in_send, *d_cout, small_mid, grad_two, grad_mixed2, delta2 = ffn_back(
        sc, plan_ff, mixed2, cross_out, norm_gain, ffn_in, ffn_out, slope, low, n1, r1, grad_three, outer
    )
    first.add(d_in, d_in_send)
    first.add(*d_cout)

    def send_home(parts):
        tokens = 2 * tok
        found = []
        for _, own, far, _ in parts:
            found.append(own)
            for j in range(1, members):
                found.append(swap(far[:, (j - 1) * tokens : j * tokens], "seq", j))
        return found

    def cross_back(at, count, deps):
        return attend_back(
            "cross_back", False, sc, ids_all, q2, grad_mixed2, lse2, delta2, k2s, v2s, at, count, deps
        )

    n = CROSS_SPLIT[0]
    cb = [cross_back(0, n, [layer_out])]
    cb.append(cross_back(n, 4 - n, [cb[0][0], *first.parts]))
    *buf_b, small_cross, grad_one, grad_mixed1, delta1, done_cross = after_cross(
        sc, plan_w, [c[0] for c in cb], grad_two, n0, r0, cross_q, mixed1, self_out, norm_gain, norm_bias,
    )
    def self_back(at, count, deps):
        return attend_back(
            "self_back", True, sc, ids_all, q1, grad_mixed1, lse1, delta1, k1s, v1s, at, count, deps
        )

    second, third = Chain(plan_w), Chain(plan_w)
    n = SELF_SPLIT[0]
    one = first.step(after=done_cross[0, 0])
    sb = []
    if not MEMORY_FIRST:
        sb.append(self_back(0, n, [one]))
        one = first.step(after=sb[0][3][0, 0])
    own_m, send_m, *buf_a, small_mem = memory_grad(
        sc, plan_w, xm, cross_kv, members, send_home(cb), deps=[grad_one, one] + [part[0] for part in sb]
    )
    if MEMORY_FIRST:
        sb.append(self_back(0, n, [small_mem]))
        one = first.step(after=sb[0][3][0, 0])
    second.after = sb[0][3][0, 0]
    second.add(*buf_b)
    second.add(*buf_a)
    sb.append(self_back(n, 4 - n, [small_mem, one, *second.parts]))
    forced = [first.step(after=sb[1][3][0, 0]) for _ in range(FORCE_FIRST - 2)]
    forced += [second.step(after=sb[1][3][0, 0]) for _ in range(FORCE_SECOND)]
    if BACK_EARLY:
        back_m = partner(send_m)
        forced.append(back_m)
    own_t, send_t, *buf_c, done = target_grad(
        sc, plan_w, x, self_qkv, grad_one, [part[0] for part in sb], members, send_home(sb),
        [small_ffn, small_mid, small_cross, small_mem], deps=forced,
    )
    third.after = done[0, 0]
    third.add(*buf_c)
    third.join()
    sends = send_t if BACK_EARLY else jnp.concatenate([send_t, send_m], axis=0)
    nb = ff // 512
    last = third.zero()
    chains = {1: first, 2: second, 3: third}
    outs_ffn = (((ff, 512), 0, 512, 0), ((512, ff), 512, 512, 1), ((512, 512), 1024, 512 // nb, 1))
    for what in ORDER:
        if what in chains:
            if chains[what].todo:
                chains[what].step(after=last)
                last = chains[what].zero()
        elif what == 9:
            back = partner((sends.astype(f32) + wide(last, width)).astype(bf16))
        elif what == 7:
            last = last + back[0, 0].astype(f32) * 0.0
        else:
            first.finish()
            d_ffn_out, d_ffn_in, d_cross_out, done = unpack("unpack_ffn", sc, FF_PLACES, [(first, outs_ffn)])
            last = last + done[0, 0]
    second.finish()
    third.finish()
    at = 8 + small_mid.shape[0]
    crs, mem, tg = at, at + 8, at + 16
    outs = (((512, 512), 0, 512, 0), ((512, 512), 512, 512, 0), ((512, 1024), 1024, 1024, 0))
    (
        d_cross_q, d_self_out, d_cross_kv, d_self_qkv,
        d_self_bias, d_cross_bias, d_norm_gain, d_norm_bias, d_ffn_in_bias, d_ffn_out_bias, _,
    ) = unpack(
        "unpack_rest", sc, W_PLACES, [(second, outs), (third, (((512, 1536), 0, 1536, 0),))],
        (
            (tg, tg + 1, crs + 3), (crs + 2, mem, 8 + 2), (crs, 8, 0), (crs + 1, 9, 1),
            tuple(16 + i for i in range(nb)), (2,),
        ),
    )
    d_ffn_in_bias, d_ffn_out_bias = d_ffn_in_bias.reshape(ff), d_ffn_out_bias.reshape(width)
    if not BACK_EARLY:
        back, back_m = back[:tok], back[tok:]
    d_target, d_memory = home(own_t, back), home(own_m, back_m)
    return (
        layer_out, d_target, d_memory, d_self_qkv, d_self_out, d_self_bias, d_cross_q, d_cross_kv,
        d_cross_out, d_cross_bias, d_ffn_in, d_ffn_in_bias, d_ffn_out, d_ffn_out_bias, d_norm_gain, d_norm_bias,
    )


def solution(mesh):
    sharded, ids, copied = P("rows", "seq", None), P("rows", "seq"), P()
    in_specs = (sharded, sharded, ids, ids) + (copied,) * 13 + (sharded,)
    out_specs = (sharded,) * 3 + (copied,) * 13
    return jax.shard_map(per_device, mesh=mesh, in_specs=in_specs, out_specs=out_specs, check_vma=False)
```

```python
import functools
import math

import jax
import jax.numpy as jnp
from jax import lax
from jax.experimental import pallas as pl
from jax.experimental.pallas import tpu as pltpu
from jax.sharding import PartitionSpec as P

HEADS = 8
PAIR = 128
EPS = 1e-05
SCALE = 0.125
NEG = -1e30
VMEM = 16 * 1024 * 1024
CROSS_SPLIT, SELF_SPLIT = (1, 3), (2, 2)
MEMORY_FIRST, CUT_FF, BACK_EARLY = True, True, True
FORCE_FIRST, FORCE_SECOND = 3, 1
ORDER = (1, 1, 1, 3, 2, 9, 3, 3, 1, 2, 3, 1, 3, 2, 2, 7, 3, 8, 2)
bf16 = jnp.bfloat16
f32 = jnp.float32


def params():
    return pltpu.CompilerParams(vmem_limit_bytes=VMEM)


def cost(flops, nbytes, trans=0):
    return pl.CostEstimate(flops=int(flops), bytes_accessed=int(nbytes), transcendentals=int(trans))


def dot(a, b):
    return jnp.dot(a, b, preferred_element_type=f32)


def dot_nt(a, b):
    return lax.dot_general(a, b, (((1,), (1,)), ((), ())), preferred_element_type=f32)


def dot_tn(a, b):
    return lax.dot_general(a, b, (((0,), (0,)), ((), ())), preferred_element_type=f32)


def col_sum(v):
    return jnp.sum(v.astype(f32), axis=0, keepdims=True)


def normalize(h):
    mean = jnp.mean(h, axis=-1, keepdims=True)
    c = h - mean
    r = lax.rsqrt(jnp.mean(c * c, axis=-1, keepdims=True) + EPS)
    return c * r, r


def norm_back(u, n, r, gain):
    w = u * gain
    return r * (
        w
        - jnp.mean(w, axis=-1, keepdims=True)
        - n * jnp.mean(w * n, axis=-1, keepdims=True)
    )


def whole(shape):
    return pl.BlockSpec(shape, lambda *_: (0,) * len(shape))


def smem():
    return pl.BlockSpec(memory_space=pltpu.SMEM)


def half_rows(g, which, count):
    at = g if which == 0 else 1 - g
    return pl.ds(pl.multiple_of(at * count, count), count)


class Plan:
    def __init__(self, cut, whole, n, digit, minimum=16):
        first = (("seq", 1), ("seq", 1))
        self.scatter, self.everywhere = [], list(whole)
        k = n
        places = [0, 0]
        for step in [first] + list(cut):
            if k % 2 == 0 and k // 2 >= minimum:
                self.scatter.append(step)
                k //= 2
                places = [place * 2 + digit(*bit) for place, bit in zip(places, step)]
            else:
                self.everywhere.append(step)
        self.n, self.k, self.chunks = n, k, n // k
        self.half = self.chunks // 2
        self.places = [place % self.half for place in places]


def swap(x, axis, off):
    size = lax.axis_size(axis)
    return lax.ppermute(x, axis, [(i, i ^ off) for i in range(size)])


def exchange(x, step):
    if step[0] == step[1]:
        return swap(x, *step[0])
    rows, seq = lax.axis_size("rows"), lax.axis_size("seq")
    pairs = []
    for r in range(rows):
        for s in range(seq):
            axis, off = step[s % 2]
            to = ((r ^ off) * seq + s) if axis == "rows" else (r * seq + (s ^ off))
            pairs.append((r * seq + s, to))
    return lax.ppermute(x, ("rows", "seq"), pairs)


CORE, FF_PLACES, W_PLACES = 2, 3, 5


def store_rel(both, value, sc, k, cols):
    half = value.shape[0] // k // 2
    for core in range(2):
        side = jnp.bitwise_xor(sc[CORE], core)
        for w in range(half):
            at = jnp.bitwise_xor(sc[W_PLACES + core], w)
            row = (core * half + w) * k
            both[side, pl.ds(pl.multiple_of(at * k, k), k), cols] = value[row : row + k].astype(both.dtype)


def store_half(keep, send, value, q, half_blocks, sc, k):
    core, at = q // half_blocks, q % half_blocks
    place = sc[FF_PLACES + core]
    value = value.astype(keep.dtype)
    for mine, ref in ((True, keep), (False, send)):

        @pl.when((sc[CORE] == core) == mine)
        def _():
            for w in range(512 // k):
                to = jnp.bitwise_xor(place, at * (512 // k) + w) * k
                ref[pl.ds(pl.multiple_of(to, k), k), :] = value[w * k : (w + 1) * k]


def store_narrow(both, value, half_blocks, sc, k):
    share, per = value.shape[1] // (2 * half_blocks), 512 // k
    for q in range(2 * half_blocks):
        core = q // half_blocks
        side = jnp.bitwise_xor(sc[CORE], core)
        place = sc[FF_PLACES + core]
        for w in range(per):
            at = jnp.bitwise_xor(place, (q % half_blocks) * per + w) * k
            both[side, pl.ds(pl.multiple_of(at, k), k), :] = value[
                w * k : (w + 1) * k, q * share : (q + 1) * share
            ].astype(both.dtype)


def wide(zero, width):
    if jnp.ndim(zero) < 2:
        return zero
    return jnp.pad(zero, ((0, 0), (0, width - zero.shape[1])))


class Chain:
    def __init__(self, plan):
        self.plan, self.parts, self.other, self.after = plan, [], None, 0.0
        self.todo = [("rs", d) for d in plan.scatter[1:]] + [("all", d) for d in plan.everywhere]
        self.todo += [("ag", d) for d in reversed(plan.scatter[1:])] + [("last", plan.scatter[0])]

    def sum(self, mine, got):
        return (mine.astype(f32) + got.astype(f32) + wide(self.after, mine.shape[1])).astype(bf16)

    def add(self, keep, send):
        got = exchange(send, self.plan.scatter[0])
        self.parts.append(self.sum(keep, got))
        return self.parts[-1]

    def join(self):
        if self.parts:
            self.buf = jnp.concatenate(self.parts, axis=1)
            self.parts = []

    def step(self, after=0.0):
        self.after = after
        self.join()
        kind, step = self.todo.pop(0)
        buf = self.buf
        if kind == "rs":
            half = buf.shape[0] // 2
            self.buf = self.sum(buf[:half], exchange(buf[half:], step))
        elif kind == "all":
            self.buf = self.sum(buf, exchange(buf, step))
        elif kind == "ag":
            got = exchange(buf, step).astype(f32) + wide(after, buf.shape[1])
            self.buf = jnp.concatenate([buf, got.astype(bf16)], axis=0)
        else:
            self.other = exchange(buf, step)
        return self.buf

    def finish(self):
        while self.todo:
            self.step()

    def zero(self):
        return self.buf[0:1, :PAIR].astype(f32) * 0.0


def call(kernel, operands, in_specs, out_specs, out_shape, name, work, scratch=(), grid=None, scalars=(), deps=(), vmem=VMEM, aliases={}):
    n_front, n_deps = len(scalars) + len(operands), len(deps)

    def body(*refs):
        kernel(*refs[:n_front], *refs[n_front + n_deps :])

    specs = list(in_specs) + [pl.BlockSpec(memory_space=pl.ANY)] * n_deps
    common = dict(
        out_shape=out_shape,
        compiler_params=pltpu.CompilerParams(vmem_limit_bytes=vmem),
        cost_estimate=work,
        input_output_aliases=aliases,
        name=name,
    )
    if scalars:
        spec = pltpu.PrefetchScalarGridSpec(
            num_scalar_prefetch=len(scalars), grid=grid, in_specs=specs, out_specs=out_specs, scratch_shapes=list(scratch)
        )
        return pl.pallas_call(body, grid_spec=spec, **common)(*scalars, *operands, *deps)
    if grid is not None:
        common["grid"] = grid
    return pl.pallas_call(
        body, in_specs=specs, out_specs=out_specs, scratch_shapes=list(scratch), **common
    )(*operands, *deps)


def unpack(name, sc, places, buffers, rows=(), deps=()):
    halves_of = [x for chain, _ in buffers for x in (chain.buf, chain.other)]
    n_out = sum(len(outs) for _, outs in buffers)
    k = buffers[0][0].plan.k
    n_copies = 0
    for chain, outs in buffers:
        blocks = max(chain.buf.shape[0] // 512, 1)
        n_copies += sum(2 * (1 if out[3] == 0 else blocks) for out in outs)

    def kernel(sc, *refs):
        sources, refs = refs[: len(halves_of)], refs[len(halves_of) :]
        goal, narrow, done = refs[:n_out], refs[n_out : n_out + len(rows)], refs[n_out + len(rows)]
        stages, sems = refs[n_out + len(rows) + 1 : -1], refs[-1]
        done[0, 0] = 0.0
        copies = []
        first_out = 0
        for i, (chain, outs) in enumerate(buffers):
            stage = stages[i]
            half = chain.buf.shape[0]
            blocks = max(half // 512, 1)
            size = half // blocks
            for side in range(2):
                src = sources[2 * i + side]
                core = jnp.bitwise_xor(sc[CORE], side)
                place = sc[places + core]
                for w in range(half // k):
                    at = pl.multiple_of(jnp.bitwise_xor(place, w) * k, k)
                    stage[side, pl.ds(at, k), :] = src[w * k : (w + 1) * k, :].astype(f32)
                for j, (shape, first, width, by) in enumerate(outs):
                    cols = slice(first, first + width)
                    out = goal[first_out + j]
                    for b in range(1 if by == 0 else blocks):
                        if by == 0:
                            part = stage.at[side, :, cols]
                            to = out.at[pl.ds(pl.multiple_of(core * half, half), half), :]
                        else:
                            at = pl.multiple_of((core * blocks + b) * width, width)
                            part, to = stage.at[side, b * size : (b + 1) * size, cols], out.at[:, pl.ds(at, width)]
                        copies.append(pltpu.make_async_copy(part, to, sems.at[len(copies)]))
                        copies[-1].start()
            first_out += len(outs)
        if rows:
            last = buffers[-1][0].buf.shape[1] - PAIR
            mine, far = stages[-1][0, :, last:], stages[-1][1, :, last:]
            straight = sc[CORE] == 0
            turned = jnp.transpose(
                jnp.concatenate([jnp.where(straight, mine, far), jnp.where(straight, far, mine)], axis=0)
            )
            for ref, picks in zip(narrow, rows):
                for i, pick in enumerate(picks):
                    if len(ref.shape) == 1:
                        ref[i * 512 : (i + 1) * 512] = turned[pick]
                    else:
                        ref[i : i + 1, :] = turned[pick : pick + 1, :]
        for copy in copies:
            copy.wait()

    vm = pl.BlockSpec(memory_space=pltpu.VMEM)
    shapes = [jax.ShapeDtypeStruct(out[0], f32) for _, outs in buffers for out in outs]
    shapes += [jax.ShapeDtypeStruct((3, 512) if len(p) == 3 else (len(p) * 512,), f32) for p in rows]
    scratch = [pltpu.VMEM((2,) + chain.buf.shape, f32) for chain, _ in buffers]
    return call(
        kernel, [sc, *halves_of], [smem()] + [vm] * len(halves_of), [hbm()] * n_out + [vm] * len(rows) + [smem()],
        shapes + [jax.ShapeDtypeStruct((1, 1), f32)], name, cost(0, 6 * sum(x.size for x in halves_of)),
        scratch=scratch + [pltpu.SemaphoreType.DMA((n_copies,))], deps=deps, vmem=24 << 20,
    )


def hbm():
    return pl.BlockSpec(memory_space=pltpu.HBM)


def write_parts(y, scales, biases, b, outs, rows):
    for i, (scale, bias) in enumerate(zip(scales, biases)):
        cols = slice(i * 512, (i + 1) * 512)
        piece = y[:, cols] if bias is None else y[:, cols] + b[bias : bias + 1, :]
        piece = piece.astype(bf16)
        if scale != 1.0:
            piece = (piece.astype(f32) * scale).astype(bf16)
        if isinstance(outs, (tuple, list)):
            outs[i][rows, :] = piece
        else:
            outs[rows, cols] = piece


def embed_own_kernel(scales, biases, sc, tgt, w, b, out, x_out, w_out, b_out, done):
    done[0, 0] = 0.0
    x_out[...] = tgt[sc[0]]
    w_out[...] = w[...]
    b_out[...] = b[...]
    write_parts(dot(x_out[...], w[...]), scales, biases, b, out, slice(None))


def embed_own(name, sc, local, w, b, scales, biases, deps=()):
    tok = local.shape[1]
    sds = jax.ShapeDtypeStruct
    vm = pl.BlockSpec(memory_space=pltpu.VMEM)
    *found, done = call(
        functools.partial(embed_own_kernel, scales, biases), [sc, local, w, b], [smem()] + [vm] * 3, [vm] * 4 + [smem()],
        [sds((tok, w.shape[1]), bf16), sds((tok, 512), bf16), sds(w.shape, bf16), sds(b.shape, f32), sds((1, 1), f32)],
        name, cost(2 * tok * 512 * w.shape[1], 3e6), deps=deps,
    )
    return found, done


def embed_kernel(scales, biases, sc, recv, done, x, w, b, x_out, *outs):
    g = sc[0]
    tok = recv.shape[0]
    own, far = half_rows(g, 0, tok), half_rows(g, 1, tok)
    x_out[own, :] = x[...]
    x_out[far, :] = recv[...]
    for i, out in enumerate(outs):
        out[own, :] = done[:, i * 512 : (i + 1) * 512]
    write_parts(dot(recv[...], w[...]), scales, biases, b, outs, far)


def embed(name, sc, recv, own, scales, biases, deps=()):
    tok = recv.shape[0]
    one = jax.ShapeDtypeStruct((2 * tok, 512), bf16)
    vm = pl.BlockSpec(memory_space=pltpu.VMEM)
    return call(
        functools.partial(embed_kernel, scales, biases), [sc, recv, *own], [smem()] + [vm] * 5,
        [vm] * (1 + len(scales)), [one] * (1 + len(scales)), name, cost(2 * tok * 512 * 512 * len(scales), 4e6), deps=deps,
    )


def embed_both_kernel(scales, biases, sc, local, recv, w, b, x_out, *outs):
    g = sc[0]
    tok = recv.shape[0]
    x_out[half_rows(g, 0, tok), :] = local[g]
    x_out[half_rows(g, 1, tok), :] = recv[...]
    write_parts(dot(x_out[...], w[...]), scales, biases, b, outs, slice(None))


def embed_both(name, sc, local, recv, w, b, scales, biases, deps=()):
    tok = recv.shape[0]
    one = jax.ShapeDtypeStruct((2 * tok, 512), bf16)
    vm = pl.BlockSpec(memory_space=pltpu.VMEM)
    return call(
        functools.partial(embed_both_kernel, scales, biases), [sc, local, recv, w, b], [smem()] + [vm] * 4,
        [vm] * (1 + len(scales)), [one] * (1 + len(scales)), name, cost(4 * tok * 512 * 512 * len(scales), 4e6), deps=deps,
    )


BIG = 2.0**100


def to_cols(row):
    return jnp.transpose(jnp.broadcast_to(row, (PAIR, row.shape[1])))


def halves(parts, tok, axis=0):
    cut = (lambda e, at: e[at : at + tok]) if axis == 0 else (lambda e, at: e[:, at : at + tok])
    return jnp.concatenate([cut(e, 0) for e in parts] + [cut(e, tok) for e in parts], axis=axis)


def key_mask(causal, t, ids, tok, axis):
    length = ids.shape[1]
    members = length // (2 * tok)
    group = ids[0:1, :] if causal else ids[1:2, :]
    group = halves([group[:, 2 * tok * j : 2 * tok * (j + 1)] for j in range(members)], tok, 1)
    shape = (PAIR, length) if axis == 0 else (length, PAIR)
    if axis == 1:
        group = to_cols(group)
    feature = lax.broadcasted_iota(jnp.int32, shape, axis) % 64
    out = jnp.where((feature < 5) & (group + 1.0 != feature.astype(f32)), -BIG, 0.0)
    out = jnp.where((feature >= 5) & (feature < 8), 1.0, out)
    if causal:
        at = lax.broadcasted_iota(jnp.int32, shape, 1 - axis)
        low = jnp.bitwise_xor((at % (members * tok)) // tok, t)
        second = at >= members * tok
        out = jnp.where((feature == 8) & (second | (low > t)), -BIG, out)
        out = jnp.where((feature == 9) & second & (low > t), -BIG, out)
    return out.astype(bf16)


def query_mask(ids, tok, axis):
    group = ids[0:1, : 2 * tok]
    shape = (PAIR, 2 * tok) if axis == 0 else (2 * tok, PAIR)
    if axis == 1:
        group = to_cols(group)
    feature = lax.broadcasted_iota(jnp.int32, shape, axis) % 64
    second = (lax.broadcasted_iota(jnp.int32, shape, 1 - axis) >= tok).astype(jnp.int32)
    hot = (feature < 5) & (group + 1.0 == feature.astype(f32))
    return jnp.where(hot | (feature == 8 + second), 1.0, 0.0).astype(bf16)


def mixed_in(h, axis, mine, other):
    return jnp.where(lax.broadcasted_iota(jnp.int32, mine.shape, axis) // 64 == h, mine, other)


def with_own(s, at, later, axis):
    end, size = at + later.shape[0], s.shape[axis]
    cut = (lambda i, j: s[i:j]) if axis == 0 else (lambda i, j: s[:, i:j])
    pieces = [cut(0, at)] if at else []
    pieces.append(cut(at, end) + later)
    if end < size:
        pieces.append(cut(end, size))
    return jnp.concatenate(pieces, axis=axis) if len(pieces) > 1 else pieces[0]


def blocks_of(causal, tok, length):
    if not causal:
        return [(slice(0, 2 * tok), length, None)]
    return [(slice(0, tok), length // 2, 0), (slice(tok, 2 * tok), length, length // 2)]


def each_pair(count, length, body, unrolled=False):
    step = (4 if unrolled and count == 4 else 2) if count % 2 == 0 and length <= 1024 else 1

    def some(i, carry):
        for p in range(step):
            body(i * step + p)
        return carry

    if count == step:
        some(0, 0)
    else:
        lax.fori_loop(0, count // step, some, 0)


def pair_lanes(p):
    return pl.ds(p * PAIR if isinstance(p, int) else pl.multiple_of(p * PAIR, PAIR), PAIR)


def attend_kernel(causal, tok, members, sc, ids, q, *refs):
    out, lse = refs[2 * members :]
    length = 2 * tok * members
    keys_side = key_mask(causal, sc[1], ids[...], tok, 1)
    queries_side = query_mask(ids[...], tok, 0)
    key_at = lax.broadcasted_iota(jnp.int32, (tok, tok), 0)
    later = jnp.where(key_at > lax.broadcasted_iota(jnp.int32, (tok, tok), 1), NEG, 0.0)
    ones = jnp.ones((64, length), bf16)

    def one_pair(p):
        lanes = pair_lanes(p)
        k = halves([ref[:, lanes] for ref in refs[:members]], tok)
        v = jnp.transpose(halves([ref[:, lanes] for ref in refs[members : 2 * members]], tok))
        qt = jnp.transpose(q[:, lanes])
        parts = []
        for h in range(2):
            kh = mixed_in(h, 1, k, keys_side)
            qh = mixed_in(h, 0, qt, queries_side)
            vh = jnp.concatenate([v[h * 64 : (h + 1) * 64], ones], axis=0)
            row = []
            for cols, seen, own in blocks_of(causal, tok, length):
                s = dot(kh[:seen], qh[:, cols])
                if own is not None:
                    s = with_own(s, own, later, 0)
                top = jnp.max(s, axis=0, keepdims=True)
                got = dot(vh[:, :seen], jnp.exp(s - top).astype(bf16))
                total = got[64:65]
                row.append(got[:64] * (1.0 / total))
                lse[p, h : h + 1, cols] = top + jnp.log(total)
            parts.append(jnp.concatenate(row, axis=1))
        out[:, lanes] = jnp.transpose(jnp.concatenate(parts, axis=0)).astype(bf16)

    each_pair(4, length, one_pair, causal)


def attend_vmem(length):
    return min(VMEM * max(length // 1024, 1), 60 * 1024 * 1024)


def attend(name, causal, sc, ids, q, ks, vs, deps=()):
    tokens = q.shape[0]
    length = ids.shape[1]
    members = len(ks)
    vm = pl.BlockSpec(memory_space=pltpu.VMEM)
    return call(
        functools.partial(attend_kernel, causal, tokens // 2, members),
        [sc, ids, q, *ks, *vs],
        [smem()] + [vm] * (2 + 2 * members),
        [vm] * 2,
        [jax.ShapeDtypeStruct((tokens, 512), bf16), jax.ShapeDtypeStruct((4, 2, tokens), f32)],
        name,
        cost(42 * tokens * length * 512, 4e6, 8 * tokens * length),
        deps=deps,
        vmem=attend_vmem(length),
    )


def three(x):
    a = x.astype(bf16)
    rest = x - a.astype(f32)
    b = rest.astype(bf16)
    return a, b, (rest - b.astype(f32)).astype(bf16)


def with_terms(side, terms):
    feature = lax.broadcasted_iota(jnp.int32, side.shape, 1) % 64
    for i, term in enumerate(terms):
        side = jnp.where(feature == 5 + i, term, side)
    return side


def attend_back_kernel(causal, tok, members, pair, count, sc, ids, q, grad, lse, delta, *refs):
    dq, own_out, far, done = refs[2 * members :]
    done[0, 0] = 0.0
    length = 2 * tok * members
    keys_side = key_mask(causal, sc[1], ids[...], tok, 0)
    queries_side = query_mask(ids[...], tok, 1)
    zero = jnp.zeros((), bf16)
    feature = lax.broadcasted_iota(jnp.int32, (PAIR, length), 0) % 64
    ones = jnp.where((feature >= 5) & (feature < 8), 1.0, 0.0).astype(bf16)
    key_at = lax.broadcasted_iota(jnp.int32, (tok, tok), 1)
    later = jnp.where(key_at > lax.broadcasted_iota(jnp.int32, (tok, tok), 0), NEG, 0.0)
    half = length // 2

    def plus(total, term):
        return term if total is None else total + term

    def one_pair(p):
        from_lanes, lanes = pair_lanes(p + pair), pair_lanes(p)
        k = halves([ref[:, from_lanes] for ref in refs[:members]], tok)
        v = halves([ref[:, from_lanes] for ref in refs[members : 2 * members]], tok)
        q_here, g_here = q[:, from_lanes], grad[:, from_lanes]
        kt, vt = jnp.transpose(k), jnp.transpose(v)
        qt, gt = jnp.transpose(q_here), jnp.transpose(g_here)
        grad_k, grad_v, grad_q = [None, None], [None, None], {}
        for h in range(2):
            minus_lse = to_cols(-lse[p + pair, h : h + 1, :])
            minus_delta = to_cols(-delta[p + pair, h : h + 1, :])
            qh = mixed_in(h, 1, q_here, with_terms(queries_side, three(minus_lse)))
            gh = mixed_in(h, 1, g_here, with_terms(jnp.zeros((2 * tok, PAIR), bf16), three(minus_delta)))
            kh, vh = mixed_in(h, 0, kt, keys_side), mixed_in(h, 0, vt, ones)
            k_only, q_only, g_only = mixed_in(h, 1, k, zero), mixed_in(h, 0, qt, zero), mixed_in(h, 0, gt, zero)
            for b in range(2):
                rows = slice(b * tok, (b + 1) * tok)
                seen = half if causal and b == 0 else length
                s = dot(qh[rows], kh[:, :seen])
                if causal:
                    s = with_own(s, b * half, later, 1)
                w = jnp.exp(s)
                ds = (w * dot(gh[rows], vh[:, :seen])).astype(bf16)
                got_v, got_k = dot(g_only[:, rows], w.astype(bf16)), dot(q_only[:, rows], ds)
                for i in range(seen // half):
                    cols = slice(i * half, (i + 1) * half)
                    grad_v[i], grad_k[i] = plus(grad_v[i], got_v[:, cols]), plus(grad_k[i], got_k[:, cols])
                grad_q[b] = plus(grad_q.get(b), dot(ds, k_only[:seen]))
        for b in range(2):
            dq[b * tok : (b + 1) * tok, lanes] = (grad_q[b] * SCALE).astype(bf16)
        for i, total in enumerate((grad_k, grad_v)):
            for b in range(2):
                value = jnp.transpose(total[b]).astype(bf16)
                for j in range(members):
                    ref = far if j else own_out
                    at = (2 * j - 2 if j else 0) * tok + b * tok
                    ref[i, at : at + tok, lanes] = value[j * tok : (j + 1) * tok]

    each_pair(count, length, one_pair)


def attend_back(name, causal, sc, ids, q, grad, lse, delta, ks, vs, first, count, deps=()):
    tokens = q.shape[0]
    length = ids.shape[1]
    members = len(ks)
    width = count * PAIR
    sds = jax.ShapeDtypeStruct
    vm = pl.BlockSpec(memory_space=pltpu.VMEM)
    return call(
        functools.partial(attend_back_kernel, causal, tokens // 2, members, first, count),
        [sc, ids, q, grad, lse, delta, *ks, *vs],
        [smem()] + [vm] * (5 + 2 * members),
        [vm] * 3 + [smem()],
        [
            sds((tokens, width), bf16),
            sds((2, tokens, width), bf16),
            sds((2, length - tokens, width), bf16),
            sds((1, 1), f32),
        ],
        name,
        cost(17 * count * tokens * length * 512, 2e6 * count, 2 * count * tokens * length),
        deps=deps,
        vmem=attend_vmem(length),
    )


def after_self_kernel(x, mixed, w_out, sbias, gain, shift, w_q, cbias, n0, r0, q2):
    h = x[...].astype(f32) + dot(mixed[...], w_out[...]) + sbias[2:3, :]
    n, r = normalize(h)
    n0[...] = n
    r0[...] = r
    first = n * gain[0:1, :] + shift[0:1, :]
    q = dot(first.astype(bf16), w_q[...]) + cbias[0:1, :]
    q2[...] = (q.astype(bf16).astype(f32) * SCALE).astype(bf16)


def after_self(x, mixed, w_out, sbias, gain, shift, w_q, cbias):
    tokens = x.shape[0]
    vm = pl.BlockSpec(memory_space=pltpu.VMEM)
    return pl.pallas_call(
        after_self_kernel,
        in_specs=[vm] * 8,
        out_specs=[vm] * 3,
        out_shape=[
            jax.ShapeDtypeStruct((tokens, 512), f32),
            jax.ShapeDtypeStruct((tokens, 1), f32),
            jax.ShapeDtypeStruct((tokens, 512), bf16),
        ],
        compiler_params=params(),
        cost_estimate=cost(4 * tokens * 512 * 512, 4e6),
        name="after_self",
    )(x, mixed, w_out, sbias, gain, shift, w_q, cbias)


def head_sums(a, b):
    prod = a * b
    high = prod.astype(bf16)
    low = (prod - high.astype(f32)).astype(bf16)
    pick = (
        lax.broadcasted_iota(jnp.int32, (HEADS, 512), 1) // 64
        == lax.broadcasted_iota(jnp.int32, (HEADS, 512), 0)
    ).astype(bf16)
    return dot_nt(pick, high) + dot_nt(pick, low)


def put_head_rows(ref, rows):
    for p in range(4):
        ref[p] = rows[2 * p : 2 * p + 2]


def gelu_parts(v):
    c = math.sqrt(2.0 / math.pi)
    v2 = v * v
    t = jnp.tanh(c * v * (1.0 + 0.044715 * v2))
    half = 0.5 * (1.0 + t)
    slope = half + 0.5 * v * (1.0 - t * t) * (c * (1.0 + 3.0 * 0.044715 * v2))
    return v * half, slope


def ffn_forward_kernel(
    chunks, k_out, sc, n0, mixed, cout, cbias, gain, shift, w_in, b_in, w_out, b_out, cot, cot_recv,
    own_out, send_out, d_keep, d_send, small, slope, low, n1, r1, grad_three, outer, total,
):
    g = sc[0]
    tok = cot_recv.shape[0]
    first = n0[...] * gain[0:1, :] + shift[0:1, :]
    n, r = normalize(first + dot(mixed[...], cout[...]) + cbias[2:3, :])
    n1[...] = n
    r1[...] = r
    second = n * gain[1:2, :] + shift[1:2, :]
    second_low = second.astype(bf16)
    low[...] = second_low
    result = second + b_out[...]
    inner = []
    for j in range(chunks):
        cols = slice(j * 512, (j + 1) * 512)
        act, grad_act = gelu_parts(dot(second_low, w_in[:, cols]) + b_in[:, cols])
        inner.append(act.astype(bf16))
        slope[:, cols] = grad_act.astype(bf16)
        result = result + dot(inner[-1], w_out[cols, :])
    n, r = normalize(result)
    total[...] = n * gain[2:3, :] + shift[2:3, :]
    own_out[...] = total[half_rows(g, 0, tok), :]
    send_out[...] = total[half_rows(g, 1, tok), :].astype(bf16)
    total[half_rows(g, 0, tok), :] = cot[g].astype(f32)
    total[half_rows(g, 1, tok), :] = cot_recv[...].astype(f32)
    u = total[...]
    back = norm_back(u, n, r, gain[2:3, :])
    back_low = back.astype(bf16)
    grad_three[...] = back
    outer[...] = back_low
    small[...] = jnp.zeros_like(small)
    small[0:1, :] = col_sum(u * n)
    small[1:2, :] = col_sum(u)
    small[2:3, :] = col_sum(back_low)
    for j in range(chunks):
        store_half(d_keep, d_send, dot_tn(inner[j], back_low), j, chunks // 2, sc, k_out)


def ffn_forward(sc, plan, n0, mixed, cout, cbias, gain, shift, w_in, b_in, w_out, b_out, cot, cot_recv, deps=()):
    tokens = n0.shape[0]
    tok = tokens // 2
    ff = w_in.shape[1]
    chunks = ff // 512
    sds = jax.ShapeDtypeStruct
    vm = pl.BlockSpec(memory_space=pltpu.VMEM)
    return call(
        functools.partial(ffn_forward_kernel, chunks, plan.k),
        [sc, n0, mixed, cout, cbias, gain, shift, w_in, b_in, w_out, b_out, cot, cot_recv],
        [smem()] + [vm] * 12,
        [vm] * 11,
        [
            sds((tok, 512), f32),
            sds((tok, 512), bf16),
            sds((ff // 2, 512), bf16),
            sds((ff // 2, 512), bf16),
            sds((8, 512), f32),
            sds((tokens, ff), bf16),
            sds((tokens, 512), bf16),
            sds((tokens, 512), f32),
            sds((tokens, 1), f32),
            sds((tokens, 512), f32),
            sds((tokens, 512), bf16),
        ],
        "ffn_forward",
        cost(4 * tokens * 512 * (3 * ff + 512), 1.5e7),
        scratch=[pltpu.VMEM((tokens, 512), f32)],
        deps=deps,
    )


def ffn_back_kernel(
    chunks, k_in, sc, mixed, cout, gain, w_in, w_out, slope, low, n1, r1, grad_three, outer,
    d_keep, d_send, c_keep, c_send, small, grad_two, grad_mixed, delta, both,
):
    small[...] = jnp.zeros_like(small)
    u = grad_three[...]
    back_outer, second_low = outer[...], low[...]
    for j in range(chunks):
        cols = slice(j * 512, (j + 1) * 512)
        pre_low = (dot_nt(back_outer, w_out[cols, :]) * slope[:, cols].astype(f32)).astype(bf16)
        small[8 + j : 9 + j, :] = col_sum(pre_low)
        u = u + dot_nt(pre_low, w_in[:, cols])
        store_half(d_keep, d_send, dot_tn(second_low, pre_low), j, chunks // 2, sc, k_in)
    n = n1[...]
    small[0:1, :] = col_sum(u * n)
    small[1:2, :] = col_sum(u)
    back = norm_back(u, n, r1[...], gain[1:2, :])
    grad_two[...] = back
    back_low = back.astype(bf16)
    small[2:3, :] = col_sum(back_low)
    g_mixed = dot_nt(back_low, cout[...]).astype(bf16)
    grad_mixed[...] = g_mixed
    put_head_rows(delta, head_sums(g_mixed.astype(f32), mixed[...].astype(f32)))
    store_narrow(both, dot_tn(mixed[...], back_low), chunks // 2, sc, k_in)
    c_keep[...] = both[0]
    c_send[...] = both[1]


def ffn_back(sc, plan, mixed, cout, gain, w_in, w_out, slope, low, n1, r1, grad_three, outer, deps=()):
    tokens = mixed.shape[0]
    ff = w_in.shape[1]
    chunks = ff // 512
    share = 512 // chunks
    sds = jax.ShapeDtypeStruct
    vm = pl.BlockSpec(memory_space=pltpu.VMEM)
    return call(
        functools.partial(ffn_back_kernel, chunks, plan.k),
        [sc, mixed, cout, gain, w_in, w_out, slope, low, n1, r1, grad_three, outer],
        [smem()] + [vm] * 11,
        [vm] * 8,
        [
            sds((ff // 2, 512), bf16),
            sds((ff // 2, 512), bf16),
            sds((ff // 2, share), bf16),
            sds((ff // 2, share), bf16),
            sds((8 + chunks + 4, 512), f32),
            sds((tokens, 512), f32),
            sds((tokens, 512), bf16),
            sds((4, 2, tokens), f32),
        ],
        "ffn_back",
        cost(4 * tokens * 512 * (3 * ff + 1024), 1.5e7),
        scratch=[pltpu.VMEM((2, ff // 2, share), bf16)],
        deps=deps,
    )


def after_cross_kernel(
    n_parts, k, sc, grad_two, n0, r0, w_q, mixed, w_out, gain, shift, *refs
):
    dq = jnp.concatenate([ref[...] for ref in refs[:n_parts]], axis=1)
    keep, send, small, grad_one, grad_mixed, delta, done, both = refs[n_parts:]
    done[0, 0] = 0.0
    n = n0[...]
    first = (n * gain[0:1, :] + shift[0:1, :]).astype(bf16)
    store_rel(both, dot_tn(first, dq), sc, k, slice(0, 512))
    u = grad_two[...] + dot_nt(dq, w_q[...])
    small[...] = jnp.zeros_like(small)
    small[0:1, :] = col_sum(u * n)
    small[1:2, :] = col_sum(u)
    small[2:3, :] = col_sum(dq)
    back = norm_back(u, n, r0[...], gain[0:1, :])
    grad_one[...] = back
    back_low = back.astype(bf16)
    small[3:4, :] = col_sum(back_low)
    store_rel(both, dot_tn(mixed[...], back_low), sc, k, slice(512, 1024))
    keep[...] = both[0]
    send[...] = both[1]
    g_mixed = dot_nt(back_low, w_out[...]).astype(bf16)
    grad_mixed[...] = g_mixed
    put_head_rows(delta, head_sums(g_mixed.astype(f32), mixed[...].astype(f32)))


def after_cross(sc, plan, dqs, grad_two, n0, r0, w_q, mixed, w_out, gain, shift, deps=()):
    tokens = n0.shape[0]
    sds = jax.ShapeDtypeStruct
    vm = pl.BlockSpec(memory_space=pltpu.VMEM)
    return call(
        functools.partial(after_cross_kernel, len(dqs), plan.k),
        [sc, grad_two, n0, r0, w_q, mixed, w_out, gain, shift, *dqs],
        [smem()] + [vm] * (8 + len(dqs)),
        [vm] * 6 + [smem()],
        [
            sds((256, 1024), bf16),
            sds((256, 1024), bf16),
            sds((8, 512), f32),
            sds((tokens, 512), f32),
            sds((tokens, 512), bf16),
            sds((4, 2, tokens), f32),
            sds((1, 1), f32),
        ],
        "after_cross",
        cost(12 * tokens * 512 * 512, 6e6),
        scratch=[pltpu.VMEM((2, 256, 1024), bf16)],
        deps=deps,
    )


def sum_members(refs, members):
    out = []
    for i in range(2):
        parts = []
        for at in range(0, len(refs), members):
            total = refs[at][i].astype(f32)
            for ref in refs[at + 1 : at + members]:
                total = total + ref[i].astype(f32)
            parts.append(total.astype(bf16))
        out.append(jnp.concatenate(parts, axis=1))
    return out


def memory_grad_kernel(members, count, k, sc, x, w, *refs):
    dk, dv = sum_members(refs[:count], members)
    own_out, send_out, keep, send, small, total, both = refs[count:]
    tok = own_out.shape[0]
    g = sc[0]
    store_rel(both, dot_tn(x[...], dk), sc, k, slice(0, 512))
    store_rel(both, dot_tn(x[...], dv), sc, k, slice(512, 1024))
    small[...] = jnp.zeros_like(small)
    small[0:1, :] = col_sum(dv)
    total[...] = dot_nt(dk, w[:, :512]) + dot_nt(dv, w[:, 512:])
    keep[...] = both[0]
    send[...] = both[1]
    own_out[...] = total[half_rows(g, 0, tok), :]
    send_out[...] = total[half_rows(g, 1, tok), :].astype(bf16)


def memory_grad(sc, plan, x, w, members, parts, deps=()):
    tokens = x.shape[0]
    tok = tokens // 2
    sds = jax.ShapeDtypeStruct
    vm = pl.BlockSpec(memory_space=pltpu.VMEM)
    return call(
        functools.partial(memory_grad_kernel, members, len(parts), plan.k),
        [sc, x, w, *parts],
        [smem()] + [vm] * (2 + len(parts)),
        [vm] * 5,
        [sds((tok, 512), f32), sds((tok, 512), bf16)] + [sds((256, 1024), bf16)] * 2 + [sds((8, 512), f32)],
        "memory_grad",
        cost(12 * tokens * 512 * 512, 6e6),
        scratch=[pltpu.VMEM((tokens, 512), f32), pltpu.VMEM((2, 256, 1024), bf16)],
        deps=deps,
    )


def target_grad_kernel(members, n_dq, count, n_small, k, sc, x, w, grad_one, *refs):
    dq = jnp.concatenate([ref[...] for ref in refs[:n_dq]], axis=1)
    refs = refs[n_dq:]
    dk, dv = sum_members(refs[:count], members)
    smalls = refs[count : count + n_small]
    own_out, send_out, keep, send, done, total, both = refs[count + n_small :]
    done[0, 0] = 0.0
    tok = own_out.shape[0]
    g = sc[0]
    for i, d in enumerate((dq, dk, dv)):
        store_rel(both, dot_tn(x[...], d), sc, k, slice(i * 512, (i + 1) * 512))
    rows = [ref[...] for ref in smalls] + [col_sum(dq), col_sum(dv)]
    used = sum(row.shape[0] for row in rows)
    rows.append(jnp.zeros((PAIR - used, 512), f32))
    store_rel(both, jnp.transpose(jnp.concatenate(rows, axis=0)), sc, k, slice(1536, 1536 + PAIR))
    total[...] = (
        grad_one[...]
        + dot_nt(dq, w[:, :512])
        + dot_nt(dk, w[:, 512:1024])
        + dot_nt(dv, w[:, 1024:])
    )
    keep[...] = both[0]
    send[...] = both[1]
    own_out[...] = total[half_rows(g, 0, tok), :]
    send_out[...] = total[half_rows(g, 1, tok), :].astype(bf16)


def target_grad(sc, plan, x, w, grad_one, dqs, members, parts, smalls, deps=()):
    tokens = x.shape[0]
    tok = tokens // 2
    sds = jax.ShapeDtypeStruct
    vm = pl.BlockSpec(memory_space=pltpu.VMEM)
    return call(
        functools.partial(target_grad_kernel, members, len(dqs), len(parts), len(smalls), plan.k),
        [sc, x, w, grad_one, *dqs, *parts, *smalls],
        [smem()] + [vm] * (3 + len(dqs) + len(parts) + len(smalls)),
        [vm] * 4 + [smem()],
        [sds((tok, 512), f32), sds((tok, 512), bf16)] + [sds((256, 1536 + PAIR), bf16)] * 2 + [sds((1, 1), f32)],
        "target_grad",
        cost(18 * tokens * 512 * 512, 8e6),
        scratch=[pltpu.VMEM((tokens, 512), f32), pltpu.VMEM((2, 256, 1536 + PAIR), bf16)],
        deps=deps,
    )


def per_device(
    target, memory, tgt_group, src_group, self_qkv, self_out, self_bias, cross_q, cross_kv, cross_out,
    cross_bias, ffn_in, ffn_in_bias, ffn_out, ffn_out_bias, norm_gain, norm_bias, cotangent,
):
    rows_here, tok, width = target.shape
    ff = ffn_in.shape[1]
    seq, rows = lax.axis_size("seq"), lax.axis_size("rows")
    members = seq // 2
    s, r = lax.axis_index("seq"), lax.axis_index("rows")
    g = s // members
    t = s % members

    def digit(axis, bit):
        return ((s if axis == "seq" else r) // bit) % 2

    def bits_of(axis, size, low):
        return [(axis, 1 << i) for i in range(low, size.bit_length() - 1)]

    x_bits, y_bits, z_bits = bits_of("seq", seq, 1), bits_of("rows", rows, 0)[:1], bits_of("rows", rows, 1)
    cut, whole_z = list(zip(x_bits + y_bits, y_bits + x_bits)), list(zip(z_bits[::-1], z_bits))
    plan_w = Plan(cut, whole_z, width, digit)
    plan_ff = Plan(cut + whole_z, [], ff, digit) if CUT_FF else Plan(cut, whole_z, ff, digit)
    sc = jnp.stack([g, t, s % 2, *plan_ff.places, *plan_w.places]).astype(jnp.int32)

    def partner(x):
        return swap(x, "seq", members)

    def others_of(x):
        return [swap(x, "seq", j) for j in range(1, members)]

    def pick(x, which):
        return lax.dynamic_index_in_dim(x, g if which == 0 else 1 - g, 0, keepdims=False)

    def home(own, back):
        back = back.astype(f32)
        return jnp.where(g == 0, jnp.stack([own, back]), jnp.stack([back, own]))

    tgt_recv = partner(pick(target, 1))
    ids = jnp.stack([tgt_group, src_group])
    ids_own = lax.dynamic_index_in_dim(ids, g, 1, keepdims=False)
    scales, biases = (SCALE, 1.0, 1.0), (0, None, 1)
    own_qkv, done = embed_own("embed_own", sc, target, self_qkv, self_bias, scales, biases)
    ids_recv = partner(lax.dynamic_index_in_dim(ids, 1 - g, 1, keepdims=False) + done[0, 0].astype(jnp.int32))
    mem_recv = partner(pick(memory, 1) + done[0, 0].astype(bf16))
    cot_recv = partner(pick(cotangent, 1) + mem_recv[0, 0] * bf16(0.0))
    ids_here = jnp.concatenate(
        [jnp.where(g == 0, ids_own, ids_recv), jnp.where(g == 0, ids_recv, ids_own)], axis=1
    ).astype(f32)
    ids_all = jnp.concatenate([ids_here] + others_of(ids_here), axis=1)

    x, q1, k1, v1 = embed("embed_target", sc, tgt_recv, own_qkv, scales, biases)
    k1s, v1s = [k1] + others_of(k1), [v1] + others_of(v1)
    mixed1, lse1 = attend("self_attend", True, sc, ids_all, q1, k1s, v1s)
    xm, k2, v2 = embed_both(
        "embed_memory", sc, memory, mem_recv, cross_kv, cross_bias, scales[1:], biases[1:], [mixed1]
    )
    k2s, v2s = [k2] + others_of(k2), [v2] + others_of(v2)

    n0, r0, q2 = after_self(x, mixed1, self_out, self_bias, norm_gain, norm_bias, cross_q, cross_bias)
    mixed2, lse2 = attend("cross_attend", False, sc, ids_all, q2, k2s, v2s)
    own_y, send_y, *d_out, small_ffn, slope, low, n1, r1, grad_three, outer = ffn_forward(
        sc, plan_ff, n0, mixed2, cross_out, cross_bias, norm_gain, norm_bias, ffn_in, ffn_in_bias[None],
        ffn_out, ffn_out_bias[None], cotangent, cot_recv,
    )
    layer_out = home(own_y, partner(send_y))
    first = Chain(plan_ff)
    first.add(*d_out)
    d_in, d_in_send, *d_cout, small_mid, grad_two, grad_mixed2, delta2 = ffn_back(
        sc, plan_ff, mixed2, cross_out, norm_gain, ffn_in, ffn_out, slope, low, n1, r1, grad_three, outer
    )
    first.add(d_in, d_in_send)
    first.add(*d_cout)

    def send_home(parts):
        tokens = 2 * tok
        found = []
        for _, own, far, _ in parts:
            found.append(own)
            for j in range(1, members):
                found.append(swap(far[:, (j - 1) * tokens : j * tokens], "seq", j))
        return found

    def cross_back(at, count, deps):
        return attend_back(
            "cross_back", False, sc, ids_all, q2, grad_mixed2, lse2, delta2, k2s, v2s, at, count, deps
        )

    n = CROSS_SPLIT[0]
    cb = [cross_back(0, n, [layer_out])]
    cb.append(cross_back(n, 4 - n, [cb[0][0], *first.parts]))
    *buf_b, small_cross, grad_one, grad_mixed1, delta1, done_cross = after_cross(
        sc, plan_w, [c[0] for c in cb], grad_two, n0, r0, cross_q, mixed1, self_out, norm_gain, norm_bias,
    )
    def self_back(at, count, deps):
        return attend_back(
            "self_back", True, sc, ids_all, q1, grad_mixed1, lse1, delta1, k1s, v1s, at, count, deps
        )

    second, third = Chain(plan_w), Chain(plan_w)
    n = SELF_SPLIT[0]
    one = first.step(after=done_cross[0, 0])
    sb = []
    if not MEMORY_FIRST:
        sb.append(self_back(0, n, [one]))
        one = first.step(after=sb[0][3][0, 0])
    own_m, send_m, *buf_a, small_mem = memory_grad(
        sc, plan_w, xm, cross_kv, members, send_home(cb), deps=[grad_one, one] + [part[0] for part in sb]
    )
    if MEMORY_FIRST:
        sb.append(self_back(0, n, [small_mem]))
        one = first.step(after=sb[0][3][0, 0])
    second.after = sb[0][3][0, 0]
    second.add(*buf_b)
    second.add(*buf_a)
    sb.append(self_back(n, 4 - n, [small_mem, one, *second.parts]))
    forced = [first.step(after=sb[1][3][0, 0]) for _ in range(FORCE_FIRST - 2)]
    forced += [second.step(after=sb[1][3][0, 0]) for _ in range(FORCE_SECOND)]
    if BACK_EARLY:
        back_m = partner(send_m)
        forced.append(back_m)
    own_t, send_t, *buf_c, done = target_grad(
        sc, plan_w, x, self_qkv, grad_one, [part[0] for part in sb], members, send_home(sb),
        [small_ffn, small_mid, small_cross, small_mem], deps=forced,
    )
    third.after = done[0, 0]
    third.add(*buf_c)
    third.join()
    sends = send_t if BACK_EARLY else jnp.concatenate([send_t, send_m], axis=0)
    nb = ff // 512
    last = third.zero()
    chains = {1: first, 2: second, 3: third}
    outs_cross = (((512, 512), 0, 512, 0), ((512, 512), 512, 512, 0), ((512, 1024), 1024, 1024, 0))
    outs_ffn = (((ff, 512), 0, 512, 0), ((512, ff), 512, 512, 1), ((512, 512), 1024, 512 // nb, 1))
    for what in ORDER:
        if what in chains:
            if chains[what].todo:
                chains[what].step(after=last)
                last = chains[what].zero()
        elif what == 9:
            back = partner((sends.astype(f32) + wide(last, width)).astype(bf16))
        elif what == 7:
            last = last + back[0, 0].astype(f32) * 0.0
        elif what == 5:
            second.finish()
            *cross, done = unpack("unpack_cross", sc, W_PLACES, [(second, outs_cross)])
            last = last + done[0, 0]
        else:
            first.finish()
            d_ffn_out, d_ffn_in, d_cross_out, done = unpack("unpack_ffn", sc, FF_PLACES, [(first, outs_ffn)])
            last = last + done[0, 0]
    second.finish()
    third.finish()
    at = 8 + small_mid.shape[0]
    crs, mem, tg = at, at + 8, at + 16
    rest = [] if 5 in ORDER else [(second, outs_cross)]
    *got, d_self_bias, d_cross_bias, d_norm_gain, d_norm_bias, d_ffn_in_bias, d_ffn_out_bias, _ = unpack(
        "unpack_rest", sc, W_PLACES, rest + [(third, (((512, 1536), 0, 1536, 0),))],
        (
            (tg, tg + 1, crs + 3), (crs + 2, mem, 8 + 2), (crs, 8, 0), (crs + 1, 9, 1),
            tuple(16 + i for i in range(nb)), (2,),
        ),
    )
    d_cross_q, d_self_out, d_cross_kv, d_self_qkv = (cross if 5 in ORDER else []) + got
    if not BACK_EARLY:
        back, back_m = back[:tok], back[tok:]
    d_target, d_memory = home(own_t, back), home(own_m, back_m)
    return (
        layer_out, d_target, d_memory, d_self_qkv, d_self_out, d_self_bias, d_cross_q, d_cross_kv,
        d_cross_out, d_cross_bias, d_ffn_in, d_ffn_in_bias, d_ffn_out, d_ffn_out_bias, d_norm_gain, d_norm_bias,
    )


def solution(mesh):
    sharded, ids, copied = P("rows", "seq", None), P("rows", "seq"), P()
    in_specs = (sharded, sharded, ids, ids) + (copied,) * 13 + (sharded,)
    out_specs = (sharded,) * 3 + (copied,) * 13
    return jax.shard_map(per_device, mesh=mesh, in_specs=in_specs, out_specs=out_specs, check_vma=False)
```

```python
import functools
import math

import jax
import jax.numpy as jnp
from jax import lax
from jax.experimental import pallas as pl
from jax.experimental.pallas import tpu as pltpu
from jax.sharding import PartitionSpec as P

HEADS = 8
PAIR = 128
EPS = 1e-05
SCALE = 0.125
NEG = -1e30
VMEM = 16 * 1024 * 1024
CROSS_SPLIT, SELF_SPLIT = (1, 3), (2, 2)
MEMORY_FIRST, CUT_FF, BACK_EARLY = True, True, True
FORCE_FIRST, FORCE_SECOND = 3, 1
ORDER = (1, 1, 1, 3, 2, 9, 3, 3, 1, 2, 3, 1, 3, 2, 2, 7, 3, 8, 2)
bf16 = jnp.bfloat16
f32 = jnp.float32


def params():
    return pltpu.CompilerParams(vmem_limit_bytes=VMEM)


def cost(flops, nbytes, trans=0):
    return pl.CostEstimate(flops=int(flops), bytes_accessed=int(nbytes), transcendentals=int(trans))


def dot(a, b):
    return jnp.dot(a, b, preferred_element_type=f32)


def dot_nt(a, b):
    return lax.dot_general(a, b, (((1,), (1,)), ((), ())), preferred_element_type=f32)


def dot_tn(a, b):
    return lax.dot_general(a, b, (((0,), (0,)), ((), ())), preferred_element_type=f32)


def col_sum(v):
    return jnp.sum(v.astype(f32), axis=0, keepdims=True)


def normalize(h):
    mean = jnp.mean(h, axis=-1, keepdims=True)
    c = h - mean
    r = lax.rsqrt(jnp.mean(c * c, axis=-1, keepdims=True) + EPS)
    return c * r, r


def norm_back(u, n, r, gain):
    w = u * gain
    return r * (
        w
        - jnp.mean(w, axis=-1, keepdims=True)
        - n * jnp.mean(w * n, axis=-1, keepdims=True)
    )


def whole(shape):
    return pl.BlockSpec(shape, lambda *_: (0,) * len(shape))


def smem():
    return pl.BlockSpec(memory_space=pltpu.SMEM)


def half_rows(g, which, count):
    at = g if which == 0 else 1 - g
    return pl.ds(pl.multiple_of(at * count, count), count)


class Plan:
    def __init__(self, cut, whole, n, digit, minimum=16):
        first = (("seq", 1), ("seq", 1))
        self.scatter, self.everywhere = [], list(whole)
        k = n
        places = [0, 0]
        for step in [first] + list(cut):
            if k % 2 == 0 and k // 2 >= minimum:
                self.scatter.append(step)
                k //= 2
                places = [place * 2 + digit(*bit) for place, bit in zip(places, step)]
            else:
                self.everywhere.append(step)
        self.n, self.k, self.chunks = n, k, n // k
        self.half = self.chunks // 2
        self.places = [place % self.half for place in places]


def swap(x, axis, off):
    size = lax.axis_size(axis)
    return lax.ppermute(x, axis, [(i, i ^ off) for i in range(size)])


def exchange(x, step):
    if step[0] == step[1]:
        return swap(x, *step[0])
    rows, seq = lax.axis_size("rows"), lax.axis_size("seq")
    pairs = []
    for r in range(rows):
        for s in range(seq):
            axis, off = step[s % 2]
            to = ((r ^ off) * seq + s) if axis == "rows" else (r * seq + (s ^ off))
            pairs.append((r * seq + s, to))
    return lax.ppermute(x, ("rows", "seq"), pairs)


CORE, FF_PLACES, W_PLACES = 2, 3, 5


def store_rel(both, value, sc, k, cols):
    half = value.shape[0] // k // 2
    for core in range(2):
        side = jnp.bitwise_xor(sc[CORE], core)
        for w in range(half):
            at = jnp.bitwise_xor(sc[W_PLACES + core], w)
            row = (core * half + w) * k
            both[side, pl.ds(pl.multiple_of(at * k, k), k), cols] = value[row : row + k].astype(both.dtype)


def store_half(keep, send, value, q, half_blocks, sc, k):
    core, at = q // half_blocks, q % half_blocks
    place = sc[FF_PLACES + core]
    value = value.astype(keep.dtype)
    for mine, ref in ((True, keep), (False, send)):

        @pl.when((sc[CORE] == core) == mine)
        def _():
            for w in range(512 // k):
                to = jnp.bitwise_xor(place, at * (512 // k) + w) * k
                ref[pl.ds(pl.multiple_of(to, k), k), :] = value[w * k : (w + 1) * k]


def store_narrow(both, value, half_blocks, sc, k):
    share, per = value.shape[1] // (2 * half_blocks), 512 // k
    for q in range(2 * half_blocks):
        core = q // half_blocks
        side = jnp.bitwise_xor(sc[CORE], core)
        place = sc[FF_PLACES + core]
        for w in range(per):
            at = jnp.bitwise_xor(place, (q % half_blocks) * per + w) * k
            both[side, pl.ds(pl.multiple_of(at, k), k), :] = value[
                w * k : (w + 1) * k, q * share : (q + 1) * share
            ].astype(both.dtype)


def wide(zero, width):
    if jnp.ndim(zero) < 2:
        return zero
    return jnp.pad(zero, ((0, 0), (0, width - zero.shape[1])))


class Chain:
    def __init__(self, plan):
        self.plan, self.parts, self.other, self.after = plan, [], None, 0.0
        self.todo = [("rs", d) for d in plan.scatter[1:]] + [("all", d) for d in plan.everywhere]
        self.todo += [("ag", d) for d in reversed(plan.scatter[1:])] + [("last", plan.scatter[0])]

    def sum(self, mine, got):
        return (mine.astype(f32) + got.astype(f32) + wide(self.after, mine.shape[1])).astype(bf16)

    def add(self, keep, send):
        got = exchange(send, self.plan.scatter[0])
        self.parts.append(self.sum(keep, got))
        return self.parts[-1]

    def join(self):
        if self.parts:
            self.buf = jnp.concatenate(self.parts, axis=1)
            self.parts = []

    def step(self, after=0.0):
        self.after = after
        self.join()
        kind, step = self.todo.pop(0)
        buf = self.buf
        if kind == "rs":
            half = buf.shape[0] // 2
            self.buf = self.sum(buf[:half], exchange(buf[half:], step))
        elif kind == "all":
            self.buf = self.sum(buf, exchange(buf, step))
        elif kind == "ag":
            got = exchange(buf, step).astype(f32) + wide(after, buf.shape[1])
            self.buf = jnp.concatenate([buf, got.astype(bf16)], axis=0)
        else:
            self.other = exchange(buf, step)
        return self.buf

    def finish(self):
        while self.todo:
            self.step()

    def zero(self):
        return self.buf[0:1, :PAIR].astype(f32) * 0.0


def call(kernel, operands, in_specs, out_specs, out_shape, name, work, scratch=(), grid=None, scalars=(), deps=(), vmem=VMEM, aliases={}):
    n_front, n_deps = len(scalars) + len(operands), len(deps)

    def body(*refs):
        kernel(*refs[:n_front], *refs[n_front + n_deps :])

    specs = list(in_specs) + [pl.BlockSpec(memory_space=pl.ANY)] * n_deps
    common = dict(
        out_shape=out_shape,
        compiler_params=pltpu.CompilerParams(vmem_limit_bytes=vmem),
        cost_estimate=work,
        input_output_aliases=aliases,
        name=name,
    )
    if scalars:
        spec = pltpu.PrefetchScalarGridSpec(
            num_scalar_prefetch=len(scalars), grid=grid, in_specs=specs, out_specs=out_specs, scratch_shapes=list(scratch)
        )
        return pl.pallas_call(body, grid_spec=spec, **common)(*scalars, *operands, *deps)
    if grid is not None:
        common["grid"] = grid
    return pl.pallas_call(
        body, in_specs=specs, out_specs=out_specs, scratch_shapes=list(scratch), **common
    )(*operands, *deps)


def unpack(name, sc, places, buffers, rows=(), deps=()):
    halves_of = [x for chain, _ in buffers for x in (chain.buf, chain.other)]
    n_out = sum(len(outs) for _, outs in buffers)
    k = buffers[0][0].plan.k
    n_copies = 0
    for chain, outs in buffers:
        half, blocks = chain.buf.shape[0], max(chain.buf.shape[0] // 512, 1)
        if half // chain.plan.k <= 4 and all(out[3] == 0 for out in outs):
            n_copies += 2 * (half // chain.plan.k) * len(outs)
        else:
            n_copies += sum(2 * (1 if out[3] == 0 else blocks) for out in outs)

    def kernel(sc, *refs):
        sources, refs = refs[: len(halves_of)], refs[len(halves_of) :]
        goal, narrow, done = refs[:n_out], refs[n_out : n_out + len(rows)], refs[n_out + len(rows)]
        stages, sems = refs[n_out + len(rows) + 1 : -1], refs[-1]
        done[0, 0] = 0.0
        copies = []
        first_out = 0
        for i, (chain, outs) in enumerate(buffers):
            stage = stages[i]
            half = chain.buf.shape[0]
            blocks = max(half // 512, 1)
            size = half // blocks
            for side in range(2):
                src = sources[2 * i + side]
                core = jnp.bitwise_xor(sc[CORE], side)
                place = sc[places + core]
                few = half // k <= 4 and all(out[3] == 0 for out in outs)
                for w in range(half // k):
                    at = pl.multiple_of(jnp.bitwise_xor(place, w) * k, k)
                    stage[side, pl.ds(at, k), :] = src[w * k : (w + 1) * k, :].astype(f32)
                    for j, (shape, first, width, by) in enumerate(outs if few else ()):
                        part = stage.at[side, pl.ds(at, k), first : first + width]
                        to = goal[first_out + j].at[pl.ds(pl.multiple_of(core * half + at, k), k), :]
                        copies.append(pltpu.make_async_copy(part, to, sems.at[len(copies)]))
                        copies[-1].start()
                if few:
                    continue
                for j, (shape, first, width, by) in enumerate(outs):
                    cols = slice(first, first + width)
                    out = goal[first_out + j]
                    for b in range(1 if by == 0 else blocks):
                        if by == 0:
                            part = stage.at[side, :, cols]
                            to = out.at[pl.ds(pl.multiple_of(core * half, half), half), :]
                        else:
                            at = pl.multiple_of((core * blocks + b) * width, width)
                            part, to = stage.at[side, b * size : (b + 1) * size, cols], out.at[:, pl.ds(at, width)]
                        copies.append(pltpu.make_async_copy(part, to, sems.at[len(copies)]))
                        copies[-1].start()
            first_out += len(outs)
        if rows:
            last = buffers[-1][0].buf.shape[1] - PAIR
            mine, far = stages[-1][0, :, last:], stages[-1][1, :, last:]
            straight = sc[CORE] == 0
            turned = jnp.transpose(
                jnp.concatenate([jnp.where(straight, mine, far), jnp.where(straight, far, mine)], axis=0)
            )
            for ref, picks in zip(narrow, rows):
                for i, pick in enumerate(picks):
                    if len(ref.shape) == 1:
                        ref[i * 512 : (i + 1) * 512] = turned[pick]
                    else:
                        ref[i : i + 1, :] = turned[pick : pick + 1, :]
        for copy in copies:
            copy.wait()

    vm = pl.BlockSpec(memory_space=pltpu.VMEM)
    shapes = [jax.ShapeDtypeStruct(out[0], f32) for _, outs in buffers for out in outs]
    shapes += [jax.ShapeDtypeStruct((3, 512) if len(p) == 3 else (len(p) * 512,), f32) for p in rows]
    scratch = [pltpu.VMEM((2,) + chain.buf.shape, f32) for chain, _ in buffers]
    return call(
        kernel, [sc, *halves_of], [smem()] + [vm] * len(halves_of), [hbm()] * n_out + [vm] * len(rows) + [smem()],
        shapes + [jax.ShapeDtypeStruct((1, 1), f32)], name, cost(0, 6 * sum(x.size for x in halves_of)),
        scratch=scratch + [pltpu.SemaphoreType.DMA((n_copies,))], deps=deps, vmem=24 << 20,
    )


def hbm():
    return pl.BlockSpec(memory_space=pltpu.HBM)


def write_parts(y, scales, biases, b, outs, rows):
    for i, (scale, bias) in enumerate(zip(scales, biases)):
        cols = slice(i * 512, (i + 1) * 512)
        piece = y[:, cols] if bias is None else y[:, cols] + b[bias : bias + 1, :]
        piece = piece.astype(bf16)
        if scale != 1.0:
            piece = (piece.astype(f32) * scale).astype(bf16)
        if isinstance(outs, (tuple, list)):
            outs[i][rows, :] = piece
        else:
            outs[rows, cols] = piece


def embed_own_kernel(scales, biases, sc, tgt, w, b, out, x_out, w_out, b_out, done):
    done[0, 0] = 0.0
    x_out[...] = tgt[sc[0]]
    w_out[...] = w[...]
    b_out[...] = b[...]
    write_parts(dot(x_out[...], w[...]), scales, biases, b, out, slice(None))


def embed_own(name, sc, local, w, b, scales, biases, deps=()):
    tok = local.shape[1]
    sds = jax.ShapeDtypeStruct
    vm = pl.BlockSpec(memory_space=pltpu.VMEM)
    *found, done = call(
        functools.partial(embed_own_kernel, scales, biases), [sc, local, w, b], [smem()] + [vm] * 3, [vm] * 4 + [smem()],
        [sds((tok, w.shape[1]), bf16), sds((tok, 512), bf16), sds(w.shape, bf16), sds(b.shape, f32), sds((1, 1), f32)],
        name, cost(2 * tok * 512 * w.shape[1], 3e6), deps=deps,
    )
    return found, done


def embed_kernel(scales, biases, sc, recv, done, x, w, b, x_out, *outs):
    g = sc[0]
    tok = recv.shape[0]
    own, far = half_rows(g, 0, tok), half_rows(g, 1, tok)
    x_out[own, :] = x[...]
    x_out[far, :] = recv[...]
    for i, out in enumerate(outs):
        out[own, :] = done[:, i * 512 : (i + 1) * 512]
    write_parts(dot(recv[...], w[...]), scales, biases, b, outs, far)


def embed(name, sc, recv, own, scales, biases, deps=()):
    tok = recv.shape[0]
    one = jax.ShapeDtypeStruct((2 * tok, 512), bf16)
    vm = pl.BlockSpec(memory_space=pltpu.VMEM)
    return call(
        functools.partial(embed_kernel, scales, biases), [sc, recv, *own], [smem()] + [vm] * 5,
        [vm] * (1 + len(scales)), [one] * (1 + len(scales)), name, cost(2 * tok * 512 * 512 * len(scales), 4e6), deps=deps,
    )


def embed_both_kernel(scales, biases, sc, local, recv, w, b, x_out, *outs):
    g = sc[0]
    tok = recv.shape[0]
    x_out[half_rows(g, 0, tok), :] = local[g]
    x_out[half_rows(g, 1, tok), :] = recv[...]
    write_parts(dot(x_out[...], w[...]), scales, biases, b, outs, slice(None))


def embed_both(name, sc, local, recv, w, b, scales, biases, deps=()):
    tok = recv.shape[0]
    one = jax.ShapeDtypeStruct((2 * tok, 512), bf16)
    vm = pl.BlockSpec(memory_space=pltpu.VMEM)
    return call(
        functools.partial(embed_both_kernel, scales, biases), [sc, local, recv, w, b], [smem()] + [vm] * 4,
        [vm] * (1 + len(scales)), [one] * (1 + len(scales)), name, cost(4 * tok * 512 * 512 * len(scales), 4e6), deps=deps,
    )


BIG = 2.0**100


def to_cols(row):
    return jnp.transpose(jnp.broadcast_to(row, (PAIR, row.shape[1])))


def halves(parts, tok, axis=0):
    cut = (lambda e, at: e[at : at + tok]) if axis == 0 else (lambda e, at: e[:, at : at + tok])
    return jnp.concatenate([cut(e, 0) for e in parts] + [cut(e, tok) for e in parts], axis=axis)


def key_mask(causal, t, ids, tok, axis):
    length = ids.shape[1]
    members = length // (2 * tok)
    group = ids[0:1, :] if causal else ids[1:2, :]
    group = halves([group[:, 2 * tok * j : 2 * tok * (j + 1)] for j in range(members)], tok, 1)
    shape = (PAIR, length) if axis == 0 else (length, PAIR)
    if axis == 1:
        group = to_cols(group)
    feature = lax.broadcasted_iota(jnp.int32, shape, axis) % 64
    out = jnp.where((feature < 5) & (group + 1.0 != feature.astype(f32)), -BIG, 0.0)
    out = jnp.where((feature >= 5) & (feature < 8), 1.0, out)
    if causal:
        at = lax.broadcasted_iota(jnp.int32, shape, 1 - axis)
        low = jnp.bitwise_xor((at % (members * tok)) // tok, t)
        second = at >= members * tok
        out = jnp.where((feature == 8) & (second | (low > t)), -BIG, out)
        out = jnp.where((feature == 9) & second & (low > t), -BIG, out)
    return out.astype(bf16)


def query_mask(ids, tok, axis):
    group = ids[0:1, : 2 * tok]
    shape = (PAIR, 2 * tok) if axis == 0 else (2 * tok, PAIR)
    if axis == 1:
        group = to_cols(group)
    feature = lax.broadcasted_iota(jnp.int32, shape, axis) % 64
    second = (lax.broadcasted_iota(jnp.int32, shape, 1 - axis) >= tok).astype(jnp.int32)
    hot = (feature < 5) & (group + 1.0 == feature.astype(f32))
    return jnp.where(hot | (feature == 8 + second), 1.0, 0.0).astype(bf16)


def mixed_in(h, axis, mine, other):
    return jnp.where(lax.broadcasted_iota(jnp.int32, mine.shape, axis) // 64 == h, mine, other)


def with_own(s, at, later, axis):
    end, size = at + later.shape[0], s.shape[axis]
    cut = (lambda i, j: s[i:j]) if axis == 0 else (lambda i, j: s[:, i:j])
    pieces = [cut(0, at)] if at else []
    pieces.append(cut(at, end) + later)
    if end < size:
        pieces.append(cut(end, size))
    return jnp.concatenate(pieces, axis=axis) if len(pieces) > 1 else pieces[0]


def blocks_of(causal, tok, length):
    if not causal:
        return [(slice(0, 2 * tok), length, None)]
    return [(slice(0, tok), length // 2, 0), (slice(tok, 2 * tok), length, length // 2)]


def each_pair(count, length, body, unrolled=False):
    step = (4 if unrolled and count == 4 else 2) if count % 2 == 0 and length <= 1024 else 1

    def some(i, carry):
        for p in range(step):
            body(i * step + p)
        return carry

    if count == step:
        some(0, 0)
    else:
        lax.fori_loop(0, count // step, some, 0)


def pair_lanes(p):
    return pl.ds(p * PAIR if isinstance(p, int) else pl.multiple_of(p * PAIR, PAIR), PAIR)


def attend_kernel(causal, tok, members, sc, ids, q, *refs):
    out, lse = refs[2 * members :]
    length = 2 * tok * members
    keys_side = key_mask(causal, sc[1], ids[...], tok, 1)
    queries_side = query_mask(ids[...], tok, 0)
    key_at = lax.broadcasted_iota(jnp.int32, (tok, tok), 0)
    later = jnp.where(key_at > lax.broadcasted_iota(jnp.int32, (tok, tok), 1), NEG, 0.0)
    ones = jnp.ones((64, length), bf16)

    def one_pair(p):
        lanes = pair_lanes(p)
        k = halves([ref[:, lanes] for ref in refs[:members]], tok)
        v = jnp.transpose(halves([ref[:, lanes] for ref in refs[members : 2 * members]], tok))
        qt = jnp.transpose(q[:, lanes])
        parts = []
        for h in range(2):
            kh = mixed_in(h, 1, k, keys_side)
            qh = mixed_in(h, 0, qt, queries_side)
            vh = jnp.concatenate([v[h * 64 : (h + 1) * 64], ones], axis=0)
            row = []
            for cols, seen, own in blocks_of(causal, tok, length):
                s = dot(kh[:seen], qh[:, cols])
                if own is not None:
                    s = with_own(s, own, later, 0)
                top = jnp.max(s, axis=0, keepdims=True)
                got = dot(vh[:, :seen], jnp.exp(s - top).astype(bf16))
                total = got[64:65]
                row.append(got[:64] * (1.0 / total))
                lse[p, h : h + 1, cols] = top + jnp.log(total)
            parts.append(jnp.concatenate(row, axis=1))
        out[:, lanes] = jnp.transpose(jnp.concatenate(parts, axis=0)).astype(bf16)

    each_pair(4, length, one_pair, causal)


def attend_vmem(length):
    return min(VMEM * max(length // 1024, 1), 60 * 1024 * 1024)


def attend(name, causal, sc, ids, q, ks, vs, deps=()):
    tokens = q.shape[0]
    length = ids.shape[1]
    members = len(ks)
    vm = pl.BlockSpec(memory_space=pltpu.VMEM)
    return call(
        functools.partial(attend_kernel, causal, tokens // 2, members),
        [sc, ids, q, *ks, *vs],
        [smem()] + [vm] * (2 + 2 * members),
        [vm] * 2,
        [jax.ShapeDtypeStruct((tokens, 512), bf16), jax.ShapeDtypeStruct((4, 2, tokens), f32)],
        name,
        cost(42 * tokens * length * 512, 4e6, 8 * tokens * length),
        deps=deps,
        vmem=attend_vmem(length),
    )


def three(x):
    a = x.astype(bf16)
    rest = x - a.astype(f32)
    b = rest.astype(bf16)
    return a, b, (rest - b.astype(f32)).astype(bf16)


def with_terms(side, terms):
    feature = lax.broadcasted_iota(jnp.int32, side.shape, 1) % 64
    for i, term in enumerate(terms):
        side = jnp.where(feature == 5 + i, term, side)
    return side


def attend_back_kernel(causal, tok, members, pair, count, sc, ids, q, grad, lse, delta, *refs):
    dq, own_out, far, done = refs[2 * members :]
    done[0, 0] = 0.0
    length = 2 * tok * members
    keys_side = key_mask(causal, sc[1], ids[...], tok, 0)
    queries_side = query_mask(ids[...], tok, 1)
    zero = jnp.zeros((), bf16)
    feature = lax.broadcasted_iota(jnp.int32, (PAIR, length), 0) % 64
    ones = jnp.where((feature >= 5) & (feature < 8), 1.0, 0.0).astype(bf16)
    key_at = lax.broadcasted_iota(jnp.int32, (tok, tok), 1)
    later = jnp.where(key_at > lax.broadcasted_iota(jnp.int32, (tok, tok), 0), NEG, 0.0)
    half = length // 2

    def plus(total, term):
        return term if total is None else total + term

    def one_pair(p):
        from_lanes, lanes = pair_lanes(p + pair), pair_lanes(p)
        k = halves([ref[:, from_lanes] for ref in refs[:members]], tok)
        v = halves([ref[:, from_lanes] for ref in refs[members : 2 * members]], tok)
        q_here, g_here = q[:, from_lanes], grad[:, from_lanes]
        kt, vt = jnp.transpose(k), jnp.transpose(v)
        qt, gt = jnp.transpose(q_here), jnp.transpose(g_here)
        grad_k, grad_v, grad_q = [None, None], [None, None], {}
        for h in range(2):
            minus_lse = to_cols(-lse[p + pair, h : h + 1, :])
            minus_delta = to_cols(-delta[p + pair, h : h + 1, :])
            qh = mixed_in(h, 1, q_here, with_terms(queries_side, three(minus_lse)))
            gh = mixed_in(h, 1, g_here, with_terms(jnp.zeros((2 * tok, PAIR), bf16), three(minus_delta)))
            kh, vh = mixed_in(h, 0, kt, keys_side), mixed_in(h, 0, vt, ones)
            k_only, q_only, g_only = mixed_in(h, 1, k, zero), mixed_in(h, 0, qt, zero), mixed_in(h, 0, gt, zero)
            for b in range(2):
                rows = slice(b * tok, (b + 1) * tok)
                seen = half if causal and b == 0 else length
                s = dot(qh[rows], kh[:, :seen])
                if causal:
                    s = with_own(s, b * half, later, 1)
                w = jnp.exp(s)
                ds = (w * dot(gh[rows], vh[:, :seen])).astype(bf16)
                got_v, got_k = dot(g_only[:, rows], w.astype(bf16)), dot(q_only[:, rows], ds)
                for i in range(seen // half):
                    cols = slice(i * half, (i + 1) * half)
                    grad_v[i], grad_k[i] = plus(grad_v[i], got_v[:, cols]), plus(grad_k[i], got_k[:, cols])
                grad_q[b] = plus(grad_q.get(b), dot(ds, k_only[:seen]))
        for b in range(2):
            dq[b * tok : (b + 1) * tok, lanes] = (grad_q[b] * SCALE).astype(bf16)
        for i, total in enumerate((grad_k, grad_v)):
            for b in range(2):
                value = jnp.transpose(total[b]).astype(bf16)
                for j in range(members):
                    ref = far if j else own_out
                    at = (2 * j - 2 if j else 0) * tok + b * tok
                    ref[i, at : at + tok, lanes] = value[j * tok : (j + 1) * tok]

    each_pair(count, length, one_pair)


def attend_back(name, causal, sc, ids, q, grad, lse, delta, ks, vs, first, count, deps=()):
    tokens = q.shape[0]
    length = ids.shape[1]
    members = len(ks)
    width = count * PAIR
    sds = jax.ShapeDtypeStruct
    vm = pl.BlockSpec(memory_space=pltpu.VMEM)
    return call(
        functools.partial(attend_back_kernel, causal, tokens // 2, members, first, count),
        [sc, ids, q, grad, lse, delta, *ks, *vs],
        [smem()] + [vm] * (5 + 2 * members),
        [vm] * 3 + [smem()],
        [
            sds((tokens, width), bf16),
            sds((2, tokens, width), bf16),
            sds((2, length - tokens, width), bf16),
            sds((1, 1), f32),
        ],
        name,
        cost(17 * count * tokens * length * 512, 2e6 * count, 2 * count * tokens * length),
        deps=deps,
        vmem=attend_vmem(length),
    )


def after_self_kernel(x, mixed, w_out, sbias, gain, shift, w_q, cbias, n0, r0, q2):
    h = x[...].astype(f32) + dot(mixed[...], w_out[...]) + sbias[2:3, :]
    n, r = normalize(h)
    n0[...] = n
    r0[...] = r
    first = n * gain[0:1, :] + shift[0:1, :]
    q = dot(first.astype(bf16), w_q[...]) + cbias[0:1, :]
    q2[...] = (q.astype(bf16).astype(f32) * SCALE).astype(bf16)


def after_self(x, mixed, w_out, sbias, gain, shift, w_q, cbias):
    tokens = x.shape[0]
    vm = pl.BlockSpec(memory_space=pltpu.VMEM)
    return pl.pallas_call(
        after_self_kernel,
        in_specs=[vm] * 8,
        out_specs=[vm] * 3,
        out_shape=[
            jax.ShapeDtypeStruct((tokens, 512), f32),
            jax.ShapeDtypeStruct((tokens, 1), f32),
            jax.ShapeDtypeStruct((tokens, 512), bf16),
        ],
        compiler_params=params(),
        cost_estimate=cost(4 * tokens * 512 * 512, 4e6),
        name="after_self",
    )(x, mixed, w_out, sbias, gain, shift, w_q, cbias)


def head_sums(a, b):
    prod = a * b
    high = prod.astype(bf16)
    low = (prod - high.astype(f32)).astype(bf16)
    pick = (
        lax.broadcasted_iota(jnp.int32, (HEADS, 512), 1) // 64
        == lax.broadcasted_iota(jnp.int32, (HEADS, 512), 0)
    ).astype(bf16)
    return dot_nt(pick, high) + dot_nt(pick, low)


def put_head_rows(ref, rows):
    for p in range(4):
        ref[p] = rows[2 * p : 2 * p + 2]


def gelu_parts(v):
    c, d = math.sqrt(2.0 / math.pi), 0.044715 * math.sqrt(2.0 / math.pi)
    v2 = v * v
    g = 0.5 + 0.5 * jnp.tanh(v * (c + d * v2))
    return v * g, g * (1.0 + v * (2.0 * c + 6.0 * d * v2) * (1.0 - g))


def ffn_forward_kernel(
    chunks, k_out, sc, n0, mixed, cout, cbias, gain, shift, w_in, b_in, w_out, b_out, cot, cot_recv,
    own_out, send_out, d_keep, d_send, small, slope, low, n1, r1, grad_three, outer, total,
):
    g = sc[0]
    tok = cot_recv.shape[0]
    first = n0[...] * gain[0:1, :] + shift[0:1, :]
    n, r = normalize(first + dot(mixed[...], cout[...]) + cbias[2:3, :])
    n1[...] = n
    r1[...] = r
    second = n * gain[1:2, :] + shift[1:2, :]
    second_low = second.astype(bf16)
    low[...] = second_low
    result = second + b_out[...]
    inner = []
    for j in range(chunks):
        cols = slice(j * 512, (j + 1) * 512)
        act, grad_act = gelu_parts(dot(second_low, w_in[:, cols]) + b_in[:, cols])
        inner.append(act.astype(bf16))
        slope[:, cols] = grad_act.astype(bf16)
        result = result + dot(inner[-1], w_out[cols, :])
    n, r = normalize(result)
    total[...] = n * gain[2:3, :] + shift[2:3, :]
    own_out[...] = total[half_rows(g, 0, tok), :]
    send_out[...] = total[half_rows(g, 1, tok), :].astype(bf16)
    total[half_rows(g, 0, tok), :] = cot[g].astype(f32)
    total[half_rows(g, 1, tok), :] = cot_recv[...].astype(f32)
    u = total[...]
    back = norm_back(u, n, r, gain[2:3, :])
    back_low = back.astype(bf16)
    grad_three[...] = back
    outer[...] = back_low
    small[...] = jnp.zeros_like(small)
    small[0:1, :] = col_sum(u * n)
    small[1:2, :] = col_sum(u)
    small[2:3, :] = col_sum(back_low)
    for j in range(chunks):
        store_half(d_keep, d_send, dot_tn(inner[j], back_low), j, chunks // 2, sc, k_out)


def ffn_forward(sc, plan, n0, mixed, cout, cbias, gain, shift, w_in, b_in, w_out, b_out, cot, cot_recv, deps=()):
    tokens = n0.shape[0]
    tok = tokens // 2
    ff = w_in.shape[1]
    chunks = ff // 512
    sds = jax.ShapeDtypeStruct
    vm = pl.BlockSpec(memory_space=pltpu.VMEM)
    return call(
        functools.partial(ffn_forward_kernel, chunks, plan.k),
        [sc, n0, mixed, cout, cbias, gain, shift, w_in, b_in, w_out, b_out, cot, cot_recv],
        [smem()] + [vm] * 12,
        [vm] * 11,
        [
            sds((tok, 512), f32),
            sds((tok, 512), bf16),
            sds((ff // 2, 512), bf16),
            sds((ff // 2, 512), bf16),
            sds((8, 512), f32),
            sds((tokens, ff), bf16),
            sds((tokens, 512), bf16),
            sds((tokens, 512), f32),
            sds((tokens, 1), f32),
            sds((tokens, 512), f32),
            sds((tokens, 512), bf16),
        ],
        "ffn_forward",
        cost(4 * tokens * 512 * (3 * ff + 512), 1.5e7),
        scratch=[pltpu.VMEM((tokens, 512), f32)],
        deps=deps,
    )


def ffn_back_kernel(
    chunks, k_in, sc, mixed, cout, gain, w_in, w_out, slope, low, n1, r1, grad_three, outer,
    d_keep, d_send, c_keep, c_send, small, grad_two, grad_mixed, delta, both,
):
    small[...] = jnp.zeros_like(small)
    u = grad_three[...]
    back_outer, second_low = outer[...], low[...]
    for j in range(chunks):
        cols = slice(j * 512, (j + 1) * 512)
        pre_low = (dot_nt(back_outer, w_out[cols, :]) * slope[:, cols].astype(f32)).astype(bf16)
        small[8 + j : 9 + j, :] = col_sum(pre_low)
        u = u + dot_nt(pre_low, w_in[:, cols])
        store_half(d_keep, d_send, dot_tn(second_low, pre_low), j, chunks // 2, sc, k_in)
    n = n1[...]
    small[0:1, :] = col_sum(u * n)
    small[1:2, :] = col_sum(u)
    back = norm_back(u, n, r1[...], gain[1:2, :])
    grad_two[...] = back
    back_low = back.astype(bf16)
    small[2:3, :] = col_sum(back_low)
    g_mixed = dot_nt(back_low, cout[...]).astype(bf16)
    grad_mixed[...] = g_mixed
    put_head_rows(delta, head_sums(g_mixed.astype(f32), mixed[...].astype(f32)))
    store_narrow(both, dot_tn(mixed[...], back_low), chunks // 2, sc, k_in)
    c_keep[...] = both[0]
    c_send[...] = both[1]


def ffn_back(sc, plan, mixed, cout, gain, w_in, w_out, slope, low, n1, r1, grad_three, outer, deps=()):
    tokens = mixed.shape[0]
    ff = w_in.shape[1]
    chunks = ff // 512
    share = 512 // chunks
    sds = jax.ShapeDtypeStruct
    vm = pl.BlockSpec(memory_space=pltpu.VMEM)
    return call(
        functools.partial(ffn_back_kernel, chunks, plan.k),
        [sc, mixed, cout, gain, w_in, w_out, slope, low, n1, r1, grad_three, outer],
        [smem()] + [vm] * 11,
        [vm] * 8,
        [
            sds((ff // 2, 512), bf16),
            sds((ff // 2, 512), bf16),
            sds((ff // 2, share), bf16),
            sds((ff // 2, share), bf16),
            sds((8 + chunks + 4, 512), f32),
            sds((tokens, 512), f32),
            sds((tokens, 512), bf16),
            sds((4, 2, tokens), f32),
        ],
        "ffn_back",
        cost(4 * tokens * 512 * (3 * ff + 1024), 1.5e7),
        scratch=[pltpu.VMEM((2, ff // 2, share), bf16)],
        deps=deps,
    )


def after_cross_kernel(
    n_parts, k, sc, grad_two, n0, r0, w_q, mixed, w_out, gain, shift, *refs
):
    dq = jnp.concatenate([ref[...] for ref in refs[:n_parts]], axis=1)
    keep, send, small, grad_one, grad_mixed, delta, done, both = refs[n_parts:]
    done[0, 0] = 0.0
    n = n0[...]
    first = (n * gain[0:1, :] + shift[0:1, :]).astype(bf16)
    store_rel(both, dot_tn(first, dq), sc, k, slice(0, 512))
    u = grad_two[...] + dot_nt(dq, w_q[...])
    small[...] = jnp.zeros_like(small)
    small[0:1, :] = col_sum(u * n)
    small[1:2, :] = col_sum(u)
    small[2:3, :] = col_sum(dq)
    back = norm_back(u, n, r0[...], gain[0:1, :])
    grad_one[...] = back
    back_low = back.astype(bf16)
    small[3:4, :] = col_sum(back_low)
    store_rel(both, dot_tn(mixed[...], back_low), sc, k, slice(512, 1024))
    keep[...] = both[0]
    send[...] = both[1]
    g_mixed = dot_nt(back_low, w_out[...]).astype(bf16)
    grad_mixed[...] = g_mixed
    put_head_rows(delta, head_sums(g_mixed.astype(f32), mixed[...].astype(f32)))


def after_cross(sc, plan, dqs, grad_two, n0, r0, w_q, mixed, w_out, gain, shift, deps=()):
    tokens = n0.shape[0]
    sds = jax.ShapeDtypeStruct
    vm = pl.BlockSpec(memory_space=pltpu.VMEM)
    return call(
        functools.partial(after_cross_kernel, len(dqs), plan.k),
        [sc, grad_two, n0, r0, w_q, mixed, w_out, gain, shift, *dqs],
        [smem()] + [vm] * (8 + len(dqs)),
        [vm] * 6 + [smem()],
        [
            sds((256, 1024), bf16),
            sds((256, 1024), bf16),
            sds((8, 512), f32),
            sds((tokens, 512), f32),
            sds((tokens, 512), bf16),
            sds((4, 2, tokens), f32),
            sds((1, 1), f32),
        ],
        "after_cross",
        cost(12 * tokens * 512 * 512, 6e6),
        scratch=[pltpu.VMEM((2, 256, 1024), bf16)],
        deps=deps,
    )


def sum_members(refs, members):
    out = []
    for i in range(2):
        parts = []
        for at in range(0, len(refs), members):
            total = refs[at][i].astype(f32)
            for ref in refs[at + 1 : at + members]:
                total = total + ref[i].astype(f32)
            parts.append(total.astype(bf16))
        out.append(jnp.concatenate(parts, axis=1))
    return out


def memory_grad_kernel(members, count, k, sc, x, w, *refs):
    dk, dv = sum_members(refs[:count], members)
    own_out, send_out, keep, send, small, total, both = refs[count:]
    tok = own_out.shape[0]
    g = sc[0]
    store_rel(both, dot_tn(x[...], dk), sc, k, slice(0, 512))
    store_rel(both, dot_tn(x[...], dv), sc, k, slice(512, 1024))
    small[...] = jnp.zeros_like(small)
    small[0:1, :] = col_sum(dv)
    total[...] = dot_nt(dk, w[:, :512]) + dot_nt(dv, w[:, 512:])
    keep[...] = both[0]
    send[...] = both[1]
    own_out[...] = total[half_rows(g, 0, tok), :]
    send_out[...] = total[half_rows(g, 1, tok), :].astype(bf16)


def memory_grad(sc, plan, x, w, members, parts, deps=()):
    tokens = x.shape[0]
    tok = tokens // 2
    sds = jax.ShapeDtypeStruct
    vm = pl.BlockSpec(memory_space=pltpu.VMEM)
    return call(
        functools.partial(memory_grad_kernel, members, len(parts), plan.k),
        [sc, x, w, *parts],
        [smem()] + [vm] * (2 + len(parts)),
        [vm] * 5,
        [sds((tok, 512), f32), sds((tok, 512), bf16)] + [sds((256, 1024), bf16)] * 2 + [sds((8, 512), f32)],
        "memory_grad",
        cost(12 * tokens * 512 * 512, 6e6),
        scratch=[pltpu.VMEM((tokens, 512), f32), pltpu.VMEM((2, 256, 1024), bf16)],
        deps=deps,
    )


def target_grad_kernel(members, n_dq, count, n_small, k, sc, x, w, grad_one, *refs):
    dq = jnp.concatenate([ref[...] for ref in refs[:n_dq]], axis=1)
    refs = refs[n_dq:]
    dk, dv = sum_members(refs[:count], members)
    smalls = refs[count : count + n_small]
    own_out, send_out, keep, send, done, total, both = refs[count + n_small :]
    done[0, 0] = 0.0
    tok = own_out.shape[0]
    g = sc[0]
    for i, d in enumerate((dq, dk, dv)):
        store_rel(both, dot_tn(x[...], d), sc, k, slice(i * 512, (i + 1) * 512))
    rows = [ref[...] for ref in smalls] + [col_sum(dq), col_sum(dv)]
    used = sum(row.shape[0] for row in rows)
    rows.append(jnp.zeros((PAIR - used, 512), f32))
    store_rel(both, jnp.transpose(jnp.concatenate(rows, axis=0)), sc, k, slice(1536, 1536 + PAIR))
    total[...] = (
        grad_one[...]
        + dot_nt(dq, w[:, :512])
        + dot_nt(dk, w[:, 512:1024])
        + dot_nt(dv, w[:, 1024:])
    )
    keep[...] = both[0]
    send[...] = both[1]
    own_out[...] = total[half_rows(g, 0, tok), :]
    send_out[...] = total[half_rows(g, 1, tok), :].astype(bf16)


def target_grad(sc, plan, x, w, grad_one, dqs, members, parts, smalls, deps=()):
    tokens = x.shape[0]
    tok = tokens // 2
    sds = jax.ShapeDtypeStruct
    vm = pl.BlockSpec(memory_space=pltpu.VMEM)
    return call(
        functools.partial(target_grad_kernel, members, len(dqs), len(parts), len(smalls), plan.k),
        [sc, x, w, grad_one, *dqs, *parts, *smalls],
        [smem()] + [vm] * (3 + len(dqs) + len(parts) + len(smalls)),
        [vm] * 4 + [smem()],
        [sds((tok, 512), f32), sds((tok, 512), bf16)] + [sds((256, 1536 + PAIR), bf16)] * 2 + [sds((1, 1), f32)],
        "target_grad",
        cost(18 * tokens * 512 * 512, 8e6),
        scratch=[pltpu.VMEM((tokens, 512), f32), pltpu.VMEM((2, 256, 1536 + PAIR), bf16)],
        deps=deps,
    )


def per_device(
    target, memory, tgt_group, src_group, self_qkv, self_out, self_bias, cross_q, cross_kv, cross_out,
    cross_bias, ffn_in, ffn_in_bias, ffn_out, ffn_out_bias, norm_gain, norm_bias, cotangent,
):
    rows_here, tok, width = target.shape
    ff = ffn_in.shape[1]
    seq, rows = lax.axis_size("seq"), lax.axis_size("rows")
    members = seq // 2
    s, r = lax.axis_index("seq"), lax.axis_index("rows")
    g = s // members
    t = s % members

    def digit(axis, bit):
        return ((s if axis == "seq" else r) // bit) % 2

    def bits_of(axis, size, low):
        return [(axis, 1 << i) for i in range(low, size.bit_length() - 1)]

    x_bits, y_bits, z_bits = bits_of("seq", seq, 1), bits_of("rows", rows, 0)[:1], bits_of("rows", rows, 1)
    cut, whole_z = list(zip(x_bits + y_bits, y_bits + x_bits)), list(zip(z_bits[::-1], z_bits))
    plan_w = Plan(cut, whole_z, width, digit)
    plan_ff = Plan(cut + whole_z, [], ff, digit) if CUT_FF else Plan(cut, whole_z, ff, digit)
    sc = jnp.stack([g, t, s % 2, *plan_ff.places, *plan_w.places]).astype(jnp.int32)

    def partner(x):
        return swap(x, "seq", members)

    def others_of(x):
        return [swap(x, "seq", j) for j in range(1, members)]

    def pick(x, which):
        return lax.dynamic_index_in_dim(x, g if which == 0 else 1 - g, 0, keepdims=False)

    def home(own, back):
        back = back.astype(f32)
        return jnp.where(g == 0, jnp.stack([own, back]), jnp.stack([back, own]))

    tgt_recv = partner(pick(target, 1))
    ids = jnp.stack([tgt_group, src_group])
    ids_own = lax.dynamic_index_in_dim(ids, g, 1, keepdims=False)
    scales, biases = (SCALE, 1.0, 1.0), (0, None, 1)
    own_qkv, done = embed_own("embed_own", sc, target, self_qkv, self_bias, scales, biases)
    ids_recv = partner(lax.dynamic_index_in_dim(ids, 1 - g, 1, keepdims=False) + done[0, 0].astype(jnp.int32))
    mem_recv = partner(pick(memory, 1) + done[0, 0].astype(bf16))
    cot_recv = partner(pick(cotangent, 1) + mem_recv[0, 0] * bf16(0.0))
    ids_here = jnp.concatenate(
        [jnp.where(g == 0, ids_own, ids_recv), jnp.where(g == 0, ids_recv, ids_own)], axis=1
    ).astype(f32)
    ids_all = jnp.concatenate([ids_here] + others_of(ids_here), axis=1)

    x, q1, k1, v1 = embed("embed_target", sc, tgt_recv, own_qkv, scales, biases)
    k1s, v1s = [k1] + others_of(k1), [v1] + others_of(v1)
    mixed1, lse1 = attend("self_attend", True, sc, ids_all, q1, k1s, v1s)
    xm, k2, v2 = embed_both(
        "embed_memory", sc, memory, mem_recv, cross_kv, cross_bias, scales[1:], biases[1:], [mixed1]
    )
    k2s, v2s = [k2] + others_of(k2), [v2] + others_of(v2)

    n0, r0, q2 = after_self(x, mixed1, self_out, self_bias, norm_gain, norm_bias, cross_q, cross_bias)
    mixed2, lse2 = attend("cross_attend", False, sc, ids_all, q2, k2s, v2s)
    own_y, send_y, *d_out, small_ffn, slope, low, n1, r1, grad_three, outer = ffn_forward(
        sc, plan_ff, n0, mixed2, cross_out, cross_bias, norm_gain, norm_bias, ffn_in, ffn_in_bias[None],
        ffn_out, ffn_out_bias[None], cotangent, cot_recv,
    )
    layer_out = home(own_y, partner(send_y))
    first = Chain(plan_ff)
    first.add(*d_out)
    d_in, d_in_send, *d_cout, small_mid, grad_two, grad_mixed2, delta2 = ffn_back(
        sc, plan_ff, mixed2, cross_out, norm_gain, ffn_in, ffn_out, slope, low, n1, r1, grad_three, outer
    )
    first.add(d_in, d_in_send)
    first.add(*d_cout)

    def send_home(parts):
        tokens = 2 * tok
        found = []
        for _, own, far, _ in parts:
            found.append(own)
            for j in range(1, members):
                found.append(swap(far[:, (j - 1) * tokens : j * tokens], "seq", j))
        return found

    def cross_back(at, count, deps):
        return attend_back(
            "cross_back", False, sc, ids_all, q2, grad_mixed2, lse2, delta2, k2s, v2s, at, count, deps
        )

    n = CROSS_SPLIT[0]
    cb = [cross_back(0, n, [layer_out])]
    cb.append(cross_back(n, 4 - n, [cb[0][0], *first.parts]))
    *buf_b, small_cross, grad_one, grad_mixed1, delta1, done_cross = after_cross(
        sc, plan_w, [c[0] for c in cb], grad_two, n0, r0, cross_q, mixed1, self_out, norm_gain, norm_bias,
    )
    def self_back(at, count, deps):
        return attend_back(
            "self_back", True, sc, ids_all, q1, grad_mixed1, lse1, delta1, k1s, v1s, at, count, deps
        )

    second, third = Chain(plan_w), Chain(plan_w)
    n = SELF_SPLIT[0]
    one = first.step(after=done_cross[0, 0])
    sb = []
    if not MEMORY_FIRST:
        sb.append(self_back(0, n, [one]))
        one = first.step(after=sb[0][3][0, 0])
    own_m, send_m, *buf_a, small_mem = memory_grad(
        sc, plan_w, xm, cross_kv, members, send_home(cb), deps=[grad_one, one] + [part[0] for part in sb]
    )
    if MEMORY_FIRST:
        sb.append(self_back(0, n, [small_mem]))
        one = first.step(after=sb[0][3][0, 0])
    second.after = sb[0][3][0, 0]
    second.add(*buf_b)
    second.add(*buf_a)
    sb.append(self_back(n, 4 - n, [small_mem, one, *second.parts]))
    forced = [first.step(after=sb[1][3][0, 0]) for _ in range(FORCE_FIRST - 2)]
    forced += [second.step(after=sb[1][3][0, 0]) for _ in range(FORCE_SECOND)]
    if BACK_EARLY:
        back_m = partner(send_m)
        forced.append(back_m)
    own_t, send_t, *buf_c, done = target_grad(
        sc, plan_w, x, self_qkv, grad_one, [part[0] for part in sb], members, send_home(sb),
        [small_ffn, small_mid, small_cross, small_mem], deps=forced,
    )
    third.after = done[0, 0]
    third.add(*buf_c)
    third.join()
    sends = send_t if BACK_EARLY else jnp.concatenate([send_t, send_m], axis=0)
    nb = ff // 512
    last = third.zero()
    chains = {1: first, 2: second, 3: third}
    outs_cross = (((512, 512), 0, 512, 0), ((512, 512), 512, 512, 0), ((512, 1024), 1024, 1024, 0))
    outs_ffn = (((ff, 512), 0, 512, 0), ((512, ff), 512, 512, 1), ((512, 512), 1024, 512 // nb, 1))
    for what in ORDER:
        if what in chains:
            if chains[what].todo:
                chains[what].step(after=last)
                last = chains[what].zero()
        elif what == 9:
            back = partner((sends.astype(f32) + wide(last, width)).astype(bf16))
        elif what == 7:
            last = last + back[0, 0].astype(f32) * 0.0
        elif what == 5:
            second.finish()
            *cross, done = unpack("unpack_cross", sc, W_PLACES, [(second, outs_cross)])
            last = last + done[0, 0]
        else:
            first.finish()
            d_ffn_out, d_ffn_in, d_cross_out, done = unpack("unpack_ffn", sc, FF_PLACES, [(first, outs_ffn)])
            last = last + done[0, 0]
    second.finish()
    third.finish()
    at = 8 + small_mid.shape[0]
    crs, mem, tg = at, at + 8, at + 16
    rest = [] if 5 in ORDER else [(second, outs_cross)]
    *got, d_self_bias, d_cross_bias, d_norm_gain, d_norm_bias, d_ffn_in_bias, d_ffn_out_bias, _ = unpack(
        "unpack_rest", sc, W_PLACES, rest + [(third, (((512, 1536), 0, 1536, 0),))],
        (
            (tg, tg + 1, crs + 3), (crs + 2, mem, 8 + 2), (crs, 8, 0), (crs + 1, 9, 1),
            tuple(16 + i for i in range(nb)), (2,),
        ),
    )
    d_cross_q, d_self_out, d_cross_kv, d_self_qkv = (cross if 5 in ORDER else []) + got
    if not BACK_EARLY:
        back, back_m = back[:tok], back[tok:]
    d_target, d_memory = home(own_t, back), home(own_m, back_m)
    return (
        layer_out, d_target, d_memory, d_self_qkv, d_self_out, d_self_bias, d_cross_q, d_cross_kv,
        d_cross_out, d_cross_bias, d_ffn_in, d_ffn_in_bias, d_ffn_out, d_ffn_out_bias, d_norm_gain, d_norm_bias,
    )


def solution(mesh):
    sharded, ids, copied = P("rows", "seq", None), P("rows", "seq"), P()
    in_specs = (sharded, sharded, ids, ids) + (copied,) * 13 + (sharded,)
    out_specs = (sharded,) * 3 + (copied,) * 13
    return jax.shard_map(per_device, mesh=mesh, in_specs=in_specs, out_specs=out_specs, check_vma=False)
```
